32 devices in a mesh: grp: 2 (over y), dev: 8 (over z, core), pair: 2 (over x), sub: 1.
Axes of the slice: x: 2, y: 2, z: 4, core: 2. Of those that a mesh axis runs over, the one named last changes fastest.
Arguments:
- queries: bfloat16 [256, 4096], P(('grp', 'dev', 'sub'), 'pair'), parts along dimension 0, may hold values from -6 to 6
- key_rows: bfloat16 [256, 4096], P(('grp', 'dev', 'sub'), 'pair'), parts along dimension 0, may hold values from -6 to 6
- value_rows: bfloat16 [256, 4096], P(('grp', 'dev', 'sub'), 'pair'), parts along dimension 0, may hold values from -6 to 6
- states: float32 [64, 32, 128, 128], P(('grp', 'dev', 'sub'), 'pair'), parts along dimension 0, may hold values from -6 to 6
- decay_rates: float32 [32], P('pair'), may hold values from 0.02 to 2
- head_gain: float32 [4096], P('pair'), may hold values from 0.5 to 1.5
- out_weight: bfloat16 [4096, 6144], P('pair', ('dev', 'sub')), may hold values from -0.09375 to 0.09375
- residual: bfloat16 [256, 6144], P(('grp', 'dev', 'pair', 'sub')), parts along dimension 0, may hold values from -6 to 6
- norm_gain: float32 [6144], replicated, may hold values from 0.5 to 1.5
- expert_ids: int32 [256, 2], P(('grp', 'dev', 'pair', 'sub')), parts along dimension 0, may hold values from 0 to 3, all different within a row; in each aligned block of 8 rows (0 to 7, 8 to 15, ...) at most 4 rows name the same one
- gate_weights: float32 [256, 2], P(('grp', 'dev', 'pair', 'sub')), parts along dimension 0, may hold values from 0.1 to 1
- expert_gate: bfloat16 [18432, 6144], P(('dev', 'pair', 'sub')), may hold values from -0.078125 to 0.078125
- expert_up: bfloat16 [18432, 6144], P(('dev', 'pair', 'sub')), may hold values from -0.078125 to 0.078125
- expert_down: bfloat16 [18432, 6144], P(('dev', 'pair', 'sub')), may hold values from -0.09375 to 0.09375
Outputs:
- layer_out: bfloat16 [256, 6144], P(('grp', 'dev', 'pair', 'sub')), parts along dimension 0
The draws below stay inside these ranges and needn't reach their ends.
There are 2 independent parts, one for each index of `grp`. The reference program is written for one: setup_inputs(seed, part) draws one part's arguments, and reference() takes and returns one part's arrays. A program takes and returns all parts, laid end to end along the dimension named above; an argument that names none is the same for every part. Nothing has to cross between parts.
Inputs may be any that keep to these rules, and one draw needn't show every extreme that they name: `expert_ids`: each row names 2 different experts. In each aligned block of 8 rows (the rows of one device) no expert is named by more than 4 rows, and in every draw some block has an expert named by exactly 4 rows.
All inputs are finite; a program needn't handle non-finite values.
Results may differ from the reference program's by a relative error of at most 0.0048.
Values may be sent and summed in bfloat16 or wider, within the bound.
No kernel may reach another device: no remote copies, remote signals or barrier semaphores. Data moves between devices by JAX's collectives and lax.ppermute only.
A program may use at most 128 MiB of HBM per device.

```python
import math
import jax
import jax.numpy as jnp
import numpy as np
from jax import lax

D = 6144
HEADS = 32
HD = 128
FF = 4608
TOPK = 2
EXPERTS = 4
REQUESTS = 32
TOKENS = 128
ROWS = 8
CAP = 4
N_DEV = 8
N_PAIR = 2
N_SUB = 1


def steps_of(stream_key, dims, cuts, least, high):
    loudness, own = 1.0, jax.random.fold_in(stream_key, 6)
    for position, shards_of in cuts:
        steps = jnp.exp(jax.random.uniform(jax.random.fold_in(own, position), (shards_of,), jnp.float32, least / len(cuts), high / len(cuts)))
        loudness = loudness * jnp.repeat(steps, dims[position] // shards_of).reshape([-1 if axis == position else 1 for axis in range(len(dims))])
    return loudness


def routed_block(stream_key, own, number, rows, amount, top, bound, slope):
    order = jax.random.permutation(stream_key, amount)
    packed, common = shares(amount, rows * top, bound, slope, True), shares(amount, rows * top, bound, slope, False)
    places = jnp.arange(amount)

    def named(tallies, offset_by):
        used = int((tallies > 0).sum())
        fixed = max(1, used // 4)
        shifted = fixed + (places - fixed + offset_by * (used - fixed)) % max(1, amount - fixed)
        return jnp.zeros((amount,), jnp.int32).at[order[jnp.where(places < fixed, places, shifted)]].set(jnp.asarray(tallies, jnp.int32))

    tallies = jnp.where(number % 4 == 0, named(packed, number // 4), named(common, number - number // 4 - 1))
    mixed = jax.random.permutation(jax.random.fold_in(own, 3), amount)
    source_of, receiver = mixed[0:amount // 2 * 2:2], mixed[1:amount // 2 * 2:2]
    room = jnp.minimum(tallies[source_of] - 1, bound - tallies[receiver]) // 2
    room = jnp.where((source_of == order[0]) | (receiver == order[0]) | (tallies[receiver] == 0), 0, jnp.maximum(room, 0))
    shifted = jax.random.randint(jax.random.fold_in(own, 4), (amount // 2,), 0, 1 << 20) % (room + 1)
    tallies = tallies.at[source_of].add(-shifted).at[receiver].add(shifted)
    members = jnp.searchsorted(jnp.cumsum(tallies), jnp.arange(rows * top), side="right").astype(jnp.int32)
    table = members.reshape(top, rows).T
    table = table[jax.random.permutation(jax.random.fold_in(own, 1), rows)]
    offset_by = jax.random.randint(jax.random.fold_in(own, 2), (rows, 1), 0, top)
    return jnp.take_along_axis(table, (jnp.arange(top)[None, :] + offset_by) % top, axis=1)


def shares(count, total, bound, lean, full):
    portions = [(1 << 20) // math.isqrt(grade ** lean) + 1 for grade in range(1, count + 1)]
    largest = bound if full else min(bound, max(-(-total // count), total * portions[0] // sum(portions)))
    least = 1 if total - largest >= count - 1 else 0
    holding, surplus = [largest] + [least] * (count - 1), total - largest - least * (count - 1)
    while surplus > 0:
        movable = [i for i in range(1, count) if holding[i] < largest] or [i for i in range(1, count) if holding[i] < bound]
        pool, left = sum([portions[i] for i in movable]), surplus
        for i in movable:
            addition = min(bound - holding[i], max(1, left * portions[i] // pool), surplus)
            holding[i] = holding[i] + addition
            surplus = surplus - addition
    return np.array(holding)


def noise(stream_key, extent, scale, reach, cuts=(), kind=jnp.bfloat16):
    factor_of = steps_of(stream_key, extent, cuts, -0.22, 0.18) if cuts else 1.0
    values = jax.random.normal(stream_key, extent, jnp.float32) * scale * factor_of
    return jnp.minimum(jnp.maximum(values, -reach), reach).astype(kind)


def setup_inputs(seed: int = 0, part: int = 0) -> dict:
    arg_keys = jax.random.split(jax.random.key(seed), 15)
    part_keys = jax.random.split(jax.random.fold_in(arg_keys[14], part), 15)
    queries = noise(part_keys[0], (TOKENS, HEADS * HD), 1.0, 6.0, ((0, 8), (1, 2)))
    key_rows = noise(part_keys[1], (TOKENS, HEADS * HD), 1.0, 6.0, ((0, 8), (1, 2)))
    value_rows = noise(part_keys[2], (TOKENS, HEADS * HD), 1.0, 6.0, ((0, 8), (1, 2)))
    states = noise(part_keys[3], (REQUESTS, HEADS, HD, HD), 1.0, 6.0, ((0, 8), (1, 2)), jnp.float32)
    decay_rates = jnp.clip(jnp.exp(math.log(2.0) - 4.6051702 * jax.random.uniform(arg_keys[4], (HEADS,), jnp.float32) ** steps_of(arg_keys[4], (HEADS,), ((0, 2),), -0.2, 0.2)), 0.02, 2.0)
    head_gain = jnp.clip(1.0 + 0.1 * jax.random.normal(arg_keys[5], (HEADS * HD,), jnp.float32), 0.5, 1.5)
    out_weight = noise(arg_keys[6], (HEADS * HD, D), (HEADS * HD) ** -0.5, 0.09375, ((0, 2), (1, 8)))
    residual = noise(part_keys[7], (TOKENS, D), 1.0, 6.0, ((0, 16),))
    norm_gain = jnp.clip(1.0 + 0.1 * jax.random.normal(arg_keys[8], (D,), jnp.float32), 0.5, 1.5)
    expert_ids_keys = jax.random.split(jax.random.fold_in(part_keys[9], 1), TOKENS // ROWS)
    expert_ids_turns = jax.random.permutation(jax.random.fold_in(part_keys[9], 3), TOKENS // ROWS)
    expert_ids = jax.vmap(lambda own, number: routed_block(jax.random.fold_in(part_keys[9], 2), own, number, ROWS, EXPERTS, TOPK, CAP, 2))(expert_ids_keys, expert_ids_turns).reshape((TOKENS, TOPK))
    gate_weights = jnp.clip(0.1 + 0.9 * jax.random.uniform(part_keys[10], (TOKENS, TOPK), jnp.float32) ** steps_of(part_keys[10], (TOKENS, TOPK), ((0, 16),), -0.2, 0.2), 0.1, 1.0)
    expert_gate = noise(arg_keys[11], (EXPERTS * FF, D), D ** -0.5, 0.078125, ((0, 16),))
    expert_up = noise(arg_keys[12], (EXPERTS * FF, D), D ** -0.5, 0.078125, ((0, 16),))
    expert_down = noise(arg_keys[13], (EXPERTS * FF, D), FF ** -0.5, 0.09375, ((0, 16),))
    return {"queries": queries, "key_rows": key_rows, "value_rows": value_rows, "states": states, "decay_rates": decay_rates, "head_gain": head_gain, "out_weight": out_weight, "residual": residual, "norm_gain": norm_gain, "expert_ids": expert_ids, "gate_weights": gate_weights, "expert_gate": expert_gate, "expert_up": expert_up, "expert_down": expert_down}


EPSILON = 1e-06
HIGHEST = lax.Precision.HIGHEST

def attend(queries, key_rows, value_rows, states, decay_rates, head_gain):
    requests = states.shape[0]
    head_count = states.shape[1]
    head_size = states.shape[2]
    positions = queries.shape[0] // requests
    layout = (requests, positions, head_count, head_size)
    query_plain = queries.reshape(layout)
    key_plain = key_rows.reshape(layout)
    query_float = query_plain.astype(jnp.float32)
    value_float = value_rows.reshape(layout).astype(jnp.float32)
    offsets = jnp.arange(positions, dtype=jnp.float32)
    carried = jnp.exp(-decay_rates[None, :] * (offsets[:, None] + 1.0))
    from_state = jnp.einsum('rphk,rhkv->rphv', query_float, states, precision=HIGHEST)
    from_state = from_state * carried[None, :, :, None]
    scores = jnp.einsum('rthk,rjhk->rhtj', query_plain, key_plain, preferred_element_type=jnp.float32)
    distance = offsets[:, None] - offsets[None, :]
    fading = jnp.exp(-decay_rates[:, None, None] * jnp.maximum(distance, 0.0)[None, :, :])
    fading = jnp.where(distance[None, :, :] >= 0.0, fading, 0.0)
    scores = scores * fading[None]
    within = jnp.einsum('rhtj,rjhv->rthv', scores, value_float, precision=HIGHEST)
    mixed_heads = from_state + within
    spread = lax.optimization_barrier(jnp.mean(mixed_heads * mixed_heads, axis=3, keepdims=True))
    normal = mixed_heads * lax.rsqrt(spread + EPSILON) * head_gain.reshape(head_count, head_size)[None, None]
    return normal.astype(jnp.bfloat16).reshape(requests * positions, head_count * head_size)

def rms_scale(combined, norm_gain):
    spread = lax.optimization_barrier(jnp.mean(combined * combined, axis=-1, keepdims=True))
    return (combined * lax.rsqrt(spread + EPSILON) * norm_gain).astype(jnp.bfloat16)

def expert_apply(picked, gate_part, up_part, down_part):
    leading = picked.shape
    flattened = picked.reshape(-1, leading[-1])
    contract = (((1,), (1,)), ((), ()))
    gate_value = lax.dot_general(flattened, gate_part, contract, preferred_element_type=jnp.float32)
    lifted = lax.dot_general(flattened, up_part, contract, preferred_element_type=jnp.float32)
    hidden = (jax.nn.silu(gate_value) * lifted).astype(jnp.bfloat16)
    output = jnp.dot(hidden, down_part, preferred_element_type=jnp.float32)
    return output.reshape(leading)

def reference(queries, key_rows, value_rows, states, decay_rates, head_gain, out_weight, residual, norm_gain, expert_ids, gate_weights, expert_gate, expert_up, expert_down):
    attended = attend(queries, key_rows, value_rows, states, decay_rates, head_gain)
    projected = jnp.dot(attended, out_weight, preferred_element_type=jnp.float32)
    combined = residual.astype(jnp.float32) + projected
    normed = rms_scale(combined, norm_gain)
    chosen_ids = expert_ids.reshape(-1).astype(jnp.int32)
    repeated = jnp.repeat(normed, TOPK, axis=0)
    most_rows = N_DEV * N_PAIR * N_SUB * CAP
    ladder = jnp.arange(most_rows, dtype=jnp.int32)

    def add_expert(expert, totals):
        expert = jnp.asarray(expert).astype(jnp.int32)
        chosen = (chosen_ids == expert).astype(jnp.int32)
        ranking = (jnp.cumsum(chosen) - 1).astype(jnp.int32)
        placing = ((ranking[None, :] == ladder[:, None]) & (chosen[None, :] == 1)).astype(jnp.bfloat16)
        picked = jnp.dot(placing, repeated, preferred_element_type=jnp.float32).astype(jnp.bfloat16)
        offset = (expert * FF).astype(jnp.int32)
        gate_part = lax.dynamic_slice_in_dim(expert_gate, offset, FF, 0)
        up_part = lax.dynamic_slice_in_dim(expert_up, offset, FF, 0)
        down_part = lax.dynamic_slice_in_dim(expert_down, offset, FF, 0)
        output = expert_apply(picked, gate_part, up_part, down_part)
        back = lax.dot_general(placing.astype(jnp.float32), output, (((0,), (0,)), ((), ())), precision=HIGHEST, preferred_element_type=jnp.float32)
        return totals + back
    totals = lax.fori_loop(0, EXPERTS, add_expert, jnp.zeros((TOKENS * TOPK, D), jnp.float32))
    weighted = totals * gate_weights.reshape(-1)[:, None]
    mixture = lax.optimization_barrier(jnp.sum(weighted.reshape(TOKENS, TOPK, D), axis=1))
    return (combined + mixture).astype(jnp.bfloat16)
```

```python
import functools

import jax
import jax.numpy as jnp
from jax import lax
from jax.experimental import pallas as pl
from jax.experimental.pallas import tpu as pltpu
from jax.sharding import Mesh
from jax.sharding import PartitionSpec as P

EPSILON = 1e-06
F32 = jnp.float32
BF16 = jnp.bfloat16
MIB = 1 << 20
VMEM = pl.BlockSpec(memory_space=pltpu.VMEM)
SMEM = pl.BlockSpec(memory_space=pltpu.SMEM)
ANY = pl.BlockSpec(memory_space=pl.ANY)


def dot(a, b):
    return jnp.dot(a, b, preferred_element_type=F32)


def dot_t(a, b):
    return lax.dot_general(a, b, (((1,), (1,)), ((), ())), preferred_element_type=F32)


def halves_of(x):
    high = x.astype(BF16)
    return high, (x - high.astype(F32)).astype(BF16)


def attend_kernel(positions, decay_ref, q_ref, k_ref, v_ref, gain_ref, s_ref, o_ref):
    requests, heads, size, _ = s_ref.shape
    rows = q_ref.shape[0]
    first = pl.program_id(0) * heads
    row = lax.broadcasted_iota(jnp.int32, (rows, rows), 0)
    col = lax.broadcasted_iota(jnp.int32, (rows, rows), 1)
    seen = (row // positions == col // positions) & (row >= col)
    distance = jnp.maximum(row - col, 0).astype(F32)
    owner = lax.broadcasted_iota(jnp.int32, (rows, size), 0)
    age = (owner % positions + 1).astype(F32)
    for i in range(heads):
        rate = decay_ref[first + i]
        at = slice(i * size, (i + 1) * size)
        q = q_ref[:, at]
        spread_q = jnp.concatenate(
            [jnp.where(owner // positions == r, q, jnp.zeros_like(q)) for r in range(requests)],
            axis=1,
        )
        high, low = halves_of(s_ref[:, i].reshape(requests * size, size))
        from_state = (dot(spread_q, high) + dot(spread_q, low)) * jnp.exp(-rate * age)
        scores = jnp.where(seen, dot_t(q, k_ref[:, at]) * jnp.exp(-rate * distance), 0.0)
        score_high, score_low = halves_of(scores)
        v = v_ref[:, at]
        mixed = from_state + dot(score_high, v) + dot(score_low, v)
        spread = jnp.mean(mixed * mixed, axis=1, keepdims=True)
        normal = mixed * lax.rsqrt(spread + EPSILON) * gain_ref[:, at]
        o_ref[:, at] = normal.astype(BF16)


def attend(queries, key_rows, value_rows, states, decay_rates, head_gain):
    requests, heads, size, _ = states.shape
    rows = queries.shape[0]
    step = 4 if heads % 4 == 0 else 1
    wide = pl.BlockSpec((rows, step * size), lambda i: (0, i))
    return pl.pallas_call(
        functools.partial(attend_kernel, rows // requests),
        grid=(heads // step,),
        in_specs=[
            SMEM,
            wide,
            wide,
            wide,
            pl.BlockSpec((1, step * size), lambda i: (0, i)),
            pl.BlockSpec((requests, step, size, size), lambda i: (0, i, 0, 0)),
        ],
        out_specs=wide,
        out_shape=jax.ShapeDtypeStruct(queries.shape, BF16),
        compiler_params=pltpu.CompilerParams(vmem_limit_bytes=16 * MIB),
        name="attention",
    )(decay_rates, queries, key_rows, value_rows, head_gain.reshape(1, -1), states)


def project_kernel(count, chunk, base_ref, *refs):
    pieces, weight_ref, out_ref = refs[:count], refs[count], refs[count + 1]
    rows = pieces[0].shape[0]
    per = rows // chunk
    for i in range(count):
        product = dot(pieces[i][...], weight_ref[...]).astype(BF16)
        for j in range(per):
            out_ref[base_ref[i] * per + j] = product[j * chunk : (j + 1) * chunk]


def project(pieces, bases, weight, chunk):
    count = len(pieces)
    rows = pieces[0].shape[0]
    columns = weight.shape[1]
    return pl.pallas_call(
        functools.partial(project_kernel, count, chunk),
        in_specs=[SMEM] + [VMEM] * (count + 1),
        out_specs=VMEM,
        out_shape=jax.ShapeDtypeStruct((count * rows // chunk, chunk, columns), BF16),
        compiler_params=pltpu.CompilerParams(vmem_limit_bytes=16 * MIB),
        name="projection",
    )(bases, *pieces, weight)


def slots_of(ids_ref, experts, capacity):
    top, rows = ids_ref.shape
    order = [(t, k) for t in range(rows) for k in range(top)]
    named = [ids_ref[k, t] for t, k in order]
    slots = {}
    for j, at in enumerate(order):
        rank = jnp.int32(0)
        for i in range(j):
            rank = rank + jnp.where(named[i] == named[j], 1, 0)
        slots[at] = named[j] * capacity + rank
    return slots


def pack_kernel(
    experts, capacity, pairs, subs, ids_ref, got_ref, residual_ref, gain_ref, combined_ref, out_ref
):
    rows, width = residual_ref.shape
    if got_ref.ndim == 2:
        combined = residual_ref[...].astype(F32) + got_ref[...]
    else:
        sources, _, columns = got_ref.shape
        blocks = []
        for b in range(sources // pairs):
            total = residual_ref[:, b * columns : (b + 1) * columns].astype(F32)
            for p in range(pairs):
                source = (b // subs * pairs + p) * subs + b % subs
                total = total + got_ref[source].astype(F32)
            blocks.append(total)
        combined = jnp.concatenate(blocks, axis=1)
    combined_ref[...] = combined
    spread = jnp.mean(combined * combined, axis=1, keepdims=True)
    normed = (combined * lax.rsqrt(spread + EPSILON) * gain_ref[...]).astype(BF16)
    count = experts * capacity
    slot = lax.broadcasted_iota(jnp.int32, (count, rows), 0)
    row = lax.broadcasted_iota(jnp.int32, (count, rows), 1)
    placing = jnp.zeros((count, rows), F32)
    for (t, k), at in slots_of(ids_ref, experts, capacity).items():
        placing = jnp.where((slot == at) & (row == t), 1.0, placing)
    packed = dot(placing.astype(BF16), normed)
    copies = out_ref.shape[0] // experts
    parts = out_ref.shape[1] // capacity
    part = width // parts
    for e in range(experts):
        mine = packed[e * capacity : (e + 1) * capacity]
        folded = jnp.concatenate(
            [mine[:, h * part : (h + 1) * part] for h in range(parts)], axis=0
        ).astype(BF16)
        for c in range(copies):
            out_ref[e * copies + c] = folded


def pack(ids, got, residual, gain, experts, capacity, copies, pairs, subs):
    rows, width = residual.shape
    parts = 8 // capacity
    return pl.pallas_call(
        functools.partial(pack_kernel, experts, capacity, pairs, subs),
        in_specs=[SMEM, VMEM, VMEM, VMEM],
        out_specs=(VMEM, VMEM),
        out_shape=(
            jax.ShapeDtypeStruct((rows, width), F32),
            jax.ShapeDtypeStruct((experts * copies, 8, width // parts), BF16),
        ),
        compiler_params=pltpu.CompilerParams(vmem_limit_bytes=16 * MIB),
        name="pack",
    )(ids, got, residual, gain.reshape(1, -1))


def expert_kernel(capacity, block, wide, count, *refs):
    pieces = refs[:count]
    gate_hbm, up_hbm, down_hbm = refs[count : count + 3]
    own_ref, other_ref = refs[count + 3], refs[count + 4 : -8]
    other_ref = other_ref[0] if other_ref else None
    x_ref, hidden_ref, gate_ref, up_ref, down_ref, gate_sem, up_sem, down_sem = refs[-8:]
    units, width = gate_hbm.shape
    chunks = pieces[0].shape[0]
    parts = 8 // capacity
    part = width // parts
    blocks = units // block
    panels = width // wide

    def gate_copy(t):
        at = pl.ds(t * block, block)
        return pltpu.make_async_copy(gate_hbm.at[at], gate_ref.at[at], gate_sem.at[t])

    def up_copy(t):
        at = pl.ds(t * block, block)
        return pltpu.make_async_copy(up_hbm.at[at], up_ref.at[at], up_sem.at[t])

    def down_copy(n):
        at = pl.ds(n * wide, wide)
        return pltpu.make_async_copy(down_hbm.at[:, at], down_ref.at[:, at], down_sem.at[n])

    for t in range(blocks):
        gate_copy(t).start()
        up_copy(t).start()
    for n in range(panels):
        down_copy(n).start()

    piece_rows = chunks * capacity
    in_part = lax.broadcasted_iota(jnp.int32, (8, part), 0) // capacity
    for i in range(count):
        for h in range(parts):
            tiles = []
            for group in range(chunks // parts):
                tile = jnp.zeros((8, part), F32)
                for p in range(parts):
                    chunk = pieces[i][group * parts + p].astype(F32)
                    shift = (p - h) * capacity % 8
                    chunk = pltpu.roll(chunk, shift, 0) if shift else chunk
                    tile = jnp.where(in_part == p, chunk, tile)
                tiles.append(tile)
            x_ref[i * piece_rows : (i + 1) * piece_rows, h * part : (h + 1) * part] = (
                jnp.concatenate(tiles, axis=0).astype(BF16)
            )

    def hidden_step(t, carry):
        at = pl.ds(pl.multiple_of(t * block, block), block)
        gate_copy(t).wait()
        gate_value = dot_t(gate_ref[at], x_ref[...])
        up_copy(t).wait()
        lifted = dot_t(up_ref[at], x_ref[...])
        hidden_ref[at] = gate_value / (1.0 + jnp.exp(-gate_value)) * lifted
        return carry

    lax.fori_loop(0, blocks, hidden_step, 0)
    hidden = hidden_ref[...].T.astype(BF16)

    for n in range(panels):
        down_copy(n).wait()
        at = slice(n * wide, (n + 1) * wide)
        x_ref[:, at] = dot(hidden, down_ref[:, at]).astype(BF16)

    for i in range(count):
        for group in range(chunks // parts):
            first = i * piece_rows + group * 8
            for p in range(parts):
                tile = jnp.zeros((8, part), F32)
                for h in range(parts):
                    rows = x_ref[first : first + 8, h * part : (h + 1) * part].astype(F32)
                    shift = (h - p) * capacity % 8
                    rows = pltpu.roll(rows, shift, 0) if shift else rows
                    tile = jnp.where(in_part == h, rows, tile)
                if i == 0:
                    own_ref[group * parts + p] = tile.astype(BF16)
                else:
                    other_ref[i - 1, group * parts + p] = tile.astype(BF16)


def expert_apply(pieces, gate_part, up_part, down_part, capacity):
    count = len(pieces)
    units, width = gate_part.shape
    block = next(b for b in (128, 96, 64, 32, 16) if units % b == 0)
    wide = 512
    rows = count * pieces[0].shape[0] * capacity
    return pl.pallas_call(
        functools.partial(expert_kernel, capacity, block, wide, count),
        in_specs=[VMEM] * count + [ANY] * 3,
        out_specs=(VMEM, VMEM),
        out_shape=(
            jax.ShapeDtypeStruct(pieces[0].shape, BF16),
            jax.ShapeDtypeStruct((count - 1,) + pieces[0].shape, BF16),
        ),
        scratch_shapes=[
            pltpu.VMEM((rows, width), BF16),
            pltpu.VMEM((units, rows), F32),
            pltpu.VMEM((units, width), BF16),
            pltpu.VMEM((units, width), BF16),
            pltpu.VMEM((units, width), BF16),
            pltpu.SemaphoreType.DMA((units // block,)),
            pltpu.SemaphoreType.DMA((units // block,)),
            pltpu.SemaphoreType.DMA((width // wide,)),
        ],
        compiler_params=pltpu.CompilerParams(vmem_limit_bytes=56 * MIB),
        name="experts",
    )(*pieces, gate_part, up_part, down_part)


def finish_kernel(experts, capacity, ids_ref, weights_ref, got_ref, combined_ref, out_ref):
    sources, tall, part = got_ref.shape
    copies = sources // experts
    parts = tall // capacity
    rows = combined_ref.shape[0]
    row = lax.broadcasted_iota(jnp.int32, (rows, sources * tall), 0)
    place = lax.broadcasted_iota(jnp.int32, (rows, sources * tall), 1)
    slot = place // (copies * tall) * capacity + place % capacity
    in_part = place % tall // capacity
    weighting = jnp.zeros((rows, sources * tall), F32)
    for (t, k), at in slots_of(ids_ref, experts, capacity).items():
        weighting = jnp.where((slot == at) & (row == t), weights_ref[k, t], weighting)
    got = got_ref[...].reshape(sources * tall, part)
    for h in range(parts):
        at = slice(h * part, (h + 1) * part)
        high, low = halves_of(jnp.where(in_part == h, weighting, 0.0))
        mixture = dot(high, got) + dot(low, got)
        out_ref[:, at] = (combined_ref[:, at] + mixture).astype(BF16)


def finish(ids, weights, got, combined, experts, capacity):
    return pl.pallas_call(
        functools.partial(finish_kernel, experts, capacity),
        in_specs=[SMEM, SMEM, VMEM, VMEM],
        out_specs=VMEM,
        out_shape=jax.ShapeDtypeStruct(combined.shape, BF16),
        compiler_params=pltpu.CompilerParams(vmem_limit_bytes=16 * MIB),
        name="finish",
    )(ids, weights, got, combined)


def shift_along(x, axes, size, by):
    return lax.ppermute(x, axes, [(i, (i + by) % size) for i in range(size)])


def on_device(
    queries,
    key_rows,
    value_rows,
    states,
    decay_rates,
    head_gain,
    out_weight,
    residual,
    norm_gain,
    expert_ids,
    gate_weights,
    expert_gate,
    expert_up,
    expert_down,
):
    experts = lax.axis_size("expert")
    pairs = lax.axis_size("pair")
    subs = lax.axis_size("sub")
    inner = ("half", "sub")
    inners = lax.axis_size("half") * subs
    local_rows, width = residual.shape
    capacity = max(2, local_rows * expert_ids.shape[1] // experts)
    ids, weights = expert_ids.T, gate_weights.T

    attended = attend(queries, key_rows, value_rows, states, decay_rates, head_gain)
    my_expert, my_inner = lax.axis_index("expert"), lax.axis_index(inner)
    pieces, bases = [], []
    for d in range(experts):
        piece = shift_along(attended, "expert", experts, d) if d else attended
        for c in range(inners):
            pieces.append(shift_along(piece, inner, inners, c) if c else piece)
            bases.append(
                (my_expert - d + experts) % experts * inners + (my_inner - c + inners) % inners
            )
    blocks = project(pieces, jnp.stack(bases).astype(jnp.int32), out_weight, local_rows)

    columns = out_weight.shape[1]
    got = lax.all_to_all(
        blocks, ("expert", "half", "pair", "sub"), split_axis=0, concat_axis=0, tiled=True
    )
    if columns % 128:
        got = got.reshape(experts * 2, pairs, subs, local_rows, columns).astype(F32)
        got = jnp.transpose(got.sum(axis=1), (2, 0, 1, 3)).reshape(local_rows, width)
    combined, outgoing = pack(
        ids, got, residual, norm_gain, experts, capacity, pairs, pairs, subs
    )

    plane = ("expert", "pair")
    routed = lax.all_to_all(outgoing, plane, split_axis=0, concat_axis=0, tiled=True)
    routed = [shift_along(routed, inner, inners, c) if c else routed for c in range(inners)]
    own, others = expert_apply(routed, expert_gate, expert_up, expert_down, capacity)

    total = own.astype(F32)
    for c in range(1, inners):
        total = total + shift_along(others[c - 1], inner, inners, inners - c).astype(F32)
    back = lax.all_to_all(total.astype(BF16), plane, split_axis=0, concat_axis=0, tiled=True)
    return finish(ids, weights, back, combined, experts, capacity)


def solution(mesh):
    sizes = dict(mesh.shape)
    experts = sizes["dev"] // 2
    cut = Mesh(
        mesh.devices.reshape(sizes["grp"], experts, 2, sizes["pair"], sizes["sub"]),
        ("grp", "expert", "half", "pair", "sub"),
    )
    dev = ("expert", "half")
    requests = P(("grp",) + dev + ("sub",), "pair")
    tokens = P(("grp",) + dev + ("pair", "sub"), None)
    units = P(dev + ("pair", "sub"), None)
    return jax.shard_map(
        on_device,
        mesh=cut,
        in_specs=(
            requests,
            requests,
            requests,
            P(("grp",) + dev + ("sub",), "pair", None, None),
            P("pair"),
            P("pair"),
            P("pair", dev + ("sub",)),
            tokens,
            P(),
            tokens,
            tokens,
            units,
            units,
            units,
        ),
        out_specs=tokens,
        check_vma=False,
    )
```

```python
import functools

import jax
import jax.numpy as jnp
from jax import lax
from jax.experimental import pallas as pl
from jax.experimental.pallas import tpu as pltpu
from jax.sharding import Mesh
from jax.sharding import PartitionSpec as P

EPSILON = 1e-06
F32 = jnp.float32
BF16 = jnp.bfloat16
MIB = 1 << 20
VMEM = pl.BlockSpec(memory_space=pltpu.VMEM)
SMEM = pl.BlockSpec(memory_space=pltpu.SMEM)
ANY = pl.BlockSpec(memory_space=pl.ANY)


def in_hbm(*arrays):
    return [pltpu.with_memory_space_constraint(a, pltpu.HBM) for a in arrays]


def limits(mib):
    return pltpu.CompilerParams(vmem_limit_bytes=mib * MIB)


def here():
    inner = lax.axis_index("half") * lax.axis_size("sub") + lax.axis_index("sub")
    return lax.axis_index("expert"), inner, lax.axis_index("pair")


def dot(a, b):
    return jnp.dot(a, b, preferred_element_type=F32)


def dot_t(a, b):
    return lax.dot_general(a, b, (((1,), (1,)), ((), ())), preferred_element_type=F32)


def halves_of(x):
    high = x.astype(BF16)
    return high, (x - high.astype(F32)).astype(BF16)


def attend_kernel(positions, decay_ref, q_ref, k_ref, v_ref, gain_ref, s_ref, o_ref):
    requests, heads, size, _ = s_ref.shape
    rows = q_ref.shape[0]
    first = pl.program_id(0) * heads
    row = lax.broadcasted_iota(jnp.int32, (rows, rows), 0)
    col = lax.broadcasted_iota(jnp.int32, (rows, rows), 1)
    seen = (row // positions == col // positions) & (row >= col)
    distance = jnp.maximum(row - col, 0).astype(F32)
    owner = lax.broadcasted_iota(jnp.int32, (rows, size), 0)
    age = (owner % positions + 1).astype(F32)
    for i in range(heads):
        rate = decay_ref[first + i]
        at = slice(i * size, (i + 1) * size)
        q = q_ref[:, at]
        spread_q = jnp.concatenate(
            [jnp.where(owner // positions == r, q, jnp.zeros_like(q)) for r in range(requests)],
            axis=1,
        )
        high, low = halves_of(s_ref[:, i].reshape(requests * size, size))
        from_state = (dot(spread_q, high) + dot(spread_q, low)) * jnp.exp(-rate * age)
        scores = jnp.where(seen, dot_t(q, k_ref[:, at]) * jnp.exp(-rate * distance), 0.0)
        score_high, score_low = halves_of(scores)
        v = v_ref[:, at]
        mixed = from_state + dot(score_high, v) + dot(score_low, v)
        spread = jnp.mean(mixed * mixed, axis=1, keepdims=True)
        normal = mixed * lax.rsqrt(spread + EPSILON) * gain_ref[:, at]
        o_ref[:, at] = normal.astype(BF16)


def attend(queries, key_rows, value_rows, states, decay_rates, head_gain):
    requests, heads, size, _ = states.shape
    rows = queries.shape[0]
    step = 4 if heads % 4 == 0 else 1
    wide = pl.BlockSpec((rows, step * size), lambda i: (0, i))
    return pl.pallas_call(
        functools.partial(attend_kernel, rows // requests),
        grid=(heads // step,),
        in_specs=[
            SMEM,
            wide,
            wide,
            wide,
            pl.BlockSpec((1, step * size), lambda i: (0, i)),
            pl.BlockSpec((requests, step, size, size), lambda i: (0, i, 0, 0)),
        ],
        out_specs=wide,
        out_shape=jax.ShapeDtypeStruct(queries.shape, BF16),
        compiler_params=limits(8),
        name="attention",
    )(*in_hbm(decay_rates, queries, key_rows, value_rows, head_gain.reshape(1, -1), states))


def load_kernel(count, *refs):
    sources, targets, sems = refs[:count], refs[count + 1 : -1], refs[-1]
    copies = [
        pltpu.make_async_copy(source, target, sems.at[i])
        for i, (source, target) in enumerate(zip(sources, targets))
    ]
    for copy in copies:
        copy.start()
    for copy in copies:
        copy.wait()


def load(arrays, after, name):
    count = len(arrays)
    size = sum(a.size * a.dtype.itemsize for a in arrays)
    return pl.pallas_call(
        functools.partial(load_kernel, count),
        in_specs=[ANY] * (count + 1),
        out_specs=[VMEM] * count,
        out_shape=[pltpu.VMEM(a.shape, a.dtype) for a in arrays],
        scratch_shapes=[pltpu.SemaphoreType.DMA((count,))],
        compiler_params=limits(1),
        cost_estimate=pl.CostEstimate(flops=0, bytes_accessed=2 * size, transcendentals=0),
        name=name,
    )(*in_hbm(*arrays), after)


def project_kernel(chunk, experts, inners, relative, *refs):
    count = experts * inners
    pieces, weight_ref = refs[:count], refs[count]
    outs, x_ref, product_ref = refs[count + 1 : -2], refs[-2], refs[-1]
    rows = pieces[0].shape[0]
    expert, inner, pair = here()
    for d in range(experts):
        for c in range(inners):
            base = (expert ^ d) * inners + (inner ^ c)
            x_ref[pl.ds(pl.multiple_of(base * rows, rows), rows)] = pieces[d * inners + c][...]
    product_ref[...] = dot(x_ref[...], weight_ref[...])
    if relative:
        me = lax.axis_index(("expert", "half", "pair", "sub"))
        for d, out in enumerate(outs):
            at = pl.ds(pl.multiple_of((me ^ d) * chunk, chunk), chunk)
            out[...] = product_ref[at].astype(BF16)
    else:
        for d in range(outs[0].shape[0]):
            outs[0][d] = product_ref[d * chunk : (d + 1) * chunk].astype(BF16)


def project(pieces, weight, chunk, experts, inners, relative):
    rows = pieces[0].shape[0] * len(pieces)
    depth, columns = weight.shape
    chunks = rows // chunk
    if relative:
        out_shape = [jax.ShapeDtypeStruct((chunk, columns), BF16)] * chunks
    else:
        out_shape = [jax.ShapeDtypeStruct((chunks, chunk, columns), BF16)]
    return pl.pallas_call(
        functools.partial(project_kernel, chunk, experts, inners, relative),
        in_specs=[VMEM] * (len(pieces) + 1),
        out_specs=[VMEM] * len(out_shape),
        out_shape=out_shape,
        scratch_shapes=[pltpu.VMEM((rows, depth), BF16), pltpu.VMEM((rows, columns), F32)],
        compiler_params=limits(8),
        name="projection",
    )(*pieces, weight)


def slots_of(ids_ref, capacity, me):
    top, rows = ids_ref.shape
    order = [(t, k) for t in range(rows) for k in range(top)]
    named = [ids_ref[k, t] for t, k in order]
    slots = {}
    for j, at in enumerate(order):
        rank = jnp.int32(0)
        for i in range(j):
            rank = rank + jnp.where(named[i] == named[j], 1, 0)
        slots[at] = (named[j] ^ me) * capacity + rank
    return slots


def pack_kernel(capacity, pairs, subs, relative, count, ids_ref, residual_ref, gain_ref, *refs):
    got, combined_ref, outs = refs[:count], refs[count], refs[count + 1 :]
    rows, width = residual_ref.shape
    experts = lax.axis_size("expert")
    if count == 1:
        combined_ref[...] = residual_ref[...].astype(F32) + got[0][...]
    else:
        combined_ref[...] = residual_ref[...].astype(F32)
        columns = got[0].shape[1]
        me = lax.axis_index(("expert", "half", "pair", "sub"))
        for d in range(count):
            source = me ^ d
            block = source // (pairs * subs) * subs + source % subs
            at = pl.ds(pl.multiple_of(block * columns, columns), columns)
            combined_ref[:, at] += got[d][...].astype(F32)
    combined = combined_ref[...]
    spread = jnp.mean(combined * combined, axis=1, keepdims=True)
    normed = (combined * lax.rsqrt(spread + EPSILON) * gain_ref[...]).astype(BF16)
    slot = lax.broadcasted_iota(jnp.int32, (experts * capacity, rows), 0)
    row = lax.broadcasted_iota(jnp.int32, (experts * capacity, rows), 1)
    placing = jnp.zeros((experts * capacity, rows), F32)
    me = lax.axis_index("expert") if relative else 0
    for (t, k), at in slots_of(ids_ref, capacity, me).items():
        placing = jnp.where((slot == at) & (row == t), 1.0, placing)
    packed = dot(placing.astype(BF16), normed)
    parts = outs[0].shape[1] // capacity
    part = width // parts
    for e in range(experts):
        mine = packed[e * capacity : (e + 1) * capacity]
        folded = jnp.concatenate(
            [mine[:, h * part : (h + 1) * part] for h in range(parts)], axis=0
        ).astype(BF16)
        if relative:
            outs[e][0] = folded
        else:
            for c in range(pairs):
                outs[0][e * pairs + c] = folded


def pack(ids, residual, gain, got, capacity, experts, pairs, subs, relative):
    rows, width = residual.shape
    parts = 8 // capacity
    if relative:
        out_shape = [jax.ShapeDtypeStruct((1, 8, width // parts), BF16)] * experts
    else:
        out_shape = [jax.ShapeDtypeStruct((experts * pairs, 8, width // parts), BF16)]
    return pl.pallas_call(
        functools.partial(pack_kernel, capacity, pairs, subs, relative, len(got)),
        in_specs=[SMEM, VMEM, VMEM] + [VMEM] * len(got),
        out_specs=[VMEM] * (1 + len(out_shape)),
        out_shape=[jax.ShapeDtypeStruct((rows, width), F32)] + out_shape,
        compiler_params=limits(8),
        name="pack",
    )(*in_hbm(ids), residual, gain, *got)


def expert_kernel(capacity, block, wide, own, count, *refs):
    pieces, gate_ref, up_ref, down_hbm = refs[:count], *refs[count : count + 3]
    own_ref, others_ref = refs[count + 3 : count + 5]
    x_ref, hidden_ref, down_ref, down_sem = refs[count + 5 :]
    units, width = gate_ref.shape
    parts = 8 // capacity
    part = width // parts
    rows = x_ref.shape[0]

    def down_copy(n):
        at = pl.ds(n * wide, wide)
        return pltpu.make_async_copy(down_hbm.at[:, at], down_ref.at[:, at], down_sem.at[n])

    panels = [[(h * part) // wide + n for h in range(parts)] for n in range(part // wide)]
    for panel in panels:
        for n in panel:
            down_copy(n).start()

    first = 0
    for piece in pieces:
        tall = piece.shape[0] * 8
        x_ref[first : first + tall] = piece[...].astype(F32).reshape(tall, part)
        first += tall
    x = x_ref[...].T.astype(BF16)

    part_of = lax.broadcasted_iota(jnp.int32, (block, rows), 1) % 8 // capacity

    def product(weight_ref, at):
        total = jnp.zeros((block, rows), F32)
        for h in range(parts):
            term = dot(weight_ref[at, h * part : (h + 1) * part], x)
            total = jnp.where(part_of == h, term, total)
        step = 1
        while step < parts:
            odd = part_of // step % 2 == 1
            by = step * capacity
            total = total + jnp.where(
                odd, pltpu.roll(total, by, 1), pltpu.roll(total, rows - by, 1)
            )
            step *= 2
        return total

    for t in range(units // block):
        at = slice(t * block, (t + 1) * block)
        gate_value = product(gate_ref, at)
        lifted = product(up_ref, at)
        hidden = gate_value / (1.0 + jnp.exp(-gate_value)) * lifted
        hidden_ref[:, at] = hidden.T.astype(BF16)

    row_part = lax.broadcasted_iota(jnp.int32, (rows, wide), 0) % 8 // capacity
    for i, panel in enumerate(panels):
        total = jnp.zeros((rows, wide), F32)
        for h, n in enumerate(panel):
            down_copy(n).wait()
            term = dot(hidden_ref[...], down_ref[:, n * wide : (n + 1) * wide])
            total = jnp.where(row_part == h, term, total)
        at = slice(i * wide, (i + 1) * wide)
        total = total.reshape(rows // 8, 8, wide)
        own_ref[:, :, at] = total[:own]
        for j in range(others_ref.shape[0]):
            others_ref[j, :, :, at] = total[(j + 1) * own : (j + 2) * own].astype(BF16)


def expert_apply(pieces, gate_part, up_part, down_part, capacity, inners):
    units, width = gate_part.shape
    block = next(b for b in (384, 288, 256, 128, 96, 64, 32, 16) if units % b == 0)
    wide = 512
    chunks = sum(piece.shape[0] for piece in pieces)
    own = chunks // inners
    part = pieces[0].shape[2]
    return pl.pallas_call(
        functools.partial(expert_kernel, capacity, block, wide, own, len(pieces)),
        in_specs=[VMEM] * (len(pieces) + 2) + [ANY],
        out_specs=(VMEM, VMEM),
        out_shape=(
            jax.ShapeDtypeStruct((own, 8, part), F32),
            jax.ShapeDtypeStruct((inners - 1, own, 8, part), BF16),
        ),
        scratch_shapes=[
            pltpu.VMEM((chunks * 8, part), F32),
            pltpu.VMEM((chunks * 8, units), BF16),
            pltpu.VMEM((units, width), BF16),
            pltpu.SemaphoreType.DMA((width // wide,)),
        ],
        compiler_params=limits(24),
        name="experts",
    )(*pieces, gate_part, up_part, *in_hbm(down_part))


def add_kernel(own_ref, *refs):
    count = refs[0].shape[0]
    others = [ref for ref in refs if len(ref.shape) == 4]
    outs = refs[len(others) :]
    total = own_ref[...]
    for other in others:
        total = total + other[0].astype(F32)
    for i, out in enumerate(outs):
        each = out.shape[0]
        out[...] = total[i * each : (i + 1) * each].astype(BF16)


def add_terms(own, others, count):
    chunks, tall, part = own.shape
    each = (chunks // count, tall, part)
    return pl.pallas_call(
        add_kernel,
        in_specs=[VMEM] * (1 + len(others)),
        out_specs=[VMEM] * count,
        out_shape=[jax.ShapeDtypeStruct(each, BF16)] * count,
        compiler_params=limits(8),
        name="terms",
    )(own, *others)


def finish_kernel(capacity, pairs, relative, count, ids_ref, weights_ref, combined_ref, *refs):
    got, out_ref = refs[:count], refs[count]
    rows = combined_ref.shape[0]
    part = got[0].shape[2]
    parts = 8 // capacity
    places = sum(piece.shape[0] for piece in got) * 8
    row = lax.broadcasted_iota(jnp.int32, (rows, places), 0)
    place = lax.broadcasted_iota(jnp.int32, (rows, places), 1)
    slot = place // (pairs * 8) * capacity + place % capacity
    in_part = place % 8 // capacity
    weighting = jnp.zeros((rows, places), F32)
    me = lax.axis_index("expert") if relative else 0
    for (t, k), at in slots_of(ids_ref, capacity, me).items():
        weighting = jnp.where((slot == at) & (row == t), weights_ref[k, t], weighting)
    terms = jnp.concatenate([piece[...].reshape(-1, part) for piece in got], axis=0)
    for h in range(parts):
        at = slice(h * part, (h + 1) * part)
        high, low = halves_of(jnp.where(in_part == h, weighting, 0.0))
        mixture = dot(high, terms) + dot(low, terms)
        out_ref[:, at] = (combined_ref[:, at] + mixture).astype(BF16)


def finish(ids, weights, combined, got, capacity, pairs, relative):
    return pl.pallas_call(
        functools.partial(finish_kernel, capacity, pairs, relative, len(got)),
        in_specs=[SMEM, SMEM, VMEM] + [VMEM] * len(got),
        out_specs=VMEM,
        out_shape=jax.ShapeDtypeStruct(combined.shape, BF16),
        compiler_params=limits(8),
        name="finish",
    )(*in_hbm(ids, weights), combined, *got)


def swap(x, axes, by):
    return lax.ppermute(x, axes, [(i, i ^ by) for i in range(lax.axis_size(axes))]) if by else x


def on_device(
    queries,
    key_rows,
    value_rows,
    states,
    decay_rates,
    head_gain,
    out_weight,
    residual,
    norm_gain,
    expert_ids,
    gate_weights,
    expert_gate,
    expert_up,
    expert_down,
):
    experts = lax.axis_size("expert")
    pairs = lax.axis_size("pair")
    subs = lax.axis_size("sub")
    inner = ("half", "sub")
    everyone = ("expert", "half", "pair", "sub")
    plane = ("expert", "pair")
    inners = lax.axis_size(inner)
    local_rows, width = residual.shape
    columns = out_weight.shape[1]
    capacity = max(2, local_rows * expert_ids.shape[1] // experts)
    ids, weights = expert_ids.T, gate_weights.T
    relative = experts * pairs * inners <= 16 and columns % 128 == 0

    attended = attend(queries, key_rows, value_rows, states, decay_rates, head_gain)
    out_here, gate_here = load([out_weight, expert_gate], attended, "load_first")
    pieces = []
    for d in range(experts):
        piece = swap(attended, "expert", d)
        pieces += [swap(piece, inner, c) for c in range(inners)]
    blocks = project(pieces, out_here, local_rows, experts, inners, relative)

    up_here, residual_here, gain_here = load(
        [expert_up, residual, norm_gain.reshape(1, -1)], blocks[0], "load_second"
    )
    if relative:
        got = [swap(block, everyone, d) for d, block in enumerate(blocks)]
    else:
        got = lax.all_to_all(blocks[0], everyone, split_axis=0, concat_axis=0, tiled=True)
        got = got.reshape(experts * 2, pairs, subs, local_rows, columns).astype(F32)
        got = [jnp.transpose(got.sum(axis=1), (2, 0, 1, 3)).reshape(local_rows, width)]
    combined, *outgoing = pack(
        ids, residual_here, gain_here, got, capacity, experts, pairs, subs, relative
    )

    if relative:
        routed = []
        for d, rows in enumerate(outgoing):
            rows = swap(rows, "expert", d)
            routed += [swap(rows, "pair", p) for p in range(pairs)]
    else:
        routed = [lax.all_to_all(outgoing[0], plane, split_axis=0, concat_axis=0, tiled=True)]
    routed = [swap(rows, inner, c) for c in range(inners) for rows in routed]
    own, others = expert_apply(routed, gate_here, up_here, expert_down, capacity, inners)

    others = [swap(others[c - 1 : c], inner, c) for c in range(1, inners)]
    terms = add_terms(own, others, len(routed) // inners)
    if relative:
        back = [swap(term, plane, d) for d, term in enumerate(terms)]
    else:
        back = [lax.all_to_all(terms[0], plane, split_axis=0, concat_axis=0, tiled=True)]
    return finish(ids, weights, combined, back, capacity, pairs, relative)


def solution(mesh):
    sizes = dict(mesh.shape)
    experts = sizes["dev"] // 2
    cut = Mesh(
        mesh.devices.reshape(sizes["grp"], experts, 2, sizes["pair"], sizes["sub"]),
        ("grp", "expert", "half", "pair", "sub"),
    )
    dev = ("expert", "half")
    requests = P(("grp",) + dev + ("sub",), "pair")
    tokens = P(("grp",) + dev + ("pair", "sub"), None)
    units = P(dev + ("pair", "sub"), None)
    return jax.shard_map(
        on_device,
        mesh=cut,
        in_specs=(
            requests,
            requests,
            requests,
            P(("grp",) + dev + ("sub",), "pair", None, None),
            P("pair"),
            P("pair"),
            P("pair", dev + ("sub",)),
            tokens,
            P(),
            tokens,
            tokens,
            units,
            units,
            units,
        ),
        out_specs=tokens,
        check_vma=False,
    )
```

```python
import functools

import jax
import jax.numpy as jnp
from jax import lax
from jax.experimental import pallas as pl
from jax.experimental.pallas import tpu as pltpu
from jax.sharding import Mesh
from jax.sharding import PartitionSpec as P

EPSILON = 1e-06
F32 = jnp.float32
BF16 = jnp.bfloat16
MIB = 1 << 20
ID_LANES = 128
HIGHEST = lax.Precision.HIGHEST
VMEM = pl.BlockSpec(memory_space=pltpu.VMEM)
SMEM = pl.BlockSpec(memory_space=pltpu.SMEM)
ANY = pl.BlockSpec(memory_space=pl.ANY)


def in_hbm(*arrays):
    return [pltpu.with_memory_space_constraint(a, pltpu.HBM) for a in arrays]


def limits(mib):
    return pltpu.CompilerParams(vmem_limit_bytes=mib * MIB)


def dot(a, b):
    return jnp.dot(a, b, preferred_element_type=F32)


def dot_t(a, b):
    return lax.dot_general(a, b, (((1,), (1,)), ((), ())), preferred_element_type=F32)


def halves_of(x):
    high = x.astype(BF16)
    return high, (x - high.astype(F32)).astype(BF16)


def attend_kernel(positions, steps, decay_ref, ids_ref, q_ref, k_ref, v_ref, gain_ref, s_ref, residual_ref, *refs):
    weight_hbm, norm_hbm, gate_hbm = refs[:3]
    outs, copies_out, sem = refs[3:-4], refs[-4:-1], refs[-1]
    requests, heads, size, _ = s_ref.shape
    rows = q_ref.shape[0]
    step = pl.program_id(0)
    first = step * heads
    copies = [
        pltpu.make_async_copy(source, target, sem.at[i])
        for i, (source, target) in enumerate(
            zip((weight_hbm, norm_hbm, gate_hbm.at[: copies_out[2].shape[0]]), copies_out)
        )
    ]

    @pl.when(step == 0)
    def _():
        copies[0].start()
        copies[1].start()
        width = steps * heads * size
        lanes = ID_LANES
        row = lax.broadcasted_iota(jnp.int32, (rows, lanes), 0)
        lane = lax.broadcasted_iota(jnp.int32, (rows, lanes), 1)
        ids = jnp.zeros((rows, lanes), jnp.int32)
        for k in range(ids_ref.shape[0]):
            for t in range(ids_ref.shape[1]):
                ids = jnp.where((row == t) & (lane == k), ids_ref[k, t], ids)
        ids = ids.astype(F32).astype(BF16)
        columns = outs[0].shape[1] - width - lanes
        expert = lax.axis_index("expert")
        for d, out in enumerate(outs):
            out[:, width : width + lanes] = ids
            base = (expert ^ d) * 2 * columns
            both = [
                residual_ref[:, pl.ds(pl.multiple_of(base + h * columns, columns), columns)]
                for h in range(2)
            ]
            both = jnp.concatenate([b.astype(F32) for b in both], axis=0)
            out[:, width + lanes :] = both.astype(BF16)

    @pl.when(step == min(1, steps - 1))
    def _():
        copies[2].start()

    row = lax.broadcasted_iota(jnp.int32, (rows, rows), 0)
    col = lax.broadcasted_iota(jnp.int32, (rows, rows), 1)
    seen = (row // positions == col // positions) & (row >= col)
    distance = jnp.maximum(row - col, 0).astype(F32)
    owner = lax.broadcasted_iota(jnp.int32, (rows, size), 0)
    age = (owner % positions + 1).astype(F32)
    for i in range(heads):
        rate = decay_ref[first + i]
        at = slice(i * size, (i + 1) * size)
        q = q_ref[:, at]
        spread_q = jnp.concatenate(
            [jnp.where(owner // positions == r, q, jnp.zeros_like(q)) for r in range(requests)],
            axis=1,
        )
        high, low = halves_of(s_ref[:, i].reshape(requests * size, size))
        from_state = (dot(spread_q, high) + dot(spread_q, low)) * jnp.exp(-rate * age)
        scores = jnp.where(seen, dot_t(q, k_ref[:, at]) * jnp.exp(-rate * distance), 0.0)
        score_high, score_low = halves_of(scores)
        v = v_ref[:, at]
        mixed = from_state + dot(score_high, v) + dot(score_low, v)
        spread = jnp.mean(mixed * mixed, axis=1, keepdims=True)
        normal = mixed * lax.rsqrt(spread + EPSILON) * gain_ref[:, at]
        normal = normal.astype(BF16)
        for out in outs:
            out[:, pl.ds(pl.multiple_of((first + i) * size, size), size)] = normal

    @pl.when(step == steps - 1)
    def _():
        for copy in copies:
            copy.wait()


def attend(
    queries, key_rows, value_rows, states, decay_rates, head_gain, ids, residual, weight, norm_gain, gate, block, experts
):
    requests, heads, size, _ = states.shape
    rows = queries.shape[0]
    step = 4 if heads % 4 == 0 else 1
    wide = pl.BlockSpec((rows, step * size), lambda i: (0, i))
    message = (rows, queries.shape[1] + ID_LANES + weight.shape[1])
    kept = [(weight.shape, weight.dtype), (norm_gain.shape, F32), ((block, gate.shape[1]), gate.dtype)]
    return pl.pallas_call(
        functools.partial(attend_kernel, rows // requests, heads // step),
        grid=(heads // step,),
        in_specs=[
            SMEM,
            SMEM,
            wide,
            wide,
            wide,
            pl.BlockSpec((1, step * size), lambda i: (0, i)),
            pl.BlockSpec((requests, step, size, size), lambda i: (0, i, 0, 0)),
            pl.BlockSpec(residual.shape, lambda i: (0, 0)),
            ANY,
            ANY,
            ANY,
        ],
        out_specs=[pl.BlockSpec(message, lambda i: (0, 0))] * experts + [VMEM] * 3,
        out_shape=[jax.ShapeDtypeStruct(message, BF16)] * experts
        + [pltpu.VMEM(shape, dtype) for shape, dtype in kept],
        scratch_shapes=[pltpu.SemaphoreType.DMA((3,))],
        compiler_params=limits(8),
        name="attention",
    )(
        *in_hbm(
            decay_rates, ids, queries, key_rows, value_rows, head_gain.reshape(1, -1), states, residual,
            weight, norm_gain, gate,
        )
    )


def project_kernel(*refs):
    pieces, weight_ref, keep_ref, send_ref, x_ref, product_ref = refs[:-5], *refs[-5:]
    depth = weight_ref.shape[0]
    rows = pieces[0].shape[0]
    expert, half, pair = lax.axis_index("expert"), lax.axis_index("half"), lax.axis_index("pair")
    for j, piece in enumerate(pieces):
        base = (expert ^ (j // 2)) * 2 + (half ^ (j % 2))
        x_ref[pl.ds(pl.multiple_of(base * rows, rows), rows)] = piece[:, :depth]
    product_ref[...] = dot(x_ref[...], weight_ref[...])
    own = rows // 2
    for b in range(len(pieces)):
        mine = pl.ds(pl.multiple_of(b * rows + pair * own, own), own)
        keep_ref[b * own : (b + 1) * own] = product_ref[mine]
    for b in range(0, len(pieces), 2):
        theirs = [
            product_ref[pl.ds(pl.multiple_of(c * rows + (1 - pair) * own, own), own)]
            for c in (b, b + 1)
        ]
        send_ref[b * own : (b + 2) * own] = jnp.concatenate(theirs, axis=0).astype(BF16)


def project(pieces, weight):
    rows = pieces[0].shape[0] * len(pieces)
    depth, columns = weight.shape
    return pl.pallas_call(
        project_kernel,
        in_specs=[VMEM] * (len(pieces) + 1),
        out_specs=[VMEM] * 2,
        out_shape=[
            jax.ShapeDtypeStruct((rows // 2, columns), F32),
            jax.ShapeDtypeStruct((rows // 2, columns), BF16),
        ],
        scratch_shapes=[pltpu.VMEM((rows, depth), BF16), pltpu.VMEM((rows, columns), F32)],
        compiler_params=limits(8),
        name="projection",
    )(*pieces, weight)


def route_kernel(capacity, top, *refs):
    pieces, choose_ref, residual_ref, ids_ref = refs[:-4], *refs[-3:]
    columns = residual_ref.shape[1]
    own = pieces[0].shape[0] // 2
    rows = ids_ref.shape[0]
    experts = len(pieces) // 2
    expert, half = lax.axis_index("expert"), lax.axis_index("half")
    for j, piece in enumerate(pieces):
        base = (expert ^ (j // 2)) * 2 + (half ^ (j % 2))
        at = pl.ds(pl.multiple_of(base * own, own), own)
        last = piece.shape[1] - columns
        both = piece[:, last:].astype(F32)
        residual_ref[at] = jnp.where(half == 0, both[:own], both[own:])
        ids_ref[at] = piece[:, last - ID_LANES : last].astype(F32)[:own]
    ids = ids_ref[...].T
    line = lax.broadcasted_iota(jnp.int32, (8, rows), 0)
    wanted = jnp.bitwise_xor(line, expert).astype(F32)
    named = jnp.zeros((8, rows), F32)
    for k in range(top):
        named = named + jnp.where(ids[k : k + 1] == wanted, 1.0, 0.0)
    before = lax.broadcasted_iota(jnp.int32, (rows, rows), 0)
    after = lax.broadcasted_iota(jnp.int32, (rows, rows), 1)
    earlier = jnp.where((before // own == after // own) & (before < after), 1.0, 0.0)
    rank = dot(named.astype(BF16), earlier.astype(BF16))
    dev = lax.broadcasted_iota(jnp.int32, (8, rows), 1) // own
    place = (dev % 2 * experts + dev // 2) * capacity
    place = jnp.where(named > 0.5, place.astype(F32) + rank, -1.0)
    count = choose_ref.shape[0] // experts
    slot = lax.broadcasted_iota(jnp.int32, (count, rows), 0).astype(F32)
    for d in range(experts):
        choose_ref[d * count : (d + 1) * count] = jnp.where(
            slot == place[d : d + 1], 1.0, 0.0
        ).astype(BF16)


def route(pieces, after, columns, capacity, top):
    rows = pieces[0].shape[0] // 2 * len(pieces)
    experts = len(pieces) // 2
    return pl.pallas_call(
        functools.partial(route_kernel, capacity, top),
        in_specs=[VMEM] * len(pieces) + [ANY],
        out_specs=[VMEM] * 2,
        out_shape=[
            jax.ShapeDtypeStruct((experts * 2 * experts * capacity, rows), BF16),
            jax.ShapeDtypeStruct((rows, columns), F32),
        ],
        scratch_shapes=[pltpu.VMEM((rows, ID_LANES), F32)],
        compiler_params=limits(4),
        cost_estimate=pl.CostEstimate(flops=10**6, bytes_accessed=10**6, transcendentals=0),
        name="route",
    )(*pieces, after)


def pack_kernel(keep_ref, got_ref, residual_ref, choose_ref, *refs):
    outs, sum_ref = refs[:-1], refs[-1]
    sum_ref[...] = keep_ref[...] + got_ref[...].astype(F32)
    combined = (sum_ref[...] + residual_ref[...]).astype(BF16)
    packed = dot(choose_ref[...], combined).astype(BF16)
    count = choose_ref.shape[0] // len(outs)
    own = outs[0].shape[0] - count
    expert = lax.axis_index("expert")
    for d, out in enumerate(outs):
        out[:count] = packed[d * count : (d + 1) * count]
        at = pl.ds(pl.multiple_of((expert ^ d) * own, own), own)
        out[count:] = sum_ref[at].astype(BF16)


def pack(keep, got, residual, choose, experts):
    rows, columns = keep.shape
    count = choose.shape[0] // experts
    return pl.pallas_call(
        pack_kernel,
        in_specs=[VMEM] * 4,
        out_specs=[VMEM] * experts,
        out_shape=[jax.ShapeDtypeStruct((count + rows // experts, columns), BF16)] * experts,
        scratch_shapes=[pltpu.VMEM((rows, columns), F32)],
        compiler_params=limits(4),
        name="pack",
    )(keep, got, residual, choose)


def expert_kernel(count, block, wide, *refs):
    near, far = refs[:8], refs[8:16]
    gain_ref, first_ref, gate_hbm, up_hbm, down_hbm = refs[16:21]
    keep_ref, send_ref = refs[21:23]
    x_ref, turned_ref, hidden_ref, gate_ref, up_ref, down_ref, gate_sem, up_sem, down_sem = refs[23:]
    units, width = up_hbm.shape
    columns = width // len(near)
    rows = x_ref.shape[0]
    blocks, panels = units // block, width // wide

    def copy_of(hbm, ref, sem, t):
        at = pl.ds(t * block, block)
        return pltpu.make_async_copy(hbm.at[at], ref.at[at], sem.at[t])

    def down_copy(n):
        at = pl.ds(n * wide, wide)
        return pltpu.make_async_copy(down_hbm.at[:, at], down_ref.at[:, at], down_sem.at[n])

    for t in range(blocks):
        if t:
            copy_of(gate_hbm, gate_ref, gate_sem, t).start()
        copy_of(up_hbm, up_ref, up_sem, t).start()
    for n in range(panels):
        down_copy(n).start()

    expert, half = lax.axis_index("expert"), lax.axis_index("half")
    for p, pieces in enumerate((near, far)):
        for j, piece in enumerate(pieces):
            base = ((expert ^ (j // 2)) * 2 + (half ^ (j % 2))) * columns
            at = pl.ds(pl.multiple_of(base, columns), columns)
            x_ref[p * count : (p + 1) * count, at] = piece[:count].astype(F32)
    squares = jnp.zeros((rows, 128), F32)
    for b in range(width // 128):
        x = x_ref[:, b * 128 : (b + 1) * 128]
        squares = squares + x * x
    scale = lax.rsqrt(jnp.sum(squares, axis=1, keepdims=True) / width + EPSILON)
    for b in range(len(near)):
        at = slice(b * columns, (b + 1) * columns)
        normed = x_ref[:, at] * scale * gain_ref[:, at]
        turned_ref[at] = normed.T.astype(BF16)

    for t in range(blocks):
        at = slice(t * block, (t + 1) * block)
        if t:
            copy_of(gate_hbm, gate_ref, gate_sem, t).wait()
            gate_value = dot(gate_ref[at], turned_ref[...])
        else:
            gate_value = dot(first_ref[...], turned_ref[...])
        copy_of(up_hbm, up_ref, up_sem, t).wait()
        lifted = dot(up_ref[at], turned_ref[...])
        hidden = gate_value / (1.0 + jnp.exp(-gate_value)) * lifted
        hidden_ref[:, at] = hidden.T.astype(BF16)

    part = count // 2
    for n in range(panels):
        down_copy(n).wait()
        at = slice(n * wide, (n + 1) * wide)
        total = dot(hidden_ref[...], down_ref[:, at])
        for p in range(2):
            low = total[p * count : p * count + part]
            high = total[p * count + part : (p + 1) * count]
            to = slice(p * part, (p + 1) * part)
            keep_ref[to, at] = jnp.where(half == 0, low, high)
            send_ref[to, at] = jnp.where(half == 0, high, low).astype(BF16)


def expert_apply(near, far, gain, first, gate_part, up_part, down_part, count):
    units, width = gate_part.shape
    block = first.shape[0]
    wide = 512
    return pl.pallas_call(
        functools.partial(expert_kernel, count, block, wide),
        in_specs=[VMEM] * 18 + [ANY] * 3,
        out_specs=(VMEM, VMEM),
        out_shape=(
            jax.ShapeDtypeStruct((count, width), F32),
            jax.ShapeDtypeStruct((count, width), BF16),
        ),
        scratch_shapes=[
            pltpu.VMEM((2 * count, width), F32),
            pltpu.VMEM((width, 2 * count), BF16),
            pltpu.VMEM((2 * count, units), BF16),
            pltpu.VMEM((units, width), BF16),
            pltpu.VMEM((units, width), BF16),
            pltpu.VMEM((units, width), BF16),
            pltpu.SemaphoreType.DMA((units // block,)),
            pltpu.SemaphoreType.DMA((units // block,)),
            pltpu.SemaphoreType.DMA((width // wide,)),
        ],
        compiler_params=limits(52),
        name="experts",
    )(*near, *far, gain, first, *in_hbm(gate_part, up_part, down_part))


def chip_sum_kernel(mine_ref, got_ref, keep_ref, send_ref):
    rows = keep_ref.shape[0]
    keep_ref[...] = mine_ref[:rows] + got_ref[:rows].astype(F32)
    send_ref[...] = (mine_ref[rows:] + got_ref[rows:].astype(F32)).astype(BF16)


def chip_sum(mine, got):
    rows, width = mine.shape
    return pl.pallas_call(
        chip_sum_kernel,
        in_specs=[VMEM] * 2,
        out_specs=[VMEM] * 2,
        out_shape=[
            jax.ShapeDtypeStruct((rows // 2, width), F32),
            jax.ShapeDtypeStruct((rows // 2, width), BF16),
        ],
        compiler_params=limits(4),
        name="chip_sum",
    )(mine, got)


def pair_sum_kernel(capacity, keep_ref, got_ref, *refs):
    outs, fold_ref = refs[:-1], refs[-1]
    experts = len(outs)
    parts = 8 // capacity
    part = outs[0].shape[1]
    total = keep_ref[...] + got_ref[...].astype(F32)
    for e in range(experts):
        mine = total[e * capacity : (e + 1) * capacity]
        fold_ref[e] = jnp.concatenate(
            [mine[:, h * part : (h + 1) * part] for h in range(parts)], axis=0
        )
    expert = lax.axis_index("expert")
    for d, out in enumerate(outs):
        out[...] = fold_ref[expert ^ d].astype(BF16)


def pair_sum(keep, got, capacity, experts):
    part = keep.shape[1] * capacity // 8
    return pl.pallas_call(
        functools.partial(pair_sum_kernel, capacity),
        in_specs=[VMEM] * 2,
        out_specs=[VMEM] * experts,
        out_shape=[jax.ShapeDtypeStruct((8, part), BF16)] * experts,
        scratch_shapes=[pltpu.VMEM((experts, 8, part), F32)],
        compiler_params=limits(4),
        name="pair_sum",
    )(keep, got)


def own_rows_kernel(capacity, count, ids_ref, weights_ref, residual_ref, *refs):
    pieces, combined_ref, weighting_ref = refs[:-3], *refs[-2:]
    rows = combined_ref.shape[0]
    columns = pieces[0].shape[1]
    expert, half = lax.axis_index("expert"), lax.axis_index("half")
    for j, piece in enumerate(pieces):
        base = ((expert ^ (j // 2)) * 2 + (half ^ (j % 2))) * columns
        at = pl.ds(pl.multiple_of(base, columns), columns)
        both = piece[count:].astype(F32)
        mine = jnp.where(half == 0, both[:rows], both[rows:])
        combined_ref[:, at] = residual_ref[:, at].astype(F32) + mine
    places = weighting_ref.shape[1]
    row = lax.broadcasted_iota(jnp.int32, (rows, places), 0)
    place = lax.broadcasted_iota(jnp.int32, (rows, places), 1)
    slot = place // 8 * capacity + place % capacity
    weighting = jnp.zeros((rows, places), F32)
    top = ids_ref.shape[0]
    order = [(t, k) for t in range(rows) for k in range(top)]
    named = [ids_ref[k, t] for t, k in order]
    for j, (t, k) in enumerate(order):
        rank = jnp.int32(0)
        for i in range(j):
            rank = rank + jnp.where(named[i] == named[j], 1, 0)
        at = (named[j] ^ expert) * capacity + rank
        weighting = jnp.where((slot == at) & (row == t), weights_ref[k, t], weighting)
    for h in range(8 // capacity):
        high, low = halves_of(jnp.where(place % 8 // capacity == h, weighting, 0.0))
        both = jnp.concatenate([high.astype(F32), low.astype(F32)], axis=0)
        weighting_ref[h * 16 : (h + 1) * 16] = both.astype(BF16)


def own_rows(ids, weights, residual, pieces, after, capacity, count):
    rows, width = residual.shape
    experts = len(pieces) // 2
    return pl.pallas_call(
        functools.partial(own_rows_kernel, capacity, count),
        in_specs=[SMEM, SMEM, VMEM] + [VMEM] * len(pieces) + [ANY],
        out_specs=[VMEM] * 2,
        out_shape=[
            jax.ShapeDtypeStruct((rows, width), F32),
            jax.ShapeDtypeStruct((16 * (8 // capacity), experts * 8), BF16),
        ],
        compiler_params=limits(4),
        cost_estimate=pl.CostEstimate(flops=10**6, bytes_accessed=10**6, transcendentals=0),
        name="own_rows",
    )(*in_hbm(ids, weights, residual), *pieces, after)


def finish_kernel(combined_ref, weighting_ref, *refs):
    got, out_ref = refs[:-1], refs[-1]
    part = got[0].shape[1]
    rows = combined_ref.shape[0]
    terms = jnp.concatenate([piece[...].astype(F32) for piece in got], axis=0).astype(BF16)
    for h in range(combined_ref.shape[1] // part):
        at = slice(h * part, (h + 1) * part)
        mixture = dot(weighting_ref[h * 16 : (h + 1) * 16], terms)
        out_ref[:, at] = (combined_ref[:, at] + mixture[:rows] + mixture[rows:]).astype(BF16)


def finish(combined, weighting, got):
    return pl.pallas_call(
        finish_kernel,
        in_specs=[VMEM] * (2 + len(got)),
        out_specs=VMEM,
        out_shape=jax.ShapeDtypeStruct(combined.shape, BF16),
        compiler_params=limits(4),
        name="finish",
    )(combined, weighting, *got)


def swap(x, axis, by):
    return lax.ppermute(x, axis, [(i, i ^ by) for i in range(lax.axis_size(axis))]) if by else x


def on_chips(
    queries,
    key_rows,
    value_rows,
    states,
    decay_rates,
    head_gain,
    out_weight,
    residual,
    norm_gain,
    expert_ids,
    gate_weights,
    expert_gate,
    expert_up,
    expert_down,
):
    experts = lax.axis_size("expert")
    local_rows = residual.shape[0]
    columns = out_weight.shape[1]
    top = expert_ids.shape[1]
    capacity = max(2, local_rows * top // experts)
    count = 2 * experts * capacity
    block = next(b for b in (384, 256, 128) if expert_gate.shape[0] % b == 0)
    ids, weights = expert_ids.T, gate_weights.T

    *messages, weight_here, gain_here, gate_first = attend(
        queries, key_rows, value_rows, states, decay_rates, head_gain, ids, residual,
        out_weight, norm_gain.reshape(1, -1), expert_gate, block, experts,
    )
    pieces = []
    for d, message in enumerate(messages):
        message = swap(message, "expert", d)
        pieces += [message, swap(message, "half", 1)]

    keep, send = project(pieces, weight_here)
    choose, residual_part = route(pieces, keep, columns, capacity, top)
    packed = pack(keep, swap(send, "pair", 1), residual_part, choose, experts)

    near, far = [], []
    for d, rows in enumerate(packed):
        rows = swap(rows, "expert", d)
        crossed = swap(rows[:count], "pair", 1)
        near += [rows, swap(rows, "half", 1)]
        far += [crossed, swap(crossed, "half", 1)]
    mine, send = expert_apply(
        near, far, gain_here, gate_first, expert_gate, expert_up, expert_down, count
    )

    combined, weighting = own_rows(ids, weights, residual, near, mine, capacity, count)
    keep, send = chip_sum(mine, swap(send, "half", 1))
    terms = pair_sum(keep, swap(send, "pair", 1), capacity, experts)
    back = [swap(term, "expert", d) for d, term in enumerate(terms)]
    return finish(combined, weighting, back)


def plain_attend(queries, key_rows, value_rows, states, decay_rates, head_gain):
    requests = states.shape[0]
    head_count = states.shape[1]
    head_size = states.shape[2]
    positions = queries.shape[0] // requests
    layout = (requests, positions, head_count, head_size)
    query_plain = queries.reshape(layout)
    key_plain = key_rows.reshape(layout)
    query_float = query_plain.astype(jnp.float32)
    value_float = value_rows.reshape(layout).astype(jnp.float32)
    offsets = jnp.arange(positions, dtype=jnp.float32)
    carried = jnp.exp(-decay_rates[None, :] * (offsets[:, None] + 1.0))
    from_state = jnp.einsum("rphk,rhkv->rphv", query_float, states, precision=HIGHEST)
    from_state = from_state * carried[None, :, :, None]
    scores = jnp.einsum(
        "rthk,rjhk->rhtj", query_plain, key_plain, preferred_element_type=jnp.float32
    )
    distance = offsets[:, None] - offsets[None, :]
    fading = jnp.exp(-decay_rates[:, None, None] * jnp.maximum(distance, 0.0)[None, :, :])
    fading = jnp.where(distance[None, :, :] >= 0.0, fading, 0.0)
    scores = scores * fading[None]
    within = jnp.einsum("rhtj,rjhv->rthv", scores, value_float, precision=HIGHEST)
    mixed_heads = from_state + within
    spread = jnp.mean(mixed_heads * mixed_heads, axis=3, keepdims=True)
    normal = (
        mixed_heads
        * lax.rsqrt(spread + EPSILON)
        * head_gain.reshape(head_count, head_size)[None, None]
    )
    return normal.astype(jnp.bfloat16).reshape(requests * positions, head_count * head_size)


def plain_experts(picked, gate_part, up_part, down_part):
    leading = picked.shape
    flattened = picked.reshape(-1, leading[-1])
    contract = (((1,), (1,)), ((), ()))
    gate_value = lax.dot_general(flattened, gate_part, contract, preferred_element_type=jnp.float32)
    lifted = lax.dot_general(flattened, up_part, contract, preferred_element_type=jnp.float32)
    hidden = (jax.nn.silu(gate_value) * lifted).astype(jnp.bfloat16)
    output = jnp.dot(hidden, down_part, preferred_element_type=jnp.float32)
    return output.reshape(leading)


def plain(
    queries,
    key_rows,
    value_rows,
    states,
    decay_rates,
    head_gain,
    out_weight,
    residual,
    norm_gain,
    expert_ids,
    gate_weights,
    expert_gate,
    expert_up,
    expert_down,
):
    outer_count = lax.axis_size("dev")
    pair_count = lax.axis_size("pair")
    core_count = lax.axis_size("sub")
    attended = plain_attend(queries, key_rows, value_rows, states, decay_rates, head_gain)
    partial_value = jnp.dot(
        lax.all_gather(attended, ("dev", "sub"), axis=0, tiled=True),
        out_weight,
        preferred_element_type=jnp.float32,
    )
    local_rows = residual.shape[0]
    columns = partial_value.shape[1]
    blocks = partial_value.reshape(outer_count, pair_count, core_count, local_rows, columns)
    ordered = jnp.transpose(blocks, (1, 0, 2, 3, 4)).reshape(
        pair_count, outer_count * core_count * local_rows, columns
    )
    shared = lax.psum_scatter(ordered, "pair", scatter_dimension=0, tiled=True)
    shared = shared.reshape(outer_count * core_count, local_rows, columns)
    regrouped = lax.all_to_all(shared, ("dev", "sub"), split_axis=0, concat_axis=2, tiled=True)
    own_rows = regrouped[0]
    combined = residual.astype(jnp.float32) + own_rows
    spread = jnp.mean(combined * combined, axis=-1, keepdims=True)
    normed = (combined * lax.rsqrt(spread + EPSILON) * norm_gain).astype(jnp.bfloat16)
    width = normed.shape[1]
    top_count = expert_ids.shape[1]
    expert_count = outer_count // 2
    capacity = max(2, local_rows * top_count // expert_count)
    chosen_ids = expert_ids.reshape(-1)
    choose = (chosen_ids[:, None] == jnp.arange(expert_count, dtype=jnp.int32)[None, :]).astype(
        jnp.int32
    )
    before = jnp.cumsum(choose, axis=0) - choose
    position = jnp.sum(before * choose, axis=1)
    target = chosen_ids * capacity + position
    placing = (
        target[None, :] == jnp.arange(expert_count * capacity, dtype=jnp.int32)[:, None]
    ).astype(jnp.bfloat16)
    repeated = jnp.repeat(normed, top_count, axis=0)
    packed = jnp.dot(placing, repeated, preferred_element_type=jnp.float32).astype(jnp.bfloat16)
    slot_rows = packed.reshape(expert_count, 1, capacity, width)
    outgoing = jnp.broadcast_to(slot_rows, (expert_count, 2, capacity, width)).reshape(
        outer_count, capacity, width
    )
    partials = plain_experts(
        lax.all_gather(
            lax.all_to_all(outgoing, "dev", split_axis=0, concat_axis=0, tiled=True)[None],
            ("pair", "sub"),
            axis=0,
            tiled=True,
        ),
        expert_gate,
        expert_up,
        expert_down,
    )
    summed_terms = lax.psum_scatter(partials, ("pair", "sub"), scatter_dimension=0, tiled=True)
    returned = lax.all_to_all(summed_terms[0], "dev", split_axis=0, concat_axis=0, tiled=True)
    halves = jnp.sum(returned.reshape(expert_count, -1, capacity, width), axis=1).reshape(
        expert_count * capacity, width
    )
    weighting = placing.astype(jnp.float32) * gate_weights.reshape(-1)[None, :]
    per_slot = lax.dot_general(
        weighting,
        halves,
        (((0,), (0,)), ((), ())),
        precision=HIGHEST,
        preferred_element_type=jnp.float32,
    )
    mixture = jnp.sum(per_slot.reshape(local_rows, top_count, width), axis=1)
    return (combined + mixture).astype(jnp.bfloat16)


def solution(mesh):
    sizes = dict(mesh.shape)
    plain_axes = (("dev",), ("pair", "sub"), ("sub",))
    chip_axes = (("expert", "half"), ("pair",), ())

    def specs(dev, inner, sub):
        requests = P(("grp",) + dev + sub, "pair")
        tokens = P(("grp",) + dev + inner, None)
        units = P(dev + inner, None)
        arguments = (
            requests,
            requests,
            requests,
            P(("grp",) + dev + sub, "pair", None, None),
            P("pair"),
            P("pair"),
            P("pair", dev + sub),
            tokens,
            P(),
            tokens,
            tokens,
            units,
            units,
            units,
        )
        return dict(in_specs=arguments, out_specs=tokens, check_vma=False)

    experts = sizes["dev"] // 2
    chips = sizes["pair"] == 2 and sizes["sub"] == 1 and experts in (2, 4, 8)

    def run(*arguments):
        rows = arguments[7].shape[0] // mesh.size
        columns = arguments[6].shape[1] // (sizes["dev"] * sizes["sub"])
        units = arguments[11].shape[0] * sizes["grp"] // mesh.size
        if chips and rows == 8 and columns % 128 == 0 and units % 128 == 0:
            cut = Mesh(
                mesh.devices.reshape(sizes["grp"], experts, 2, 2),
                ("grp", "expert", "half", "pair"),
            )
            return jax.shard_map(on_chips, mesh=cut, **specs(*chip_axes))(*arguments)
        return jax.shard_map(plain, mesh=mesh, **specs(*plain_axes))(*arguments)

    return run
```

```python
import functools

import jax
import jax.numpy as jnp
from jax import lax
from jax.experimental import pallas as pl
from jax.experimental.pallas import tpu as pltpu
from jax.sharding import Mesh
from jax.sharding import PartitionSpec as P

EPSILON = 1e-06
F32 = jnp.float32
BF16 = jnp.bfloat16
MIB = 1 << 20
ID_LANES = 128
HIGHEST = lax.Precision.HIGHEST
VMEM = pl.BlockSpec(memory_space=pltpu.VMEM)
SMEM = pl.BlockSpec(memory_space=pltpu.SMEM)
ANY = pl.BlockSpec(memory_space=pl.ANY)


def in_hbm(*arrays):
    return [pltpu.with_memory_space_constraint(a, pltpu.HBM) for a in arrays]


def limits(mib):
    return pltpu.CompilerParams(vmem_limit_bytes=mib * MIB)


def dot(a, b):
    return jnp.dot(a, b, preferred_element_type=F32)


def dot_t(a, b):
    return lax.dot_general(a, b, (((1,), (1,)), ((), ())), preferred_element_type=F32)


def halves_of(x):
    high = x.astype(BF16)
    return high, (x - high.astype(F32)).astype(BF16)


def attend_kernel(positions, steps, decay_ref, ids_ref, q_ref, k_ref, v_ref, gain_ref, s_ref, residual_ref, *refs):
    sources, outs, targets, sem = refs[:2], refs[2:-3], refs[-3:-1], refs[-1]
    requests, heads, size, _ = s_ref.shape
    rows = q_ref.shape[0]
    step = pl.program_id(0)
    first = step * heads
    copies = [
        pltpu.make_async_copy(source, target, sem.at[i])
        for i, (source, target) in enumerate(zip(sources, targets))
    ]

    @pl.when(step == 0)
    def _():
        for copy in copies:
            copy.start()
        width = steps * heads * size
        lanes = ID_LANES
        row = lax.broadcasted_iota(jnp.int32, (rows, lanes), 0)
        lane = lax.broadcasted_iota(jnp.int32, (rows, lanes), 1)
        ids = jnp.zeros((rows, lanes), jnp.int32)
        for k in range(ids_ref.shape[0]):
            for t in range(ids_ref.shape[1]):
                ids = jnp.where((row == t) & (lane == k), ids_ref[k, t], ids)
        ids = ids.astype(F32).astype(BF16)
        columns = outs[0].shape[1] - width - lanes
        expert = lax.axis_index("expert")
        for d, out in enumerate(outs):
            out[:, width : width + lanes] = ids
            base = (expert ^ d) * 2 * columns
            both = [
                residual_ref[:, pl.ds(pl.multiple_of(base + h * columns, columns), columns)]
                for h in range(2)
            ]
            both = jnp.concatenate([b.astype(F32) for b in both], axis=0)
            out[:, width + lanes :] = both.astype(BF16)

    row = lax.broadcasted_iota(jnp.int32, (rows, rows), 0)
    col = lax.broadcasted_iota(jnp.int32, (rows, rows), 1)
    seen = (row // positions == col // positions) & (row >= col)
    distance = jnp.maximum(row - col, 0).astype(F32)
    owner = lax.broadcasted_iota(jnp.int32, (rows, size), 0)
    age = (owner % positions + 1).astype(F32)
    for i in range(heads):
        rate = decay_ref[first + i]
        at = slice(i * size, (i + 1) * size)
        q = q_ref[:, at]
        spread_q = jnp.concatenate(
            [jnp.where(owner // positions == r, q, jnp.zeros_like(q)) for r in range(requests)],
            axis=1,
        )
        high, low = halves_of(s_ref[:, i].reshape(requests * size, size))
        from_state = (dot(spread_q, high) + dot(spread_q, low)) * jnp.exp(-rate * age)
        scores = jnp.where(seen, dot_t(q, k_ref[:, at]) * jnp.exp(-rate * distance), 0.0)
        score_high, score_low = halves_of(scores)
        v = v_ref[:, at]
        mixed = from_state + dot(score_high, v) + dot(score_low, v)
        spread = jnp.mean(mixed * mixed, axis=1, keepdims=True)
        normal = mixed * lax.rsqrt(spread + EPSILON) * gain_ref[:, at]
        normal = normal.astype(BF16)
        for out in outs:
            out[:, pl.ds(pl.multiple_of((first + i) * size, size), size)] = normal

    @pl.when(step == steps - 1)
    def _():
        for copy in copies:
            copy.wait()


def attend(
    queries, key_rows, value_rows, states, decay_rates, head_gain, ids, residual, weight, norm_gain, experts
):
    requests, heads, size, _ = states.shape
    rows = queries.shape[0]
    step = 4 if heads % 4 == 0 else 1
    wide = pl.BlockSpec((rows, step * size), lambda i: (0, i))
    message = (rows, queries.shape[1] + ID_LANES + weight.shape[1])
    return pl.pallas_call(
        functools.partial(attend_kernel, rows // requests, heads // step),
        grid=(heads // step,),
        in_specs=[
            SMEM,
            SMEM,
            wide,
            wide,
            wide,
            pl.BlockSpec((1, step * size), lambda i: (0, i)),
            pl.BlockSpec((requests, step, size, size), lambda i: (0, i, 0, 0)),
            pl.BlockSpec(residual.shape, lambda i: (0, 0)),
            ANY,
            ANY,
        ],
        out_specs=[pl.BlockSpec(message, lambda i: (0, 0))] * experts + [VMEM] * 2,
        out_shape=[jax.ShapeDtypeStruct(message, BF16)] * experts
        + [pltpu.VMEM(a.shape, a.dtype) for a in (weight, norm_gain)],
        scratch_shapes=[pltpu.SemaphoreType.DMA((2,))],
        compiler_params=limits(8),
        name="attention",
    )(
        *in_hbm(
            decay_rates, ids, queries, key_rows, value_rows, head_gain.reshape(1, -1), states, residual,
            weight, norm_gain,
        )
    )


def load_kernel(rows_hbm, weight_hbm, rows_ref, weight_ref, sem):
    copies = [
        pltpu.make_async_copy(weight_hbm, weight_ref, sem.at[0]),
        pltpu.make_async_copy(rows_hbm, rows_ref, sem.at[1]),
    ]
    for copy in copies:
        copy.start()
    for copy in copies:
        copy.wait()


def load(rows, weight):
    return pl.pallas_call(
        load_kernel,
        in_specs=[ANY, ANY],
        out_specs=[VMEM, VMEM],
        out_shape=[
            jax.ShapeDtypeStruct(rows.shape, rows.dtype),
            pltpu.VMEM(weight.shape, weight.dtype),
        ],
        scratch_shapes=[pltpu.SemaphoreType.DMA((2,))],
        compiler_params=limits(1),
        cost_estimate=pl.CostEstimate(
            flops=0, bytes_accessed=weight.size * weight.dtype.itemsize, transcendentals=0
        ),
        name="load",
    )(rows, *in_hbm(weight))


def project_kernel(*refs):
    pieces, weight_ref, keep_ref, send_ref, x_ref, product_ref = refs[:-5], *refs[-5:]
    depth = weight_ref.shape[0]
    rows = pieces[0].shape[0]
    expert, half, pair = lax.axis_index("expert"), lax.axis_index("half"), lax.axis_index("pair")
    for j, piece in enumerate(pieces):
        base = (expert ^ (j // 2)) * 2 + (half ^ (j % 2))
        x_ref[pl.ds(pl.multiple_of(base * rows, rows), rows)] = piece[:, :depth]
    product_ref[...] = dot(x_ref[...], weight_ref[...])
    own = rows // 2
    for b in range(len(pieces)):
        mine = pl.ds(pl.multiple_of(b * rows + pair * own, own), own)
        keep_ref[b * own : (b + 1) * own] = product_ref[mine]
    for b in range(0, len(pieces), 2):
        theirs = [
            product_ref[pl.ds(pl.multiple_of(c * rows + (1 - pair) * own, own), own)]
            for c in (b, b + 1)
        ]
        send_ref[b * own : (b + 2) * own] = jnp.concatenate(theirs, axis=0).astype(BF16)


def project(pieces, weight):
    rows = pieces[0].shape[0] * len(pieces)
    depth, columns = weight.shape
    return pl.pallas_call(
        project_kernel,
        in_specs=[VMEM] * (len(pieces) + 1),
        out_specs=[VMEM] * 2,
        out_shape=[
            jax.ShapeDtypeStruct((rows // 2, columns), F32),
            jax.ShapeDtypeStruct((rows // 2, columns), BF16),
        ],
        scratch_shapes=[pltpu.VMEM((rows, depth), BF16), pltpu.VMEM((rows, columns), F32)],
        compiler_params=limits(8),
        name="projection",
    )(*pieces, weight)


def route_kernel(capacity, top, *refs):
    pieces, weight_hbm = refs[:-7], refs[-6]
    choose_ref, residual_ref, weight_ref, ids_ref, sem = refs[-5:]
    copy = pltpu.make_async_copy(weight_hbm.at[: weight_ref.shape[0]], weight_ref, sem)
    copy.start()
    columns = residual_ref.shape[1]
    own = pieces[0].shape[0] // 2
    rows = ids_ref.shape[0]
    experts = len(pieces) // 2
    expert, half = lax.axis_index("expert"), lax.axis_index("half")
    for j, piece in enumerate(pieces):
        base = (expert ^ (j // 2)) * 2 + (half ^ (j % 2))
        at = pl.ds(pl.multiple_of(base * own, own), own)
        last = piece.shape[1] - columns
        both = piece[:, last:].astype(F32)
        residual_ref[at] = jnp.where(half == 0, both[:own], both[own:])
        ids_ref[at] = piece[:, last - ID_LANES : last].astype(F32)[:own]
    ids = ids_ref[...].T
    line = lax.broadcasted_iota(jnp.int32, (8, rows), 0)
    wanted = jnp.bitwise_xor(line, expert).astype(F32)
    named = jnp.zeros((8, rows), F32)
    for k in range(top):
        named = named + jnp.where(ids[k : k + 1] == wanted, 1.0, 0.0)
    before = lax.broadcasted_iota(jnp.int32, (rows, rows), 0)
    after = lax.broadcasted_iota(jnp.int32, (rows, rows), 1)
    earlier = jnp.where((before // own == after // own) & (before < after), 1.0, 0.0)
    rank = dot(named.astype(BF16), earlier.astype(BF16))
    dev = lax.broadcasted_iota(jnp.int32, (8, rows), 1) // own
    place = (dev % 2 * experts + dev // 2) * capacity
    place = jnp.where(named > 0.5, place.astype(F32) + rank, -1.0)
    count = choose_ref.shape[0] // experts
    slot = lax.broadcasted_iota(jnp.int32, (count, rows), 0).astype(F32)
    for d in range(experts):
        choose_ref[d * count : (d + 1) * count] = jnp.where(
            slot == place[d : d + 1], 1.0, 0.0
        ).astype(BF16)
    copy.wait()


def route(pieces, after, columns, capacity, top, weight, first):
    rows = pieces[0].shape[0] // 2 * len(pieces)
    experts = len(pieces) // 2
    return pl.pallas_call(
        functools.partial(route_kernel, capacity, top),
        in_specs=[VMEM] * len(pieces) + [ANY] * 2,
        out_specs=[VMEM] * 3,
        out_shape=[
            jax.ShapeDtypeStruct((experts * 2 * experts * capacity, rows), BF16),
            jax.ShapeDtypeStruct((rows, columns), F32),
            pltpu.VMEM((first, weight.shape[1]), weight.dtype),
        ],
        scratch_shapes=[pltpu.VMEM((rows, ID_LANES), F32), pltpu.SemaphoreType.DMA],
        compiler_params=limits(4),
        cost_estimate=pl.CostEstimate(flops=10**6, bytes_accessed=8 * 10**6, transcendentals=0),
        name="route",
    )(*pieces, after, *in_hbm(weight))


def pack_kernel(keep_ref, got_ref, residual_ref, choose_ref, *refs):
    outs, own_ref, sum_ref = refs[:-2], refs[-2], refs[-1]
    sum_ref[...] = keep_ref[...] + got_ref[...].astype(F32)
    combined = (sum_ref[...] + residual_ref[...]).astype(BF16)
    packed = dot(choose_ref[...], combined).astype(BF16)
    count = choose_ref.shape[0] // len(outs)
    own = own_ref.shape[1]
    expert = lax.axis_index("expert")
    for d, out in enumerate(outs):
        out[...] = packed[d * count : (d + 1) * count]
        at = pl.ds(pl.multiple_of((expert ^ d) * own, own), own)
        own_ref[d] = sum_ref[at].astype(BF16)


def pack(keep, got, residual, choose, experts):
    rows, columns = keep.shape
    count = choose.shape[0] // experts
    return pl.pallas_call(
        pack_kernel,
        in_specs=[VMEM] * 4,
        out_specs=[VMEM] * (experts + 1),
        out_shape=[jax.ShapeDtypeStruct((count, columns), BF16)] * experts
        + [jax.ShapeDtypeStruct((experts, rows // experts, columns), BF16)],
        scratch_shapes=[pltpu.VMEM((rows, columns), F32)],
        compiler_params=limits(4),
        name="pack",
    )(keep, got, residual, choose)


def expert_kernel(count, wide, each, *refs):
    groups = 16 // each // 4
    near, near_cross, far, far_cross = (refs[g * groups : (g + 1) * groups] for g in range(4))
    refs = refs[4 * groups :]
    gain_ref, gate_ref, first_ref, up_hbm, down_hbm = refs[:5]
    keep_ref, send_ref, x_ref, turned_ref, hidden_ref, rest_ref, down_ref, sem, down_sem = refs[5:]
    units, width = up_hbm.shape
    columns = width // 8
    rows = x_ref.shape[0]
    cut = first_ref.shape[0]
    rest = pltpu.make_async_copy(up_hbm.at[cut:], rest_ref, sem)
    rest.start()
    thirds = down_sem.shape[0]
    tall = units // thirds
    downs = [
        pltpu.make_async_copy(
            down_hbm.at[t * tall : (t + 1) * tall], down_ref.at[t * tall : (t + 1) * tall], down_sem.at[t]
        )
        for t in range(thirds)
    ]

    expert, half = lax.axis_index("expert"), lax.axis_index("half")
    for p, halves in enumerate(((near, near_cross), (far, far_cross))):
        for c, pieces in enumerate(halves):
            for d in range(4):
                piece = pieces[d // each][d % each * count : (d % each + 1) * count]
                base = ((expert ^ d) * 2 + (half ^ c)) * columns
                at = pl.ds(pl.multiple_of(base, columns), columns)
                x_ref[p * count : (p + 1) * count, at] = piece.astype(F32)
    squares = jnp.zeros((rows, 128), F32)
    for b in range(width // 128):
        x = x_ref[:, b * 128 : (b + 1) * 128]
        squares = squares + x * x
    scale = lax.rsqrt(jnp.sum(squares, axis=1, keepdims=True) / width + EPSILON)
    for b in range(8):
        at = slice(b * columns, (b + 1) * columns)
        normed = x_ref[:, at] * scale * gain_ref[:, at]
        turned_ref[at] = normed.T.astype(BF16)
    downs[0].start()

    for at, up_ref in ((slice(0, cut), first_ref), (slice(cut, units), rest_ref)):
        gate_value = dot(gate_ref[at], turned_ref[...])
        if up_ref is rest_ref:
            rest.wait()
            for down in downs[1:]:
                down.start()
        lifted = dot(up_ref[...], turned_ref[...])
        hidden = gate_value / (1.0 + jnp.exp(-gate_value)) * lifted
        hidden_ref[:, at] = hidden.T.astype(BF16)

    part = count // 2
    for down in downs:
        down.wait()
    for n in range(width // wide):
        at = slice(n * wide, (n + 1) * wide)
        total = dot(hidden_ref[...], down_ref[:, at])
        for p in range(2):
            low = total[p * count : p * count + part]
            high = total[p * count + part : (p + 1) * count]
            to = slice(p * part, (p + 1) * part)
            keep_ref[to, at] = jnp.where(half == 0, low, high)
            send_ref[to, at] = jnp.where(half == 0, high, low).astype(BF16)


def expert_apply(pieces, gain, gate, first, up_part, down_part, count):
    units, width = up_part.shape
    wide = 512
    each = pieces[0].shape[0] // count
    return pl.pallas_call(
        functools.partial(expert_kernel, count, wide, each),
        in_specs=[VMEM] * (len(pieces) + 3) + [ANY] * 2,
        out_specs=(VMEM, VMEM),
        out_shape=(
            jax.ShapeDtypeStruct((count, width), F32),
            jax.ShapeDtypeStruct((count, width), BF16),
        ),
        scratch_shapes=[
            pltpu.VMEM((2 * count, width), F32),
            pltpu.VMEM((width, 2 * count), BF16),
            pltpu.VMEM((2 * count, units), BF16),
            pltpu.VMEM((units - first.shape[0], width), BF16),
            pltpu.VMEM((units, width), BF16),
            pltpu.SemaphoreType.DMA,
            pltpu.SemaphoreType.DMA((3,)),
        ],
        compiler_params=limits(30),
        name="experts",
    )(*pieces, gain, gate, first, *in_hbm(up_part, down_part))


def chip_sum_kernel(mine_ref, got_ref, own_ref, keep_ref, send_ref, *outs):
    rows = keep_ref.shape[0]
    keep_ref[...] = mine_ref[:rows] + got_ref[:rows].astype(F32)
    send_ref[...] = (mine_ref[rows:] + got_ref[rows:].astype(F32)).astype(BF16)
    for d, out in enumerate(outs):
        out[...] = own_ref[d]


def chip_sum(mine, got, own):
    rows, width = mine.shape
    return pl.pallas_call(
        chip_sum_kernel,
        in_specs=[VMEM] * 3,
        out_specs=[VMEM] * (2 + own.shape[0]),
        out_shape=[
            jax.ShapeDtypeStruct((rows // 2, width), F32),
            jax.ShapeDtypeStruct((rows // 2, width), BF16),
        ]
        + [jax.ShapeDtypeStruct(own.shape[1:], BF16)] * own.shape[0],
        compiler_params=limits(4),
        name="chip_sum",
    )(mine, got, own)


def pair_sum_kernel(capacity, keep_ref, got_ref, *refs):
    outs, fold_ref = refs[:-1], refs[-1]
    experts = len(outs)
    parts = 8 // capacity
    part = outs[0].shape[1]
    total = keep_ref[...] + got_ref[...].astype(F32)
    for e in range(experts):
        mine = total[e * capacity : (e + 1) * capacity]
        fold_ref[e] = jnp.concatenate(
            [mine[:, h * part : (h + 1) * part] for h in range(parts)], axis=0
        )
    expert = lax.axis_index("expert")
    for d, out in enumerate(outs):
        out[...] = fold_ref[expert ^ d].astype(BF16)


def pair_sum(keep, got, capacity, experts):
    part = keep.shape[1] * capacity // 8
    return pl.pallas_call(
        functools.partial(pair_sum_kernel, capacity),
        in_specs=[VMEM] * 2,
        out_specs=[VMEM] * experts,
        out_shape=[jax.ShapeDtypeStruct((8, part), BF16)] * experts,
        scratch_shapes=[pltpu.VMEM((experts, 8, part), F32)],
        compiler_params=limits(4),
        name="pair_sum",
    )(keep, got)


def own_rows_kernel(capacity, ids_ref, weights_ref, residual_ref, *refs):
    pieces, cross_ref, combined_ref, weighting_ref = refs[:-3], *refs[-3:]
    rows = combined_ref.shape[0]
    columns = pieces[0].shape[1]
    expert, half = lax.axis_index("expert"), lax.axis_index("half")
    for d, piece in enumerate(pieces):
        cross = cross_ref[d * 2 * rows : (d + 1) * 2 * rows]
        for c, both in enumerate((piece[...], cross)):
            base = ((expert ^ d) * 2 + (half ^ c)) * columns
            at = pl.ds(pl.multiple_of(base, columns), columns)
            both = both.astype(F32)
            mine = jnp.where(half == 0, both[:rows], both[rows:])
            combined_ref[:, at] = residual_ref[:, at].astype(F32) + mine
    places = weighting_ref.shape[1]
    row = lax.broadcasted_iota(jnp.int32, (rows, places), 0)
    place = lax.broadcasted_iota(jnp.int32, (rows, places), 1)
    slot = place // 8 * capacity + place % capacity
    weighting = jnp.zeros((rows, places), F32)
    top = ids_ref.shape[0]
    order = [(t, k) for t in range(rows) for k in range(top)]
    named = [ids_ref[k, t] for t, k in order]
    for j, (t, k) in enumerate(order):
        rank = jnp.int32(0)
        for i in range(j):
            rank = rank + jnp.where(named[i] == named[j], 1, 0)
        at = (named[j] ^ expert) * capacity + rank
        weighting = jnp.where((slot == at) & (row == t), weights_ref[k, t], weighting)
    for h in range(8 // capacity):
        high, low = halves_of(jnp.where(place % 8 // capacity == h, weighting, 0.0))
        both = jnp.concatenate([high.astype(F32), low.astype(F32)], axis=0)
        weighting_ref[h * 16 : (h + 1) * 16] = both.astype(BF16)


def own_rows(ids, weights, residual, pieces, cross, capacity):
    rows, width = residual.shape
    experts = len(pieces)
    return pl.pallas_call(
        functools.partial(own_rows_kernel, capacity),
        in_specs=[SMEM, SMEM, VMEM] + [VMEM] * (experts + 1),
        out_specs=[VMEM] * 2,
        out_shape=[
            jax.ShapeDtypeStruct((rows, width), F32),
            jax.ShapeDtypeStruct((16 * (8 // capacity), experts * 8), BF16),
        ],
        compiler_params=limits(4),
        cost_estimate=pl.CostEstimate(flops=10**6, bytes_accessed=10**6, transcendentals=0),
        name="own_rows",
    )(*in_hbm(ids, weights, residual), *pieces, cross)


def finish_kernel(combined_ref, weighting_ref, *refs):
    got, out_ref = refs[:-1], refs[-1]
    part = got[0].shape[1]
    rows = combined_ref.shape[0]
    terms = jnp.concatenate([piece[...].astype(F32) for piece in got], axis=0).astype(BF16)
    for h in range(combined_ref.shape[1] // part):
        at = slice(h * part, (h + 1) * part)
        mixture = dot(weighting_ref[h * 16 : (h + 1) * 16], terms)
        out_ref[:, at] = (combined_ref[:, at] + mixture[:rows] + mixture[rows:]).astype(BF16)


def finish(combined, weighting, got):
    return pl.pallas_call(
        finish_kernel,
        in_specs=[VMEM] * (2 + len(got)),
        out_specs=VMEM,
        out_shape=jax.ShapeDtypeStruct(combined.shape, BF16),
        compiler_params=limits(4),
        name="finish",
    )(combined, weighting, *got)


def swap(x, axis, by):
    return lax.ppermute(x, axis, [(i, i ^ by) for i in range(lax.axis_size(axis))]) if by else x


def on_chips(
    queries,
    key_rows,
    value_rows,
    states,
    decay_rates,
    head_gain,
    out_weight,
    residual,
    norm_gain,
    expert_ids,
    gate_weights,
    expert_gate,
    expert_up,
    expert_down,
):
    experts = lax.axis_size("expert")
    local_rows = residual.shape[0]
    columns = out_weight.shape[1]
    top = expert_ids.shape[1]
    capacity = max(2, local_rows * top // experts)
    count = 2 * experts * capacity
    ids, weights = expert_ids.T, gate_weights.T

    *messages, weight_here, gain_here = attend(
        queries, key_rows, value_rows, states, decay_rates, head_gain, ids, residual,
        out_weight, norm_gain.reshape(1, -1), experts,
    )
    messages[0], gate_here = load(messages[0], expert_gate)
    pieces = []
    for d, message in enumerate(messages):
        message = swap(message, "expert", d)
        pieces += [message, swap(message, "half", 1)]

    keep, send = project(pieces, weight_here)
    first = expert_up.shape[0] // 256 * 128 + 128
    choose, residual_part, up_first = route(
        pieces, keep, columns, capacity, top, expert_up, first
    )
    *packed, own = pack(keep, swap(send, "pair", 1), residual_part, choose, experts)

    order = [2, 3, 1, 0]
    arrived = {d: swap(packed[d], "expert", d) for d in order}
    near = [jnp.concatenate([arrived[d], arrived[d + 1]], axis=0) for d in range(0, experts, 2)]
    far = [swap(rows, "pair", 1) for rows in near]
    routed = near + [swap(n, "half", 1) for n in near] + far + [swap(f, "half", 1) for f in far]
    mine, send = expert_apply(
        routed, gain_here, gate_here, up_first, expert_up, expert_down, count
    )

    keep, send, *own = chip_sum(mine, swap(send, "half", 1), own)
    terms = pair_sum(keep, swap(send, "pair", 1), capacity, experts)
    own = [swap(rows, "expert", d) for d, rows in enumerate(own)]
    cross = swap(jnp.concatenate(own, axis=0), "half", 1)
    combined, weighting = own_rows(ids, weights, residual, own, cross, capacity)
    back = [swap(term, "expert", d) for d, term in enumerate(terms)]
    return finish(combined, weighting, back)


def plain_attend(queries, key_rows, value_rows, states, decay_rates, head_gain):
    requests = states.shape[0]
    head_count = states.shape[1]
    head_size = states.shape[2]
    positions = queries.shape[0] // requests
    layout = (requests, positions, head_count, head_size)
    query_plain = queries.reshape(layout)
    key_plain = key_rows.reshape(layout)
    query_float = query_plain.astype(jnp.float32)
    value_float = value_rows.reshape(layout).astype(jnp.float32)
    offsets = jnp.arange(positions, dtype=jnp.float32)
    carried = jnp.exp(-decay_rates[None, :] * (offsets[:, None] + 1.0))
    from_state = jnp.einsum("rphk,rhkv->rphv", query_float, states, precision=HIGHEST)
    from_state = from_state * carried[None, :, :, None]
    scores = jnp.einsum(
        "rthk,rjhk->rhtj", query_plain, key_plain, preferred_element_type=jnp.float32
    )
    distance = offsets[:, None] - offsets[None, :]
    fading = jnp.exp(-decay_rates[:, None, None] * jnp.maximum(distance, 0.0)[None, :, :])
    fading = jnp.where(distance[None, :, :] >= 0.0, fading, 0.0)
    scores = scores * fading[None]
    within = jnp.einsum("rhtj,rjhv->rthv", scores, value_float, precision=HIGHEST)
    mixed_heads = from_state + within
    spread = jnp.mean(mixed_heads * mixed_heads, axis=3, keepdims=True)
    normal = (
        mixed_heads
        * lax.rsqrt(spread + EPSILON)
        * head_gain.reshape(head_count, head_size)[None, None]
    )
    return normal.astype(jnp.bfloat16).reshape(requests * positions, head_count * head_size)


def plain_experts(picked, gate_part, up_part, down_part):
    leading = picked.shape
    flattened = picked.reshape(-1, leading[-1])
    contract = (((1,), (1,)), ((), ()))
    gate_value = lax.dot_general(flattened, gate_part, contract, preferred_element_type=jnp.float32)
    lifted = lax.dot_general(flattened, up_part, contract, preferred_element_type=jnp.float32)
    hidden = (jax.nn.silu(gate_value) * lifted).astype(jnp.bfloat16)
    output = jnp.dot(hidden, down_part, preferred_element_type=jnp.float32)
    return output.reshape(leading)


def plain(
    queries,
    key_rows,
    value_rows,
    states,
    decay_rates,
    head_gain,
    out_weight,
    residual,
    norm_gain,
    expert_ids,
    gate_weights,
    expert_gate,
    expert_up,
    expert_down,
):
    outer_count = lax.axis_size("dev")
    pair_count = lax.axis_size("pair")
    core_count = lax.axis_size("sub")
    attended = plain_attend(queries, key_rows, value_rows, states, decay_rates, head_gain)
    partial_value = jnp.dot(
        lax.all_gather(attended, ("dev", "sub"), axis=0, tiled=True),
        out_weight,
        preferred_element_type=jnp.float32,
    )
    local_rows = residual.shape[0]
    columns = partial_value.shape[1]
    blocks = partial_value.reshape(outer_count, pair_count, core_count, local_rows, columns)
    ordered = jnp.transpose(blocks, (1, 0, 2, 3, 4)).reshape(
        pair_count, outer_count * core_count * local_rows, columns
    )
    shared = lax.psum_scatter(ordered, "pair", scatter_dimension=0, tiled=True)
    shared = shared.reshape(outer_count * core_count, local_rows, columns)
    regrouped = lax.all_to_all(shared, ("dev", "sub"), split_axis=0, concat_axis=2, tiled=True)
    own_rows = regrouped[0]
    combined = residual.astype(jnp.float32) + own_rows
    spread = jnp.mean(combined * combined, axis=-1, keepdims=True)
    normed = (combined * lax.rsqrt(spread + EPSILON) * norm_gain).astype(jnp.bfloat16)
    width = normed.shape[1]
    top_count = expert_ids.shape[1]
    expert_count = outer_count // 2
    capacity = max(2, local_rows * top_count // expert_count)
    chosen_ids = expert_ids.reshape(-1)
    choose = (chosen_ids[:, None] == jnp.arange(expert_count, dtype=jnp.int32)[None, :]).astype(
        jnp.int32
    )
    before = jnp.cumsum(choose, axis=0) - choose
    position = jnp.sum(before * choose, axis=1)
    target = chosen_ids * capacity + position
    placing = (
        target[None, :] == jnp.arange(expert_count * capacity, dtype=jnp.int32)[:, None]
    ).astype(jnp.bfloat16)
    repeated = jnp.repeat(normed, top_count, axis=0)
    packed = jnp.dot(placing, repeated, preferred_element_type=jnp.float32).astype(jnp.bfloat16)
    slot_rows = packed.reshape(expert_count, 1, capacity, width)
    outgoing = jnp.broadcast_to(slot_rows, (expert_count, 2, capacity, width)).reshape(
        outer_count, capacity, width
    )
    partials = plain_experts(
        lax.all_gather(
            lax.all_to_all(outgoing, "dev", split_axis=0, concat_axis=0, tiled=True)[None],
            ("pair", "sub"),
            axis=0,
            tiled=True,
        ),
        expert_gate,
        expert_up,
        expert_down,
    )
    summed_terms = lax.psum_scatter(partials, ("pair", "sub"), scatter_dimension=0, tiled=True)
    returned = lax.all_to_all(summed_terms[0], "dev", split_axis=0, concat_axis=0, tiled=True)
    halves = jnp.sum(returned.reshape(expert_count, -1, capacity, width), axis=1).reshape(
        expert_count * capacity, width
    )
    weighting = placing.astype(jnp.float32) * gate_weights.reshape(-1)[None, :]
    per_slot = lax.dot_general(
        weighting,
        halves,
        (((0,), (0,)), ((), ())),
        precision=HIGHEST,
        preferred_element_type=jnp.float32,
    )
    mixture = jnp.sum(per_slot.reshape(local_rows, top_count, width), axis=1)
    return (combined + mixture).astype(jnp.bfloat16)


def solution(mesh):
    sizes = dict(mesh.shape)
    plain_axes = (("dev",), ("pair", "sub"), ("sub",))
    chip_axes = (("expert", "half"), ("pair",), ())

    def specs(dev, inner, sub):
        requests = P(("grp",) + dev + sub, "pair")
        tokens = P(("grp",) + dev + inner, None)
        units = P(dev + inner, None)
        arguments = (
            requests,
            requests,
            requests,
            P(("grp",) + dev + sub, "pair", None, None),
            P("pair"),
            P("pair"),
            P("pair", dev + sub),
            tokens,
            P(),
            tokens,
            tokens,
            units,
            units,
            units,
        )
        return dict(in_specs=arguments, out_specs=tokens, check_vma=False)

    experts = sizes["dev"] // 2
    chips = sizes["pair"] == 2 and sizes["sub"] == 1 and experts == 4

    def run(*arguments):
        rows = arguments[7].shape[0] // mesh.size
        columns = arguments[6].shape[1] // (sizes["dev"] * sizes["sub"])
        units = arguments[11].shape[0] * sizes["grp"] // mesh.size
        if chips and rows == 8 and columns % 128 == 0 and units % 384 == 0:
            cut = Mesh(
                mesh.devices.reshape(sizes["grp"], experts, 2, 2),
                ("grp", "expert", "half", "pair"),
            )
            return jax.shard_map(on_chips, mesh=cut, **specs(*chip_axes))(*arguments)
        return jax.shard_map(plain, mesh=mesh, **specs(*plain_axes))(*arguments)

    return run
```

```python
import functools

import jax
import jax.numpy as jnp
from jax import lax
from jax.experimental import pallas as pl
from jax.experimental.pallas import tpu as pltpu
from jax.sharding import Mesh
from jax.sharding import PartitionSpec as P

EPSILON = 1e-06
F32 = jnp.float32
BF16 = jnp.bfloat16
MIB = 1 << 20
ID_LANES = 128
HIGHEST = lax.Precision.HIGHEST
VMEM = pl.BlockSpec(memory_space=pltpu.VMEM)
SMEM = pl.BlockSpec(memory_space=pltpu.SMEM)
ANY = pl.BlockSpec(memory_space=pl.ANY)


def in_hbm(*arrays):
    return [pltpu.with_memory_space_constraint(a, pltpu.HBM) for a in arrays]


def limits(mib):
    return pltpu.CompilerParams(vmem_limit_bytes=mib * MIB)


def dot(a, b):
    return jnp.dot(a, b, preferred_element_type=F32)


def dot_t(a, b):
    return lax.dot_general(a, b, (((1,), (1,)), ((), ())), preferred_element_type=F32)


def halves_of(x):
    high = x.astype(BF16)
    return high, (x - high.astype(F32)).astype(BF16)


def attend_kernel(positions, steps, decay_ref, ids_ref, q_ref, k_ref, v_ref, gain_ref, s_ref, residual_ref, *refs):
    sources, outs, targets, sem = refs[:2], refs[2:-3], refs[-3:-1], refs[-1]
    requests, heads, size, _ = s_ref.shape
    rows = q_ref.shape[0]
    step = pl.program_id(0)
    first = step * heads
    copies = [
        pltpu.make_async_copy(source, target, sem.at[i])
        for i, (source, target) in enumerate(zip(sources, targets))
    ]

    @pl.when(step == 0)
    def _():
        for copy in copies:
            copy.start()
        width = steps * heads * size
        lanes = ID_LANES
        row = lax.broadcasted_iota(jnp.int32, (rows, lanes), 0)
        lane = lax.broadcasted_iota(jnp.int32, (rows, lanes), 1)
        ids = jnp.zeros((rows, lanes), jnp.int32)
        for k in range(ids_ref.shape[0]):
            for t in range(ids_ref.shape[1]):
                ids = jnp.where((row == t) & (lane == k), ids_ref[k, t], ids)
        ids = ids.astype(F32).astype(BF16)
        columns = outs[0].shape[1] - width - lanes
        expert = lax.axis_index("expert")
        for d, out in enumerate(outs):
            out[:, width : width + lanes] = ids
            base = (expert ^ d) * 2 * columns
            both = [
                residual_ref[:, pl.ds(pl.multiple_of(base + h * columns, columns), columns)]
                for h in range(2)
            ]
            both = jnp.concatenate([b.astype(F32) for b in both], axis=0)
            out[:, width + lanes :] = both.astype(BF16)

    row = lax.broadcasted_iota(jnp.int32, (rows, rows), 0)
    col = lax.broadcasted_iota(jnp.int32, (rows, rows), 1)
    seen = (row // positions == col // positions) & (row >= col)
    distance = jnp.maximum(row - col, 0).astype(F32)
    owner = lax.broadcasted_iota(jnp.int32, (rows, size), 0)
    age = (owner % positions + 1).astype(F32)
    for i in range(heads):
        rate = decay_ref[first + i]
        at = slice(i * size, (i + 1) * size)
        q = q_ref[:, at]
        spread_q = jnp.concatenate(
            [jnp.where(owner // positions == r, q, jnp.zeros_like(q)) for r in range(requests)],
            axis=1,
        )
        high, low = halves_of(s_ref[:, i].reshape(requests * size, size))
        from_state = (dot(spread_q, high) + dot(spread_q, low)) * jnp.exp(-rate * age)
        scores = jnp.where(seen, dot_t(q, k_ref[:, at]) * jnp.exp(-rate * distance), 0.0)
        score_high, score_low = halves_of(scores)
        v = v_ref[:, at]
        mixed = from_state + dot(score_high, v) + dot(score_low, v)
        spread = jnp.mean(mixed * mixed, axis=1, keepdims=True)
        normal = mixed * lax.rsqrt(spread + EPSILON) * gain_ref[:, at]
        normal = normal.astype(BF16)
        for out in outs:
            out[:, pl.ds(pl.multiple_of((first + i) * size, size), size)] = normal

    @pl.when(step == steps - 1)
    def _():
        for copy in copies:
            copy.wait()


def attend(
    queries, key_rows, value_rows, states, decay_rates, head_gain, ids, residual, weight, norm_gain, experts
):
    requests, heads, size, _ = states.shape
    rows = queries.shape[0]
    step = 4 if heads % 4 == 0 else 1
    wide = pl.BlockSpec((rows, step * size), lambda i: (0, i))
    message = (rows, queries.shape[1] + ID_LANES + weight.shape[1])
    return pl.pallas_call(
        functools.partial(attend_kernel, rows // requests, heads // step),
        grid=(heads // step,),
        in_specs=[
            SMEM,
            SMEM,
            wide,
            wide,
            wide,
            pl.BlockSpec((1, step * size), lambda i: (0, i)),
            pl.BlockSpec((requests, step, size, size), lambda i: (0, i, 0, 0)),
            pl.BlockSpec(residual.shape, lambda i: (0, 0)),
            ANY,
            ANY,
        ],
        out_specs=[pl.BlockSpec(message, lambda i: (0, 0))] * experts + [VMEM] * 2,
        out_shape=[jax.ShapeDtypeStruct(message, BF16)] * experts
        + [pltpu.VMEM(a.shape, a.dtype) for a in (weight, norm_gain)],
        scratch_shapes=[pltpu.SemaphoreType.DMA((2,))],
        compiler_params=limits(8),
        name="attention",
    )(
        *in_hbm(
            decay_rates, ids, queries, key_rows, value_rows, head_gain.reshape(1, -1), states, residual,
            weight, norm_gain,
        )
    )


def load_kernel(rows_hbm, weight_hbm, rows_ref, weight_ref, sem):
    copies = [
        pltpu.make_async_copy(weight_hbm, weight_ref, sem.at[0]),
        pltpu.make_async_copy(rows_hbm, rows_ref, sem.at[1]),
    ]
    for copy in copies:
        copy.start()
    for copy in copies:
        copy.wait()


def load(rows, weight):
    return pl.pallas_call(
        load_kernel,
        in_specs=[ANY, ANY],
        out_specs=[VMEM, VMEM],
        out_shape=[
            jax.ShapeDtypeStruct(rows.shape, rows.dtype),
            pltpu.VMEM(weight.shape, weight.dtype),
        ],
        scratch_shapes=[pltpu.SemaphoreType.DMA((2,))],
        compiler_params=limits(1),
        cost_estimate=pl.CostEstimate(
            flops=0, bytes_accessed=weight.size * weight.dtype.itemsize, transcendentals=0
        ),
        name="load",
    )(rows, *in_hbm(weight))


def project_kernel(*refs):
    pieces, weight_ref, keep_ref, send_ref, x_ref, product_ref = refs[:-5], *refs[-5:]
    depth = weight_ref.shape[0]
    rows = pieces[0].shape[0]
    expert, half, pair = lax.axis_index("expert"), lax.axis_index("half"), lax.axis_index("pair")
    for j, piece in enumerate(pieces):
        base = (expert ^ (j // 2)) * 2 + (half ^ (j % 2))
        x_ref[pl.ds(pl.multiple_of(base * rows, rows), rows)] = piece[:, :depth]
    product_ref[...] = dot(x_ref[...], weight_ref[...])
    own = rows // 2
    for b in range(len(pieces)):
        mine = pl.ds(pl.multiple_of(b * rows + pair * own, own), own)
        keep_ref[b * own : (b + 1) * own] = product_ref[mine]
    for b in range(0, len(pieces), 2):
        theirs = [
            product_ref[pl.ds(pl.multiple_of(c * rows + (1 - pair) * own, own), own)]
            for c in (b, b + 1)
        ]
        send_ref[b * own : (b + 2) * own] = jnp.concatenate(theirs, axis=0).astype(BF16)


def project(pieces, weight):
    rows = pieces[0].shape[0] * len(pieces)
    depth, columns = weight.shape
    return pl.pallas_call(
        project_kernel,
        in_specs=[VMEM] * (len(pieces) + 1),
        out_specs=[VMEM] * 2,
        out_shape=[
            jax.ShapeDtypeStruct((rows // 2, columns), F32),
            jax.ShapeDtypeStruct((rows // 2, columns), BF16),
        ],
        scratch_shapes=[pltpu.VMEM((rows, depth), BF16), pltpu.VMEM((rows, columns), F32)],
        compiler_params=limits(8),
        name="projection",
    )(*pieces, weight)


def route_kernel(capacity, own_ids_ref, weights_ref, *refs):
    pieces, weight_hbm = refs[:-8], refs[-7]
    choose_ref, residual_ref, weight_ref, weighting_ref, ids_ref, sem = refs[-6:]
    top, own_count = own_ids_ref.shape
    copy = pltpu.make_async_copy(weight_hbm.at[: weight_ref.shape[0]], weight_ref, sem)
    copy.start()
    columns = residual_ref.shape[1]
    own = pieces[0].shape[0] // 2
    rows = ids_ref.shape[0]
    experts = len(pieces) // 2
    expert, half = lax.axis_index("expert"), lax.axis_index("half")
    for j, piece in enumerate(pieces):
        base = (expert ^ (j // 2)) * 2 + (half ^ (j % 2))
        at = pl.ds(pl.multiple_of(base * own, own), own)
        last = piece.shape[1] - columns
        both = piece[:, last:].astype(F32)
        residual_ref[at] = jnp.where(half == 0, both[:own], both[own:])
        ids_ref[at] = piece[:, last - ID_LANES : last].astype(F32)[:own]
    ids = ids_ref[...].T
    line = lax.broadcasted_iota(jnp.int32, (8, rows), 0)
    wanted = jnp.bitwise_xor(line, expert).astype(F32)
    named = jnp.zeros((8, rows), F32)
    for k in range(top):
        named = named + jnp.where(ids[k : k + 1] == wanted, 1.0, 0.0)
    before = lax.broadcasted_iota(jnp.int32, (rows, rows), 0)
    after = lax.broadcasted_iota(jnp.int32, (rows, rows), 1)
    earlier = jnp.where((before // own == after // own) & (before < after), 1.0, 0.0)
    rank = dot(named.astype(BF16), earlier.astype(BF16))
    dev = lax.broadcasted_iota(jnp.int32, (8, rows), 1) // own
    place = (dev % 2 * experts + dev // 2) * capacity
    place = jnp.where(named > 0.5, place.astype(F32) + rank, -1.0)
    count = choose_ref.shape[0] // experts
    slot = lax.broadcasted_iota(jnp.int32, (count, rows), 0).astype(F32)
    for d in range(experts):
        choose_ref[d * count : (d + 1) * count] = jnp.where(
            slot == place[d : d + 1], 1.0, 0.0
        ).astype(BF16)

    places = weighting_ref.shape[1]
    row = lax.broadcasted_iota(jnp.int32, (own_count, places), 0)
    at_place = lax.broadcasted_iota(jnp.int32, (own_count, places), 1)
    slot = at_place // 8 * capacity + at_place % capacity
    weighting = jnp.zeros((own_count, places), F32)
    order = [(t, k) for t in range(own_count) for k in range(top)]
    named = [own_ids_ref[k, t] for t, k in order]
    for j, (t, k) in enumerate(order):
        rank = jnp.int32(0)
        for i in range(j):
            rank = rank + jnp.where(named[i] == named[j], 1, 0)
        to = (named[j] ^ expert) * capacity + rank
        weighting = jnp.where((slot == to) & (row == t), weights_ref[k, t], weighting)
    for h in range(8 // capacity):
        high, low = halves_of(jnp.where(at_place % 8 // capacity == h, weighting, 0.0))
        both = jnp.concatenate([high.astype(F32), low.astype(F32)], axis=0)
        weighting_ref[h * 16 : (h + 1) * 16] = both.astype(BF16)
    copy.wait()


def route(ids, weights, pieces, after, columns, capacity, weight, first):
    rows = pieces[0].shape[0] // 2 * len(pieces)
    experts = len(pieces) // 2
    return pl.pallas_call(
        functools.partial(route_kernel, capacity),
        in_specs=[SMEM] * 2 + [VMEM] * len(pieces) + [ANY] * 2,
        out_specs=[VMEM] * 4,
        out_shape=[
            jax.ShapeDtypeStruct((experts * 2 * experts * capacity, rows), BF16),
            jax.ShapeDtypeStruct((rows, columns), F32),
            pltpu.VMEM((first, weight.shape[1]), weight.dtype),
            jax.ShapeDtypeStruct((16 * (8 // capacity), experts * 8), BF16),
        ],
        scratch_shapes=[pltpu.VMEM((rows, ID_LANES), F32), pltpu.SemaphoreType.DMA],
        compiler_params=limits(4),
        cost_estimate=pl.CostEstimate(flops=10**6, bytes_accessed=8 * 10**6, transcendentals=0),
        name="route",
    )(*in_hbm(ids, weights), *pieces, after, *in_hbm(weight))


def pack_kernel(keep_ref, got_ref, residual_ref, choose_ref, *refs):
    outs, own_ref, sum_ref = refs[:-2], refs[-2], refs[-1]
    sum_ref[...] = keep_ref[...] + got_ref[...].astype(F32)
    combined = (sum_ref[...] + residual_ref[...]).astype(BF16)
    packed = dot(choose_ref[...], combined).astype(BF16)
    count = choose_ref.shape[0] // len(outs)
    own = own_ref.shape[1]
    expert = lax.axis_index("expert")
    for d, out in enumerate(outs):
        out[...] = packed[d * count : (d + 1) * count]
        at = pl.ds(pl.multiple_of((expert ^ d) * own, own), own)
        own_ref[d] = sum_ref[at].astype(BF16)


def pack(keep, got, residual, choose, experts):
    rows, columns = keep.shape
    count = choose.shape[0] // experts
    return pl.pallas_call(
        pack_kernel,
        in_specs=[VMEM] * 4,
        out_specs=[VMEM] * (experts + 1),
        out_shape=[jax.ShapeDtypeStruct((count, columns), BF16)] * experts
        + [jax.ShapeDtypeStruct((experts, rows // experts, columns), BF16)],
        scratch_shapes=[pltpu.VMEM((rows, columns), F32)],
        compiler_params=limits(4),
        name="pack",
    )(keep, got, residual, choose)


def turn(turned_ref, gain_ref, pieces, first, count):
    near, near_cross, far, far_cross = pieces
    columns = near.shape[1]
    expert, half = lax.axis_index("expert"), lax.axis_index("half")
    squares = jnp.zeros((2 * count, 128), F32)
    for d in range(2):
        for c, (mine, theirs) in enumerate(((near, far), (near_cross, far_cross))):
            rows = slice(d * count, (d + 1) * count)
            x = jnp.concatenate([mine[rows].astype(F32), theirs[rows].astype(F32)], axis=0)
            for b in range(columns // 128):
                part = x[:, b * 128 : (b + 1) * 128]
                squares = squares + part * part
            block = (expert ^ (first + d)) * 2 + (half ^ c)
            at = pl.ds(pl.multiple_of(block * columns, columns), columns)
            to = pl.ds(pl.multiple_of(block % 4 * columns, columns), columns)
            turned_ref[to] = (x * gain_ref[:, at]).T.astype(BF16)
    return squares


def half_of(ref, first):
    width = ref.shape[1] // 2
    which = (lax.axis_index("expert") ^ first) // 2
    return pl.ds(pl.multiple_of(which * width, width), width)


def expert_first_kernel(count, *refs):
    pieces, gain_ref, gate_ref, up_ref, up_hbm = refs[:4], *refs[4:8]
    gate_sum_ref, up_sum_ref, squares_ref, up_rest_ref, turned_ref, sem = refs[8:]
    cut = up_ref.shape[0]
    rest = pltpu.make_async_copy(up_hbm.at[cut:], up_rest_ref, sem)
    rest.start()
    squares_ref[...] = turn(turned_ref, gain_ref, pieces, 0, count)
    columns = half_of(gate_ref, 0)
    for at in (slice(0, cut), slice(cut, gate_ref.shape[0])):
        gate_sum_ref[at] = dot(gate_ref[at, columns], turned_ref[...])
    up_sum_ref[:cut] = dot(up_ref[:, columns], turned_ref[...])
    rest.wait()
    up_sum_ref[cut:] = dot(up_rest_ref[:, columns], turned_ref[...])


def expert_second_kernel(count, *refs):
    pieces, gain_ref, gate_ref, up_ref, up_rest_ref = refs[:4], *refs[4:8]
    gate_sum_ref, up_sum_ref, squares_ref, down_hbm, hidden_ref, down_ref, turned_ref, sem = refs[8:]
    units, width = gate_ref.shape
    cut = up_ref.shape[0]
    down = pltpu.make_async_copy(down_hbm, down_ref, sem)
    down.start()
    squares = squares_ref[...] + turn(turned_ref, gain_ref, pieces, 2, count)
    spread = jnp.sum(squares.T, axis=0, keepdims=True) / width
    scale = lax.rsqrt(spread + EPSILON)
    columns = half_of(gate_ref, 2)
    for at, weight_ref in ((slice(0, cut), up_ref), (slice(cut, units), up_rest_ref)):
        gate_value = (gate_sum_ref[at] + dot(gate_ref[at, columns], turned_ref[...])) * scale
        lifted = (up_sum_ref[at] + dot(weight_ref[:, columns], turned_ref[...])) * scale
        hidden = gate_value / (1.0 + jnp.exp(-gate_value)) * lifted
        hidden_ref[:, at] = hidden.T.astype(BF16)
    down.wait()


def down_kernel(start, wide, hidden_ref, weight_ref, keep_ref, send_ref):
    half = lax.axis_index("half")
    count = keep_ref.shape[0]
    part = count // 2
    for n in range(keep_ref.shape[1] // wide):
        at = slice(start + n * wide, start + (n + 1) * wide)
        out = slice(n * wide, (n + 1) * wide)
        total = dot(hidden_ref[...], weight_ref[:, at])
        for p in range(2):
            low = total[p * count : p * count + part]
            high = total[p * count + part : (p + 1) * count]
            to = slice(p * part, (p + 1) * part)
            keep_ref[to, out] = jnp.where(half == 0, low, high)
            send_ref[to, out] = jnp.where(half == 0, high, low).astype(BF16)


def cost(flops, size):
    return pl.CostEstimate(flops=flops, bytes_accessed=size, transcendentals=0)


def expert_first(pieces, gain, gate, up_first, up_part, count):
    units, width = gate.shape
    cut = up_first.shape[0]
    sums = jax.ShapeDtypeStruct((units, 2 * count), F32)
    return pl.pallas_call(
        functools.partial(expert_first_kernel, count),
        in_specs=[VMEM] * 7 + [ANY],
        out_specs=[VMEM] * 4,
        out_shape=[
            sums,
            sums,
            jax.ShapeDtypeStruct((2 * count, 128), F32),
            pltpu.VMEM((units - cut, width), BF16),
        ],
        scratch_shapes=[pltpu.VMEM((width // 2, 2 * count), BF16), pltpu.SemaphoreType.DMA],
        compiler_params=limits(8),
        cost_estimate=cost(4 * units * width * count, 2 * units * width),
        name="experts_first",
    )(*pieces, gain, gate, up_first, *in_hbm(up_part))


def relay_kernel(rows_ref, after_ref, out_ref):
    out_ref[...] = rows_ref[...]


def relay(rows, after):
    return pl.pallas_call(
        relay_kernel,
        in_specs=[VMEM] * 2,
        out_specs=VMEM,
        out_shape=jax.ShapeDtypeStruct(rows.shape, rows.dtype),
        compiler_params=limits(2),
        cost_estimate=cost(0, 10**5),
        name="relay",
    )(rows, after)


def expert_second(pieces, gain, gate, up_first, up_rest, sums, down_part, count):
    units, width = gate.shape
    return pl.pallas_call(
        functools.partial(expert_second_kernel, count),
        in_specs=[VMEM] * 11 + [ANY],
        out_specs=[VMEM] * 2,
        out_shape=[
            jax.ShapeDtypeStruct((2 * count, units), BF16),
            pltpu.VMEM((units, width), BF16),
        ],
        scratch_shapes=[pltpu.VMEM((width // 2, 2 * count), BF16), pltpu.SemaphoreType.DMA],
        compiler_params=limits(8),
        cost_estimate=cost(4 * units * width * count, 2 * units * width),
        name="experts_second",
    )(*pieces, gain, gate, up_first, up_rest, *sums, *in_hbm(down_part))


def expert_down(hidden, weight, start, width, count):
    return pl.pallas_call(
        functools.partial(down_kernel, start, 512),
        in_specs=[VMEM] * 2,
        out_specs=[VMEM] * 2,
        out_shape=[
            jax.ShapeDtypeStruct((count, width), F32),
            jax.ShapeDtypeStruct((count, width), BF16),
        ],
        compiler_params=limits(8),
        cost_estimate=cost(4 * hidden.size * width, 2 * hidden.shape[1] * width),
        name="experts_down",
    )(hidden, weight)


def chip_sum_kernel(count, *refs):
    mine, got, own_ref = refs[:count], refs[count : 2 * count], refs[2 * count]
    keep_ref, send_ref, *outs = refs[2 * count + 1 :]
    rows = keep_ref.shape[0]
    width = mine[0].shape[1]
    for g in range(count):
        at = slice(g * width, (g + 1) * width)
        keep_ref[:, at] = mine[g][:rows] + got[g][:rows].astype(F32)
        send_ref[:, at] = (mine[g][rows:] + got[g][rows:].astype(F32)).astype(BF16)
    for d, out in enumerate(outs):
        out[...] = own_ref[d]


def chip_sum(mine, got, own):
    rows, width = mine[0].shape
    shape = (rows // 2, width * len(mine))
    return pl.pallas_call(
        functools.partial(chip_sum_kernel, len(mine)),
        in_specs=[VMEM] * (2 * len(mine) + 1),
        out_specs=[VMEM] * (2 + own.shape[0]),
        out_shape=[jax.ShapeDtypeStruct(shape, F32), jax.ShapeDtypeStruct(shape, BF16)]
        + [jax.ShapeDtypeStruct(own.shape[1:], BF16)] * own.shape[0],
        compiler_params=limits(4),
        name="chip_sum",
    )(*mine, *got, own)


def pair_sum_kernel(capacity, keep_ref, got_ref, *refs):
    outs, fold_ref = refs[:-1], refs[-1]
    experts = len(outs)
    parts = 8 // capacity
    part = outs[0].shape[1]
    total = keep_ref[...] + got_ref[...].astype(F32)
    for e in range(experts):
        mine = total[e * capacity : (e + 1) * capacity]
        fold_ref[e] = jnp.concatenate(
            [mine[:, h * part : (h + 1) * part] for h in range(parts)], axis=0
        )
    expert = lax.axis_index("expert")
    for d, out in enumerate(outs):
        out[...] = fold_ref[expert ^ d].astype(BF16)


def pair_sum(keep, got, capacity, experts):
    part = keep.shape[1] * capacity // 8
    return pl.pallas_call(
        functools.partial(pair_sum_kernel, capacity),
        in_specs=[VMEM] * 2,
        out_specs=[VMEM] * experts,
        out_shape=[jax.ShapeDtypeStruct((8, part), BF16)] * experts,
        scratch_shapes=[pltpu.VMEM((experts, 8, part), F32)],
        compiler_params=limits(4),
        name="pair_sum",
    )(keep, got)


def own_rows_kernel(residual_ref, *refs):
    pieces, cross_ref, combined_ref = refs[:-2], *refs[-2:]
    rows = combined_ref.shape[0]
    columns = pieces[0].shape[1]
    expert, half = lax.axis_index("expert"), lax.axis_index("half")
    for d, piece in enumerate(pieces):
        cross = cross_ref[d * 2 * rows : (d + 1) * 2 * rows]
        for c, both in enumerate((piece[...], cross)):
            base = ((expert ^ d) * 2 + (half ^ c)) * columns
            at = pl.ds(pl.multiple_of(base, columns), columns)
            both = both.astype(F32)
            mine = jnp.where(half == 0, both[:rows], both[rows:])
            combined_ref[:, at] = residual_ref[:, at].astype(F32) + mine


def own_rows(residual, pieces, cross):
    return pl.pallas_call(
        own_rows_kernel,
        in_specs=[VMEM] * (len(pieces) + 2),
        out_specs=VMEM,
        out_shape=jax.ShapeDtypeStruct(residual.shape, F32),
        compiler_params=limits(4),
        cost_estimate=cost(10**6, 10**6),
        name="own_rows",
    )(*in_hbm(residual), *pieces, cross)


def finish_kernel(combined_ref, weighting_ref, *refs):
    got, out_ref = refs[:-1], refs[-1]
    part = got[0].shape[1]
    rows = combined_ref.shape[0]
    terms = jnp.concatenate([piece[...].astype(F32) for piece in got], axis=0).astype(BF16)
    for h in range(combined_ref.shape[1] // part):
        at = slice(h * part, (h + 1) * part)
        mixture = dot(weighting_ref[h * 16 : (h + 1) * 16], terms)
        out_ref[:, at] = (combined_ref[:, at] + mixture[:rows] + mixture[rows:]).astype(BF16)


def finish(combined, weighting, got):
    return pl.pallas_call(
        finish_kernel,
        in_specs=[VMEM] * (2 + len(got)),
        out_specs=VMEM,
        out_shape=jax.ShapeDtypeStruct(combined.shape, BF16),
        compiler_params=limits(4),
        name="finish",
    )(combined, weighting, *got)


def swap(x, axis, by):
    return lax.ppermute(x, axis, [(i, i ^ by) for i in range(lax.axis_size(axis))]) if by else x


def on_chips(
    queries,
    key_rows,
    value_rows,
    states,
    decay_rates,
    head_gain,
    out_weight,
    residual,
    norm_gain,
    expert_ids,
    gate_weights,
    expert_gate,
    expert_up,
    expert_down_part,
):
    experts = lax.axis_size("expert")
    local_rows = residual.shape[0]
    columns = out_weight.shape[1]
    top = expert_ids.shape[1]
    capacity = max(2, local_rows * top // experts)
    count = 2 * experts * capacity
    ids, weights = expert_ids.T, gate_weights.T

    *messages, weight_here, gain_here = attend(
        queries, key_rows, value_rows, states, decay_rates, head_gain, ids, residual,
        out_weight, norm_gain.reshape(1, -1), experts,
    )
    messages[0], gate_here = load(messages[0], expert_gate)
    pieces = []
    for d, message in enumerate(messages):
        message = swap(message, "expert", d)
        pieces += [message, swap(message, "half", 1)]

    keep, send = project(pieces, weight_here)
    first = expert_up.shape[0] // 256 * 128 + 128
    choose, residual_part, up_first, weighting = route(
        ids, weights, pieces, keep, columns, capacity, expert_up, first
    )
    *packed, own = pack(keep, swap(send, "pair", 1), residual_part, choose, experts)

    arrived = [swap(rows, "expert", d) for d, rows in enumerate(packed)]
    near = [jnp.concatenate(arrived[d : d + 2], axis=0) for d in range(0, experts, 2)]
    far = [swap(rows, "pair", 1) for rows in near]
    near_cross = [swap(rows, "half", 1) for rows in near]
    *sums, up_rest = expert_first(
        [near[0], near_cross[0], far[0], swap(far[0], "half", 1)],
        gain_here, gate_here, up_first, expert_up, count,
    )
    far[1] = relay(far[1], sums[2])
    hidden, down_here = expert_second(
        [near[1], near_cross[1], far[1], swap(far[1], "half", 1)],
        gain_here, gate_here, up_first, up_rest, sums, expert_down_part, count,
    )

    width = residual.shape[1] // 2
    mine, got = [], []
    for g in range(2):
        terms, send = expert_down(hidden, down_here, g * width, width, count)
        mine.append(terms)
        got.append(swap(send, "half", 1))
    keep, send, *own = chip_sum(mine, got, own)
    terms = pair_sum(keep, swap(send, "pair", 1), capacity, experts)
    own = [swap(rows, "expert", d) for d, rows in enumerate(own)]
    cross = swap(jnp.concatenate(own, axis=0), "half", 1)
    combined = own_rows(residual, own, cross)
    back = [swap(term, "expert", d) for d, term in enumerate(terms)]
    return finish(combined, weighting, back)


def plain_attend(queries, key_rows, value_rows, states, decay_rates, head_gain):
    requests = states.shape[0]
    head_count = states.shape[1]
    head_size = states.shape[2]
    positions = queries.shape[0] // requests
    layout = (requests, positions, head_count, head_size)
    query_plain = queries.reshape(layout)
    key_plain = key_rows.reshape(layout)
    query_float = query_plain.astype(jnp.float32)
    value_float = value_rows.reshape(layout).astype(jnp.float32)
    offsets = jnp.arange(positions, dtype=jnp.float32)
    carried = jnp.exp(-decay_rates[None, :] * (offsets[:, None] + 1.0))
    from_state = jnp.einsum("rphk,rhkv->rphv", query_float, states, precision=HIGHEST)
    from_state = from_state * carried[None, :, :, None]
    scores = jnp.einsum(
        "rthk,rjhk->rhtj", query_plain, key_plain, preferred_element_type=jnp.float32
    )
    distance = offsets[:, None] - offsets[None, :]
    fading = jnp.exp(-decay_rates[:, None, None] * jnp.maximum(distance, 0.0)[None, :, :])
    fading = jnp.where(distance[None, :, :] >= 0.0, fading, 0.0)
    scores = scores * fading[None]
    within = jnp.einsum("rhtj,rjhv->rthv", scores, value_float, precision=HIGHEST)
    mixed_heads = from_state + within
    spread = jnp.mean(mixed_heads * mixed_heads, axis=3, keepdims=True)
    normal = (
        mixed_heads
        * lax.rsqrt(spread + EPSILON)
        * head_gain.reshape(head_count, head_size)[None, None]
    )
    return normal.astype(jnp.bfloat16).reshape(requests * positions, head_count * head_size)


def plain_experts(picked, gate_part, up_part, down_part):
    leading = picked.shape
    flattened = picked.reshape(-1, leading[-1])
    contract = (((1,), (1,)), ((), ()))
    gate_value = lax.dot_general(flattened, gate_part, contract, preferred_element_type=jnp.float32)
    lifted = lax.dot_general(flattened, up_part, contract, preferred_element_type=jnp.float32)
    hidden = (jax.nn.silu(gate_value) * lifted).astype(jnp.bfloat16)
    output = jnp.dot(hidden, down_part, preferred_element_type=jnp.float32)
    return output.reshape(leading)


def plain(
    queries,
    key_rows,
    value_rows,
    states,
    decay_rates,
    head_gain,
    out_weight,
    residual,
    norm_gain,
    expert_ids,
    gate_weights,
    expert_gate,
    expert_up,
    expert_down,
):
    outer_count = lax.axis_size("dev")
    pair_count = lax.axis_size("pair")
    core_count = lax.axis_size("sub")
    attended = plain_attend(queries, key_rows, value_rows, states, decay_rates, head_gain)
    partial_value = jnp.dot(
        lax.all_gather(attended, ("dev", "sub"), axis=0, tiled=True),
        out_weight,
        preferred_element_type=jnp.float32,
    )
    local_rows = residual.shape[0]
    columns = partial_value.shape[1]
    blocks = partial_value.reshape(outer_count, pair_count, core_count, local_rows, columns)
    ordered = jnp.transpose(blocks, (1, 0, 2, 3, 4)).reshape(
        pair_count, outer_count * core_count * local_rows, columns
    )
    shared = lax.psum_scatter(ordered, "pair", scatter_dimension=0, tiled=True)
    shared = shared.reshape(outer_count * core_count, local_rows, columns)
    regrouped = lax.all_to_all(shared, ("dev", "sub"), split_axis=0, concat_axis=2, tiled=True)
    own_rows = regrouped[0]
    combined = residual.astype(jnp.float32) + own_rows
    spread = jnp.mean(combined * combined, axis=-1, keepdims=True)
    normed = (combined * lax.rsqrt(spread + EPSILON) * norm_gain).astype(jnp.bfloat16)
    width = normed.shape[1]
    top_count = expert_ids.shape[1]
    expert_count = outer_count // 2
    capacity = max(2, local_rows * top_count // expert_count)
    chosen_ids = expert_ids.reshape(-1)
    choose = (chosen_ids[:, None] == jnp.arange(expert_count, dtype=jnp.int32)[None, :]).astype(
        jnp.int32
    )
    before = jnp.cumsum(choose, axis=0) - choose
    position = jnp.sum(before * choose, axis=1)
    target = chosen_ids * capacity + position
    placing = (
        target[None, :] == jnp.arange(expert_count * capacity, dtype=jnp.int32)[:, None]
    ).astype(jnp.bfloat16)
    repeated = jnp.repeat(normed, top_count, axis=0)
    packed = jnp.dot(placing, repeated, preferred_element_type=jnp.float32).astype(jnp.bfloat16)
    slot_rows = packed.reshape(expert_count, 1, capacity, width)
    outgoing = jnp.broadcast_to(slot_rows, (expert_count, 2, capacity, width)).reshape(
        outer_count, capacity, width
    )
    partials = plain_experts(
        lax.all_gather(
            lax.all_to_all(outgoing, "dev", split_axis=0, concat_axis=0, tiled=True)[None],
            ("pair", "sub"),
            axis=0,
            tiled=True,
        ),
        expert_gate,
        expert_up,
        expert_down,
    )
    summed_terms = lax.psum_scatter(partials, ("pair", "sub"), scatter_dimension=0, tiled=True)
    returned = lax.all_to_all(summed_terms[0], "dev", split_axis=0, concat_axis=0, tiled=True)
    halves = jnp.sum(returned.reshape(expert_count, -1, capacity, width), axis=1).reshape(
        expert_count * capacity, width
    )
    weighting = placing.astype(jnp.float32) * gate_weights.reshape(-1)[None, :]
    per_slot = lax.dot_general(
        weighting,
        halves,
        (((0,), (0,)), ((), ())),
        precision=HIGHEST,
        preferred_element_type=jnp.float32,
    )
    mixture = jnp.sum(per_slot.reshape(local_rows, top_count, width), axis=1)
    return (combined + mixture).astype(jnp.bfloat16)


def solution(mesh):
    sizes = dict(mesh.shape)
    plain_axes = (("dev",), ("pair", "sub"), ("sub",))
    chip_axes = (("expert", "half"), ("pair",), ())

    def specs(dev, inner, sub):
        requests = P(("grp",) + dev + sub, "pair")
        tokens = P(("grp",) + dev + inner, None)
        units = P(dev + inner, None)
        arguments = (
            requests,
            requests,
            requests,
            P(("grp",) + dev + sub, "pair", None, None),
            P("pair"),
            P("pair"),
            P("pair", dev + sub),
            tokens,
            P(),
            tokens,
            tokens,
            units,
            units,
            units,
        )
        return dict(in_specs=arguments, out_specs=tokens, check_vma=False)

    experts = sizes["dev"] // 2
    chips = sizes["pair"] == 2 and sizes["sub"] == 1 and experts == 4

    def run(*arguments):
        rows = arguments[7].shape[0] // mesh.size
        columns = arguments[6].shape[1] // (sizes["dev"] * sizes["sub"])
        units = arguments[11].shape[0] * sizes["grp"] // mesh.size
        if chips and rows == 8 and columns % 128 == 0 and units % 384 == 0:
            cut = Mesh(
                mesh.devices.reshape(sizes["grp"], experts, 2, 2),
                ("grp", "expert", "half", "pair"),
            )
            return jax.shard_map(on_chips, mesh=cut, **specs(*chip_axes))(*arguments)
        return jax.shard_map(plain, mesh=mesh, **specs(*plain_axes))(*arguments)

    return run
```

```python
import functools

import jax
import jax.numpy as jnp
from jax import lax
from jax.experimental import pallas as pl
from jax.experimental.pallas import tpu as pltpu
from jax.sharding import Mesh
from jax.sharding import PartitionSpec as P

EPSILON = 1e-06
F32 = jnp.float32
BF16 = jnp.bfloat16
MIB = 1 << 20
ID_LANES = 128
HIGHEST = lax.Precision.HIGHEST
VMEM = pl.BlockSpec(memory_space=pltpu.VMEM)
SMEM = pl.BlockSpec(memory_space=pltpu.SMEM)
ANY = pl.BlockSpec(memory_space=pl.ANY)


def in_hbm(*arrays):
    return [pltpu.with_memory_space_constraint(a, pltpu.HBM) for a in arrays]


def limits(mib):
    return pltpu.CompilerParams(vmem_limit_bytes=mib * MIB)


def dot(a, b):
    return jnp.dot(a, b, preferred_element_type=F32)


def dot_t(a, b):
    return lax.dot_general(a, b, (((1,), (1,)), ((), ())), preferred_element_type=F32)


def halves_of(x):
    high = x.astype(BF16)
    return high, (x - high.astype(F32)).astype(BF16)


def attend_kernel(positions, steps, decay_ref, ids_ref, q_ref, k_ref, v_ref, gain_ref, s_ref, residual_ref, *refs):
    outs = refs
    requests, heads, size, _ = s_ref.shape
    rows = q_ref.shape[0]
    step = pl.program_id(0)
    first = step * heads
    @pl.when(step == 0)
    def _():
        width = steps * heads * size
        lanes = ID_LANES
        row = lax.broadcasted_iota(jnp.int32, (rows, lanes), 0)
        lane = lax.broadcasted_iota(jnp.int32, (rows, lanes), 1)
        ids = jnp.zeros((rows, lanes), jnp.int32)
        for k in range(ids_ref.shape[0]):
            for t in range(ids_ref.shape[1]):
                ids = jnp.where((row == t) & (lane == k), ids_ref[k, t], ids)
        ids = ids.astype(F32).astype(BF16)
        columns = outs[0].shape[1] - width - lanes
        expert = lax.axis_index("expert")
        for d, out in enumerate(outs):
            out[:, width : width + lanes] = ids
            base = (expert ^ d) * 2 * columns
            both = [
                residual_ref[:, pl.ds(pl.multiple_of(base + h * columns, columns), columns)]
                for h in range(2)
            ]
            both = jnp.concatenate([b.astype(F32) for b in both], axis=0)
            out[:, width + lanes :] = both.astype(BF16)

    row = lax.broadcasted_iota(jnp.int32, (rows, rows), 0)
    col = lax.broadcasted_iota(jnp.int32, (rows, rows), 1)
    seen = (row // positions == col // positions) & (row >= col)
    distance = jnp.maximum(row - col, 0).astype(F32)
    owner = lax.broadcasted_iota(jnp.int32, (rows, size), 0)
    age = (owner % positions + 1).astype(F32)
    for i in range(heads):
        rate = decay_ref[first + i]
        at = slice(i * size, (i + 1) * size)
        q = q_ref[:, at]
        spread_q = jnp.concatenate(
            [jnp.where(owner // positions == r, q, jnp.zeros_like(q)) for r in range(requests)],
            axis=1,
        )
        high, low = halves_of(s_ref[:, i].reshape(requests * size, size))
        from_state = (dot(spread_q, high) + dot(spread_q, low)) * jnp.exp(-rate * age)
        scores = jnp.where(seen, dot_t(q, k_ref[:, at]) * jnp.exp(-rate * distance), 0.0)
        score_high, score_low = halves_of(scores)
        v = v_ref[:, at]
        mixed = from_state + dot(score_high, v) + dot(score_low, v)
        spread = jnp.mean(mixed * mixed, axis=1, keepdims=True)
        normal = mixed * lax.rsqrt(spread + EPSILON) * gain_ref[:, at]
        normal = normal.astype(BF16)
        for out in outs:
            out[:, pl.ds(pl.multiple_of((first + i) * size, size), size)] = normal


def attend(
    queries, key_rows, value_rows, states, decay_rates, head_gain, ids, residual, columns, experts
):
    requests, heads, size, _ = states.shape
    rows = queries.shape[0]
    step = 4 if heads % 4 == 0 else 1
    wide = pl.BlockSpec((rows, step * size), lambda i: (0, i))
    message = (rows, queries.shape[1] + ID_LANES + columns)
    return pl.pallas_call(
        functools.partial(attend_kernel, rows // requests, heads // step),
        grid=(heads // step,),
        in_specs=[
            SMEM,
            SMEM,
            wide,
            wide,
            wide,
            pl.BlockSpec((1, step * size), lambda i: (0, i)),
            pl.BlockSpec((requests, step, size, size), lambda i: (0, i, 0, 0)),
            pl.BlockSpec(residual.shape, lambda i: (0, 0)),
        ],
        out_specs=[pl.BlockSpec(message, lambda i: (0, 0))] * experts,
        out_shape=[jax.ShapeDtypeStruct(message, BF16)] * experts,
        compiler_params=limits(8),
        name="attention",
    )(
        *in_hbm(
            decay_rates, ids, queries, key_rows, value_rows, head_gain.reshape(1, -1), states, residual,
        )
    )


def load_kernel(count, rows_hbm, *refs):
    sources, rows_ref, targets, sem = refs[:count], refs[count], refs[count + 1 : -1], refs[-1]
    copies = [
        pltpu.make_async_copy(source, target, sem.at[i])
        for i, (source, target) in enumerate(zip(sources, targets))
    ]
    copies.append(pltpu.make_async_copy(rows_hbm, rows_ref, sem.at[count]))
    for copy in copies:
        copy.start()
    for copy in copies:
        copy.wait()


def load(rows, weights):
    size = sum(w.size * w.dtype.itemsize for w in weights)
    return pl.pallas_call(
        functools.partial(load_kernel, len(weights)),
        in_specs=[ANY] * (1 + len(weights)),
        out_specs=[VMEM] * (1 + len(weights)),
        out_shape=[jax.ShapeDtypeStruct(rows.shape, rows.dtype)]
        + [pltpu.VMEM(w.shape, w.dtype) for w in weights],
        scratch_shapes=[pltpu.SemaphoreType.DMA((1 + len(weights),))],
        compiler_params=limits(1),
        cost_estimate=pl.CostEstimate(flops=0, bytes_accessed=size, transcendentals=0),
        name="load",
    )(rows, *in_hbm(*weights))


def project_kernel(*refs):
    pieces, weight_ref, keep_ref, send_ref, x_ref, product_ref = refs[:-5], *refs[-5:]
    depth = weight_ref.shape[0]
    rows = pieces[0].shape[0]
    expert, half, pair = lax.axis_index("expert"), lax.axis_index("half"), lax.axis_index("pair")
    for j, piece in enumerate(pieces):
        base = (expert ^ (j // 2)) * 2 + (half ^ (j % 2))
        x_ref[pl.ds(pl.multiple_of(base * rows, rows), rows)] = piece[:, :depth]
    product_ref[...] = dot(x_ref[...], weight_ref[...])
    own = rows // 2
    for b in range(len(pieces)):
        mine = pl.ds(pl.multiple_of(b * rows + pair * own, own), own)
        keep_ref[b * own : (b + 1) * own] = product_ref[mine]
    for b in range(0, len(pieces), 2):
        theirs = [
            product_ref[pl.ds(pl.multiple_of(c * rows + (1 - pair) * own, own), own)]
            for c in (b, b + 1)
        ]
        send_ref[b * own : (b + 2) * own] = jnp.concatenate(theirs, axis=0).astype(BF16)


def project(pieces, weight):
    rows = pieces[0].shape[0] * len(pieces)
    depth, columns = weight.shape
    return pl.pallas_call(
        project_kernel,
        in_specs=[VMEM] * (len(pieces) + 1),
        out_specs=[VMEM] * 2,
        out_shape=[
            jax.ShapeDtypeStruct((rows // 2, columns), F32),
            jax.ShapeDtypeStruct((rows // 2, columns), BF16),
        ],
        scratch_shapes=[pltpu.VMEM((rows, depth), BF16), pltpu.VMEM((rows, columns), F32)],
        compiler_params=limits(8),
        name="projection",
    )(*pieces, weight)


def route_kernel(capacity, own_ids_ref, weights_ref, *refs):
    pieces, weight_hbm = refs[:-8], refs[-7]
    choose_ref, residual_ref, weight_ref, weighting_ref, ids_ref, sem = refs[-6:]
    top, own_count = own_ids_ref.shape
    copy = pltpu.make_async_copy(weight_hbm.at[: weight_ref.shape[0]], weight_ref, sem)
    copy.start()
    columns = residual_ref.shape[1]
    own = pieces[0].shape[0] // 2
    rows = ids_ref.shape[0]
    experts = len(pieces) // 2
    expert, half = lax.axis_index("expert"), lax.axis_index("half")
    for j, piece in enumerate(pieces):
        base = (expert ^ (j // 2)) * 2 + (half ^ (j % 2))
        at = pl.ds(pl.multiple_of(base * own, own), own)
        last = piece.shape[1] - columns
        both = piece[:, last:].astype(F32)
        residual_ref[at] = jnp.where(half == 0, both[:own], both[own:])
        ids_ref[at] = piece[:, last - ID_LANES : last].astype(F32)[:own]
    ids = ids_ref[...].T
    line = lax.broadcasted_iota(jnp.int32, (8, rows), 0)
    wanted = jnp.bitwise_xor(line, expert).astype(F32)
    named = jnp.zeros((8, rows), F32)
    for k in range(top):
        named = named + jnp.where(ids[k : k + 1] == wanted, 1.0, 0.0)
    before = lax.broadcasted_iota(jnp.int32, (rows, rows), 0)
    after = lax.broadcasted_iota(jnp.int32, (rows, rows), 1)
    earlier = jnp.where((before // own == after // own) & (before < after), 1.0, 0.0)
    rank = dot(named.astype(BF16), earlier.astype(BF16))
    dev = lax.broadcasted_iota(jnp.int32, (8, rows), 1) // own
    place = (dev % 2 * experts + dev // 2) * capacity
    place = jnp.where(named > 0.5, place.astype(F32) + rank, -1.0)
    count = choose_ref.shape[0] // experts
    slot = lax.broadcasted_iota(jnp.int32, (count, rows), 0).astype(F32)
    for d in range(experts):
        choose_ref[d * count : (d + 1) * count] = jnp.where(
            slot == place[d : d + 1], 1.0, 0.0
        ).astype(BF16)

    places = weighting_ref.shape[1]
    row = lax.broadcasted_iota(jnp.int32, (own_count, places), 0)
    at_place = lax.broadcasted_iota(jnp.int32, (own_count, places), 1)
    slot = at_place // 8 * capacity + at_place % capacity
    weighting = jnp.zeros((own_count, places), F32)
    order = [(t, k) for t in range(own_count) for k in range(top)]
    named = [own_ids_ref[k, t] for t, k in order]
    for j, (t, k) in enumerate(order):
        rank = jnp.int32(0)
        for i in range(j):
            rank = rank + jnp.where(named[i] == named[j], 1, 0)
        to = (named[j] ^ expert) * capacity + rank
        weighting = jnp.where((slot == to) & (row == t), weights_ref[k, t], weighting)
    for h in range(8 // capacity):
        high, low = halves_of(jnp.where(at_place % 8 // capacity == h, weighting, 0.0))
        both = jnp.concatenate([high.astype(F32), low.astype(F32)], axis=0)
        weighting_ref[h * 16 : (h + 1) * 16] = both.astype(BF16)
    copy.wait()


def route(ids, weights, pieces, after, columns, capacity, weight, first):
    rows = pieces[0].shape[0] // 2 * len(pieces)
    experts = len(pieces) // 2
    return pl.pallas_call(
        functools.partial(route_kernel, capacity),
        in_specs=[SMEM] * 2 + [VMEM] * len(pieces) + [ANY] * 2,
        out_specs=[VMEM] * 4,
        out_shape=[
            jax.ShapeDtypeStruct((experts * 2 * experts * capacity, rows), BF16),
            jax.ShapeDtypeStruct((rows, columns), F32),
            pltpu.VMEM((first, weight.shape[1]), weight.dtype),
            jax.ShapeDtypeStruct((16 * (8 // capacity), experts * 8), BF16),
        ],
        scratch_shapes=[pltpu.VMEM((rows, ID_LANES), F32), pltpu.SemaphoreType.DMA],
        compiler_params=limits(4),
        cost_estimate=pl.CostEstimate(flops=10**6, bytes_accessed=8 * 10**6, transcendentals=0),
        name="route",
    )(*in_hbm(ids, weights), *pieces, after, *in_hbm(weight))


def pack_kernel(keep_ref, got_ref, residual_ref, choose_ref, *refs):
    outs, own_ref, sum_ref = refs[:-2], refs[-2], refs[-1]
    sum_ref[...] = keep_ref[...] + got_ref[...].astype(F32)
    combined = (sum_ref[...] + residual_ref[...]).astype(BF16)
    packed = dot(choose_ref[...], combined).astype(BF16)
    count = choose_ref.shape[0] // len(outs)
    own = own_ref.shape[1]
    expert = lax.axis_index("expert")
    for d, out in enumerate(outs):
        out[...] = packed[d * count : (d + 1) * count]
        at = pl.ds(pl.multiple_of((expert ^ d) * own, own), own)
        own_ref[d] = sum_ref[at].astype(BF16)


def pack(keep, got, residual, choose, experts):
    rows, columns = keep.shape
    count = choose.shape[0] // experts
    return pl.pallas_call(
        pack_kernel,
        in_specs=[VMEM] * 4,
        out_specs=[VMEM] * (experts + 1),
        out_shape=[jax.ShapeDtypeStruct((count, columns), BF16)] * experts
        + [jax.ShapeDtypeStruct((experts, rows // experts, columns), BF16)],
        scratch_shapes=[pltpu.VMEM((rows, columns), F32)],
        compiler_params=limits(4),
        name="pack",
    )(keep, got, residual, choose)


def turn(turned_ref, gain_ref, pieces, first, count):
    near, near_cross, far, far_cross = pieces
    columns = near.shape[1]
    expert, half = lax.axis_index("expert"), lax.axis_index("half")
    squares = jnp.zeros((2 * count, 128), F32)
    for d in range(2):
        for c, (mine, theirs) in enumerate(((near, far), (near_cross, far_cross))):
            rows = slice(d * count, (d + 1) * count)
            x = jnp.concatenate([mine[rows].astype(F32), theirs[rows].astype(F32)], axis=0)
            for b in range(columns // 128):
                part = x[:, b * 128 : (b + 1) * 128]
                squares = squares + part * part
            block = (expert ^ (first + d)) * 2 + (half ^ c)
            at = pl.ds(pl.multiple_of(block * columns, columns), columns)
            to = pl.ds(pl.multiple_of(block % 4 * columns, columns), columns)
            turned_ref[to] = (x * gain_ref[:, at]).T.astype(BF16)
    return squares


def half_of(ref, first):
    width = ref.shape[1] // 2
    which = (lax.axis_index("expert") ^ first) // 2
    return pl.ds(pl.multiple_of(which * width, width), width)


def expert_first_kernel(count, *refs):
    pieces, gain_ref, gate_ref, up_ref, up_hbm = refs[:4], *refs[4:8]
    gate_sum_ref, up_sum_ref, squares_ref, up_rest_ref, turned_ref, sem = refs[8:]
    cut = up_ref.shape[0]
    rest = pltpu.make_async_copy(up_hbm.at[cut:], up_rest_ref, sem)
    rest.start()
    squares_ref[...] = turn(turned_ref, gain_ref, pieces, 0, count)
    columns = half_of(gate_ref, 0)
    for at in (slice(0, cut), slice(cut, gate_ref.shape[0])):
        gate_sum_ref[at] = dot(gate_ref[at, columns], turned_ref[...])
    up_sum_ref[:cut] = dot(up_ref[:, columns], turned_ref[...])
    rest.wait()
    up_sum_ref[cut:] = dot(up_rest_ref[:, columns], turned_ref[...])


def expert_second_kernel(count, *refs):
    pieces, gain_ref, gate_ref, up_ref, up_rest_ref = refs[:4], *refs[4:8]
    gate_sum_ref, up_sum_ref, squares_ref, down_hbm, hidden_ref, down_ref, turned_ref, sem = refs[8:]
    units, width = gate_ref.shape
    cut = up_ref.shape[0]
    down = pltpu.make_async_copy(down_hbm, down_ref, sem)
    down.start()
    squares = squares_ref[...] + turn(turned_ref, gain_ref, pieces, 2, count)
    spread = jnp.sum(squares.T, axis=0, keepdims=True) / width
    scale = lax.rsqrt(spread + EPSILON)
    columns = half_of(gate_ref, 2)
    for at, weight_ref in ((slice(0, cut), up_ref), (slice(cut, units), up_rest_ref)):
        gate_value = (gate_sum_ref[at] + dot(gate_ref[at, columns], turned_ref[...])) * scale
        lifted = (up_sum_ref[at] + dot(weight_ref[:, columns], turned_ref[...])) * scale
        hidden = gate_value / (1.0 + jnp.exp(-gate_value)) * lifted
        hidden_ref[:, at] = hidden.T.astype(BF16)
    down.wait()


def down_kernel(start, wide, hidden_ref, weight_ref, keep_ref, send_ref):
    half = lax.axis_index("half")
    count = keep_ref.shape[0]
    part = count // 2
    for n in range(keep_ref.shape[1] // wide):
        at = slice(start + n * wide, start + (n + 1) * wide)
        out = slice(n * wide, (n + 1) * wide)
        total = dot(hidden_ref[...], weight_ref[:, at])
        for p in range(2):
            low = total[p * count : p * count + part]
            high = total[p * count + part : (p + 1) * count]
            to = slice(p * part, (p + 1) * part)
            keep_ref[to, out] = jnp.where(half == 0, low, high)
            send_ref[to, out] = jnp.where(half == 0, high, low).astype(BF16)


def cost(flops, size):
    return pl.CostEstimate(flops=flops, bytes_accessed=size, transcendentals=0)


def expert_first(pieces, gain, gate, up_first, up_part, count):
    units, width = gate.shape
    cut = up_first.shape[0]
    sums = jax.ShapeDtypeStruct((units, 2 * count), F32)
    return pl.pallas_call(
        functools.partial(expert_first_kernel, count),
        in_specs=[VMEM] * 7 + [ANY],
        out_specs=[VMEM] * 4,
        out_shape=[
            sums,
            sums,
            jax.ShapeDtypeStruct((2 * count, 128), F32),
            pltpu.VMEM((units - cut, width), BF16),
        ],
        scratch_shapes=[pltpu.VMEM((width // 2, 2 * count), BF16), pltpu.SemaphoreType.DMA],
        compiler_params=limits(8),
        cost_estimate=cost(4 * units * width * count, 2 * units * width),
        name="experts_first",
    )(*pieces, gain, gate, up_first, *in_hbm(up_part))


def relay_kernel(rows_ref, *refs):
    refs[-1][...] = rows_ref[...]


def relay(rows, *after):
    return pl.pallas_call(
        relay_kernel,
        in_specs=[VMEM] * (1 + len(after)),
        out_specs=VMEM,
        out_shape=jax.ShapeDtypeStruct(rows.shape, rows.dtype),
        compiler_params=limits(2),
        cost_estimate=cost(0, 10**5),
        name="relay",
    )(rows, *after)


def expert_second(pieces, gain, gate, up_first, up_rest, sums, down_part, count):
    units, width = gate.shape
    return pl.pallas_call(
        functools.partial(expert_second_kernel, count),
        in_specs=[VMEM] * 11 + [ANY],
        out_specs=[VMEM] * 2,
        out_shape=[
            jax.ShapeDtypeStruct((2 * count, units), BF16),
            pltpu.VMEM((units, width), BF16),
        ],
        scratch_shapes=[pltpu.VMEM((width // 2, 2 * count), BF16), pltpu.SemaphoreType.DMA],
        compiler_params=limits(8),
        cost_estimate=cost(4 * units * width * count, 2 * units * width),
        name="experts_second",
    )(*pieces, gain, gate, up_first, up_rest, *sums, *in_hbm(down_part))


def expert_down(hidden, weight, start, width, count):
    return pl.pallas_call(
        functools.partial(down_kernel, start, 512),
        in_specs=[VMEM] * 2,
        out_specs=[VMEM] * 2,
        out_shape=[
            jax.ShapeDtypeStruct((count, width), F32),
            jax.ShapeDtypeStruct((count, width), BF16),
        ],
        compiler_params=limits(8),
        cost_estimate=cost(4 * hidden.size * width, 2 * hidden.shape[1] * width),
        name="experts_down",
    )(hidden, weight)


def chip_sum_kernel(count, *refs):
    mine, got = refs[:count], refs[count : 2 * count]
    keep_ref, send_ref = refs[2 * count :]
    rows = keep_ref.shape[0]
    width = mine[0].shape[1]
    for g in range(count):
        at = slice(g * width, (g + 1) * width)
        keep_ref[:, at] = mine[g][:rows] + got[g][:rows].astype(F32)
        send_ref[:, at] = (mine[g][rows:] + got[g][rows:].astype(F32)).astype(BF16)


def chip_sum(mine, got):
    rows, width = mine[0].shape
    shape = (rows // 2, width * len(mine))
    return pl.pallas_call(
        functools.partial(chip_sum_kernel, len(mine)),
        in_specs=[VMEM] * (2 * len(mine)),
        out_specs=[VMEM] * 2,
        out_shape=[jax.ShapeDtypeStruct(shape, F32), jax.ShapeDtypeStruct(shape, BF16)],
        compiler_params=limits(4),
        name="chip_sum",
    )(*mine, *got)


def cut_kernel(own_ref, after_ref, *outs):
    for d, out in enumerate(outs):
        out[...] = own_ref[d]


def cut(own, after):
    return pl.pallas_call(
        cut_kernel,
        in_specs=[VMEM] * 2,
        out_specs=[VMEM] * own.shape[0],
        out_shape=[jax.ShapeDtypeStruct(own.shape[1:], own.dtype)] * own.shape[0],
        compiler_params=limits(2),
        cost_estimate=cost(0, 10**5),
        name="cut",
    )(own, after)


def join_kernel(*refs):
    pieces, out_ref = refs[:-2], refs[-1]
    rows = pieces[0].shape[0]
    for d, piece in enumerate(pieces):
        out_ref[d * rows : (d + 1) * rows] = piece[...]


def join(pieces, after):
    rows, columns = pieces[0].shape
    return pl.pallas_call(
        join_kernel,
        in_specs=[VMEM] * (len(pieces) + 1),
        out_specs=VMEM,
        out_shape=jax.ShapeDtypeStruct((rows * len(pieces), columns), pieces[0].dtype),
        compiler_params=limits(2),
        cost_estimate=cost(0, 10**5),
        name="join",
    )(*pieces, after)


def pair_sum_kernel(capacity, keep_ref, got_ref, *refs):
    outs, fold_ref = refs[:-1], refs[-1]
    experts = len(outs)
    parts = 8 // capacity
    part = outs[0].shape[1]
    total = keep_ref[...] + got_ref[...].astype(F32)
    for e in range(experts):
        mine = total[e * capacity : (e + 1) * capacity]
        fold_ref[e] = jnp.concatenate(
            [mine[:, h * part : (h + 1) * part] for h in range(parts)], axis=0
        )
    expert = lax.axis_index("expert")
    for d, out in enumerate(outs):
        out[...] = fold_ref[expert ^ d].astype(BF16)


def pair_sum(keep, got, capacity, experts):
    part = keep.shape[1] * capacity // 8
    return pl.pallas_call(
        functools.partial(pair_sum_kernel, capacity),
        in_specs=[VMEM] * 2,
        out_specs=[VMEM] * experts,
        out_shape=[jax.ShapeDtypeStruct((8, part), BF16)] * experts,
        scratch_shapes=[pltpu.VMEM((experts, 8, part), F32)],
        compiler_params=limits(4),
        name="pair_sum",
    )(keep, got)


def own_rows_kernel(residual_ref, *refs):
    pieces, cross_ref, combined_ref = refs[:-2], *refs[-2:]
    rows = combined_ref.shape[0]
    columns = pieces[0].shape[1]
    expert, half = lax.axis_index("expert"), lax.axis_index("half")
    for d, piece in enumerate(pieces):
        cross = cross_ref[d * 2 * rows : (d + 1) * 2 * rows]
        for c, both in enumerate((piece[...], cross)):
            base = ((expert ^ d) * 2 + (half ^ c)) * columns
            at = pl.ds(pl.multiple_of(base, columns), columns)
            both = both.astype(F32)
            mine = jnp.where(half == 0, both[:rows], both[rows:])
            combined_ref[:, at] = residual_ref[:, at].astype(F32) + mine


def own_rows(residual, pieces, cross):
    return pl.pallas_call(
        own_rows_kernel,
        in_specs=[VMEM] * (len(pieces) + 2),
        out_specs=VMEM,
        out_shape=jax.ShapeDtypeStruct(residual.shape, F32),
        compiler_params=limits(4),
        cost_estimate=cost(10**6, 10**6),
        name="own_rows",
    )(*in_hbm(residual), *pieces, cross)


def finish_kernel(combined_ref, weighting_ref, *refs):
    got, out_ref = refs[:-1], refs[-1]
    part = got[0].shape[1]
    rows = combined_ref.shape[0]
    terms = jnp.concatenate([piece[...].astype(F32) for piece in got], axis=0).astype(BF16)
    for h in range(combined_ref.shape[1] // part):
        at = slice(h * part, (h + 1) * part)
        mixture = dot(weighting_ref[h * 16 : (h + 1) * 16], terms)
        out_ref[:, at] = (combined_ref[:, at] + mixture[:rows] + mixture[rows:]).astype(BF16)


def finish(combined, weighting, got):
    return pl.pallas_call(
        finish_kernel,
        in_specs=[VMEM] * (2 + len(got)),
        out_specs=VMEM,
        out_shape=jax.ShapeDtypeStruct(combined.shape, BF16),
        compiler_params=limits(4),
        name="finish",
    )(combined, weighting, *got)


def swap(x, axis, by):
    return lax.ppermute(x, axis, [(i, i ^ by) for i in range(lax.axis_size(axis))]) if by else x


def on_chips(
    queries,
    key_rows,
    value_rows,
    states,
    decay_rates,
    head_gain,
    out_weight,
    residual,
    norm_gain,
    expert_ids,
    gate_weights,
    expert_gate,
    expert_up,
    expert_down_part,
):
    experts = lax.axis_size("expert")
    local_rows = residual.shape[0]
    columns = out_weight.shape[1]
    top = expert_ids.shape[1]
    capacity = max(2, local_rows * top // experts)
    count = 2 * experts * capacity
    ids, weights = expert_ids.T, gate_weights.T

    messages = attend(
        queries, key_rows, value_rows, states, decay_rates, head_gain, ids, residual, columns, experts
    )
    messages = list(messages)
    messages[0], weight_here, gain_here, gate_here = load(
        messages[0], [out_weight, norm_gain.reshape(1, -1), expert_gate]
    )
    pieces = []
    for d, message in enumerate(messages):
        message = swap(message, "expert", d)
        pieces += [message, swap(message, "half", 1)]

    keep, send = project(pieces, weight_here)
    first = expert_up.shape[0] // 256 * 128
    choose, residual_part, up_first, weighting = route(
        ids, weights, pieces, keep, columns, capacity, expert_up, first
    )
    *packed, own = pack(keep, swap(send, "pair", 1), residual_part, choose, experts)

    packed[2:] = [relay(rows, packed[1]) for rows in packed[2:]]
    arrived = [swap(rows, "expert", d) for d, rows in enumerate(packed)]
    near = [jnp.concatenate(arrived[d : d + 2], axis=0) for d in range(0, experts, 2)]
    far = [swap(rows, "pair", 1) for rows in near]
    near_cross = [swap(rows, "half", 1) for rows in near]
    *sums, up_rest = expert_first(
        [near[0], near_cross[0], far[0], swap(far[0], "half", 1)],
        gain_here, gate_here, up_first, expert_up, count,
    )
    far[1] = relay(far[1], sums[2])
    hidden, down_here = expert_second(
        [near[1], near_cross[1], far[1], swap(far[1], "half", 1)],
        gain_here, gate_here, up_first, up_rest, sums, expert_down_part, count,
    )

    width = residual.shape[1] // 2
    mine, got = [], []
    for g in range(2):
        terms, send = expert_down(hidden, down_here, g * width, width, count)
        mine.append(terms)
        got.append(swap(send, "half", 1))
    keep, send = chip_sum(mine, got)
    own = [swap(rows, "expert", d) for d, rows in enumerate(cut(own, keep))]
    terms = pair_sum(keep, swap(send, "pair", 1), capacity, experts)
    cross = swap(join(own, terms[0]), "half", 1)
    combined = own_rows(residual, own, cross)
    back = [swap(term, "expert", d) for d, term in enumerate(terms)]
    return finish(combined, weighting, back)


def plain_attend(queries, key_rows, value_rows, states, decay_rates, head_gain):
    requests = states.shape[0]
    head_count = states.shape[1]
    head_size = states.shape[2]
    positions = queries.shape[0] // requests
    layout = (requests, positions, head_count, head_size)
    query_plain = queries.reshape(layout)
    key_plain = key_rows.reshape(layout)
    query_float = query_plain.astype(jnp.float32)
    value_float = value_rows.reshape(layout).astype(jnp.float32)
    offsets = jnp.arange(positions, dtype=jnp.float32)
    carried = jnp.exp(-decay_rates[None, :] * (offsets[:, None] + 1.0))
    from_state = jnp.einsum("rphk,rhkv->rphv", query_float, states, precision=HIGHEST)
    from_state = from_state * carried[None, :, :, None]
    scores = jnp.einsum(
        "rthk,rjhk->rhtj", query_plain, key_plain, preferred_element_type=jnp.float32
    )
    distance = offsets[:, None] - offsets[None, :]
    fading = jnp.exp(-decay_rates[:, None, None] * jnp.maximum(distance, 0.0)[None, :, :])
    fading = jnp.where(distance[None, :, :] >= 0.0, fading, 0.0)
    scores = scores * fading[None]
    within = jnp.einsum("rhtj,rjhv->rthv", scores, value_float, precision=HIGHEST)
    mixed_heads = from_state + within
    spread = jnp.mean(mixed_heads * mixed_heads, axis=3, keepdims=True)
    normal = (
        mixed_heads
        * lax.rsqrt(spread + EPSILON)
        * head_gain.reshape(head_count, head_size)[None, None]
    )
    return normal.astype(jnp.bfloat16).reshape(requests * positions, head_count * head_size)


def plain_experts(picked, gate_part, up_part, down_part):
    leading = picked.shape
    flattened = picked.reshape(-1, leading[-1])
    contract = (((1,), (1,)), ((), ()))
    gate_value = lax.dot_general(flattened, gate_part, contract, preferred_element_type=jnp.float32)
    lifted = lax.dot_general(flattened, up_part, contract, preferred_element_type=jnp.float32)
    hidden = (jax.nn.silu(gate_value) * lifted).astype(jnp.bfloat16)
    output = jnp.dot(hidden, down_part, preferred_element_type=jnp.float32)
    return output.reshape(leading)


def plain(
    queries,
    key_rows,
    value_rows,
    states,
    decay_rates,
    head_gain,
    out_weight,
    residual,
    norm_gain,
    expert_ids,
    gate_weights,
    expert_gate,
    expert_up,
    expert_down,
):
    outer_count = lax.axis_size("dev")
    pair_count = lax.axis_size("pair")
    core_count = lax.axis_size("sub")
    attended = plain_attend(queries, key_rows, value_rows, states, decay_rates, head_gain)
    partial_value = jnp.dot(
        lax.all_gather(attended, ("dev", "sub"), axis=0, tiled=True),
        out_weight,
        preferred_element_type=jnp.float32,
    )
    local_rows = residual.shape[0]
    columns = partial_value.shape[1]
    blocks = partial_value.reshape(outer_count, pair_count, core_count, local_rows, columns)
    ordered = jnp.transpose(blocks, (1, 0, 2, 3, 4)).reshape(
        pair_count, outer_count * core_count * local_rows, columns
    )
    shared = lax.psum_scatter(ordered, "pair", scatter_dimension=0, tiled=True)
    shared = shared.reshape(outer_count * core_count, local_rows, columns)
    regrouped = lax.all_to_all(shared, ("dev", "sub"), split_axis=0, concat_axis=2, tiled=True)
    own_rows = regrouped[0]
    combined = residual.astype(jnp.float32) + own_rows
    spread = jnp.mean(combined * combined, axis=-1, keepdims=True)
    normed = (combined * lax.rsqrt(spread + EPSILON) * norm_gain).astype(jnp.bfloat16)
    width = normed.shape[1]
    top_count = expert_ids.shape[1]
    expert_count = outer_count // 2
    capacity = max(2, local_rows * top_count // expert_count)
    chosen_ids = expert_ids.reshape(-1)
    choose = (chosen_ids[:, None] == jnp.arange(expert_count, dtype=jnp.int32)[None, :]).astype(
        jnp.int32
    )
    before = jnp.cumsum(choose, axis=0) - choose
    position = jnp.sum(before * choose, axis=1)
    target = chosen_ids * capacity + position
    placing = (
        target[None, :] == jnp.arange(expert_count * capacity, dtype=jnp.int32)[:, None]
    ).astype(jnp.bfloat16)
    repeated = jnp.repeat(normed, top_count, axis=0)
    packed = jnp.dot(placing, repeated, preferred_element_type=jnp.float32).astype(jnp.bfloat16)
    slot_rows = packed.reshape(expert_count, 1, capacity, width)
    outgoing = jnp.broadcast_to(slot_rows, (expert_count, 2, capacity, width)).reshape(
        outer_count, capacity, width
    )
    partials = plain_experts(
        lax.all_gather(
            lax.all_to_all(outgoing, "dev", split_axis=0, concat_axis=0, tiled=True)[None],
            ("pair", "sub"),
            axis=0,
            tiled=True,
        ),
        expert_gate,
        expert_up,
        expert_down,
    )
    summed_terms = lax.psum_scatter(partials, ("pair", "sub"), scatter_dimension=0, tiled=True)
    returned = lax.all_to_all(summed_terms[0], "dev", split_axis=0, concat_axis=0, tiled=True)
    halves = jnp.sum(returned.reshape(expert_count, -1, capacity, width), axis=1).reshape(
        expert_count * capacity, width
    )
    weighting = placing.astype(jnp.float32) * gate_weights.reshape(-1)[None, :]
    per_slot = lax.dot_general(
        weighting,
        halves,
        (((0,), (0,)), ((), ())),
        precision=HIGHEST,
        preferred_element_type=jnp.float32,
    )
    mixture = jnp.sum(per_slot.reshape(local_rows, top_count, width), axis=1)
    return (combined + mixture).astype(jnp.bfloat16)


def solution(mesh):
    sizes = dict(mesh.shape)
    plain_axes = (("dev",), ("pair", "sub"), ("sub",))
    chip_axes = (("expert", "half"), ("pair",), ())

    def specs(dev, inner, sub):
        requests = P(("grp",) + dev + sub, "pair")
        tokens = P(("grp",) + dev + inner, None)
        units = P(dev + inner, None)
        arguments = (
            requests,
            requests,
            requests,
            P(("grp",) + dev + sub, "pair", None, None),
            P("pair"),
            P("pair"),
            P("pair", dev + sub),
            tokens,
            P(),
            tokens,
            tokens,
            units,
            units,
            units,
        )
        return dict(in_specs=arguments, out_specs=tokens, check_vma=False)

    experts = sizes["dev"] // 2
    chips = sizes["pair"] == 2 and sizes["sub"] == 1 and experts == 4

    def run(*arguments):
        rows = arguments[7].shape[0] // mesh.size
        columns = arguments[6].shape[1] // (sizes["dev"] * sizes["sub"])
        units = arguments[11].shape[0] * sizes["grp"] // mesh.size
        if chips and rows == 8 and columns % 128 == 0 and units % 384 == 0:
            cut = Mesh(
                mesh.devices.reshape(sizes["grp"], experts, 2, 2),
                ("grp", "expert", "half", "pair"),
            )
            return jax.shard_map(on_chips, mesh=cut, **specs(*chip_axes))(*arguments)
        return jax.shard_map(plain, mesh=mesh, **specs(*plain_axes))(*arguments)

    return run
```

```python
import functools

import jax
import jax.numpy as jnp
from jax import lax
from jax.experimental import pallas as pl
from jax.experimental.pallas import tpu as pltpu
from jax.sharding import Mesh
from jax.sharding import PartitionSpec as P

EPSILON = 1e-06
F32 = jnp.float32
BF16 = jnp.bfloat16
MIB = 1 << 20
ID_LANES = 128
HIGHEST = lax.Precision.HIGHEST
VMEM = pl.BlockSpec(memory_space=pltpu.VMEM)
SMEM = pl.BlockSpec(memory_space=pltpu.SMEM)
ANY = pl.BlockSpec(memory_space=pl.ANY)


def in_hbm(*arrays):
    return [pltpu.with_memory_space_constraint(a, pltpu.HBM) for a in arrays]


def limits(mib):
    return pltpu.CompilerParams(vmem_limit_bytes=mib * MIB)


def dot(a, b):
    return jnp.dot(a, b, preferred_element_type=F32)


def dot_t(a, b):
    return lax.dot_general(a, b, (((1,), (1,)), ((), ())), preferred_element_type=F32)


def halves_of(x):
    high = x.astype(BF16)
    return high, (x - high.astype(F32)).astype(BF16)


def attend_kernel(positions, steps, decay_ref, ids_ref, q_ref, k_ref, v_ref, gain_ref, s_ref, residual_ref, *refs):
    outs = refs
    requests, heads, size, _ = s_ref.shape
    rows = q_ref.shape[0]
    step = pl.program_id(0)
    first = step * heads
    @pl.when(step == 0)
    def _():
        width = steps * heads * size
        lanes = ID_LANES
        row = lax.broadcasted_iota(jnp.int32, (rows, lanes), 0)
        lane = lax.broadcasted_iota(jnp.int32, (rows, lanes), 1)
        ids = jnp.zeros((rows, lanes), jnp.int32)
        for k in range(ids_ref.shape[0]):
            for t in range(ids_ref.shape[1]):
                ids = jnp.where((row == t) & (lane == k), ids_ref[k, t], ids)
        ids = ids.astype(F32).astype(BF16)
        columns = outs[0].shape[1] - width - lanes
        expert = lax.axis_index("expert")
        for d, out in enumerate(outs):
            out[:, width : width + lanes] = ids
            base = (expert ^ d) * 2 * columns
            both = [
                residual_ref[:, pl.ds(pl.multiple_of(base + h * columns, columns), columns)]
                for h in range(2)
            ]
            both = jnp.concatenate([b.astype(F32) for b in both], axis=0)
            out[:, width + lanes :] = both.astype(BF16)

    row = lax.broadcasted_iota(jnp.int32, (rows, rows), 0)
    col = lax.broadcasted_iota(jnp.int32, (rows, rows), 1)
    seen = (row // positions == col // positions) & (row >= col)
    distance = jnp.maximum(row - col, 0).astype(F32)
    owner = lax.broadcasted_iota(jnp.int32, (rows, size), 0)
    age = (owner % positions + 1).astype(F32)
    for i in range(heads):
        rate = decay_ref[first + i]
        at = slice(i * size, (i + 1) * size)
        q = q_ref[:, at]
        spread_q = jnp.concatenate(
            [jnp.where(owner // positions == r, q, jnp.zeros_like(q)) for r in range(requests)],
            axis=1,
        )
        high, low = halves_of(s_ref[:, i].reshape(requests * size, size))
        from_state = (dot(spread_q, high) + dot(spread_q, low)) * jnp.exp(-rate * age)
        scores = jnp.where(seen, dot_t(q, k_ref[:, at]) * jnp.exp(-rate * distance), 0.0)
        score_high, score_low = halves_of(scores)
        v = v_ref[:, at]
        mixed = from_state + dot(score_high, v) + dot(score_low, v)
        spread = jnp.mean(mixed * mixed, axis=1, keepdims=True)
        normal = mixed * lax.rsqrt(spread + EPSILON) * gain_ref[:, at]
        normal = normal.astype(BF16)
        for out in outs:
            out[:, pl.ds(pl.multiple_of((first + i) * size, size), size)] = normal


def attend(
    queries, key_rows, value_rows, states, decay_rates, head_gain, ids, residual, columns, experts
):
    requests, heads, size, _ = states.shape
    rows = queries.shape[0]
    step = 4 if heads % 4 == 0 else 1
    wide = pl.BlockSpec((rows, step * size), lambda i: (0, i))
    message = (rows, queries.shape[1] + ID_LANES + columns)
    return pl.pallas_call(
        functools.partial(attend_kernel, rows // requests, heads // step),
        grid=(heads // step,),
        in_specs=[
            SMEM,
            SMEM,
            wide,
            wide,
            wide,
            pl.BlockSpec((1, step * size), lambda i: (0, i)),
            pl.BlockSpec((requests, step, size, size), lambda i: (0, i, 0, 0)),
            pl.BlockSpec(residual.shape, lambda i: (0, 0)),
        ],
        out_specs=[pl.BlockSpec(message, lambda i: (0, 0))] * experts,
        out_shape=[jax.ShapeDtypeStruct(message, BF16)] * experts,
        compiler_params=limits(8),
        name="attention",
    )(
        *in_hbm(
            decay_rates, ids, queries, key_rows, value_rows, head_gain.reshape(1, -1), states, residual,
        )
    )


def load_kernel(count, rows_hbm, *refs):
    sources, rows_ref, targets, sem = refs[:count], refs[count], refs[count + 1 : -1], refs[-1]
    copies = [
        pltpu.make_async_copy(source, target, sem.at[i])
        for i, (source, target) in enumerate(zip(sources, targets))
    ]
    copies.append(pltpu.make_async_copy(rows_hbm, rows_ref, sem.at[count]))
    for copy in copies:
        copy.start()
    for copy in copies:
        copy.wait()


def load(rows, weights):
    size = sum(w.size * w.dtype.itemsize for w in weights)
    return pl.pallas_call(
        functools.partial(load_kernel, len(weights)),
        in_specs=[ANY] * (1 + len(weights)),
        out_specs=[VMEM] * (1 + len(weights)),
        out_shape=[jax.ShapeDtypeStruct(rows.shape, rows.dtype)]
        + [pltpu.VMEM(w.shape, w.dtype) for w in weights],
        scratch_shapes=[pltpu.SemaphoreType.DMA((1 + len(weights),))],
        compiler_params=limits(1),
        cost_estimate=pl.CostEstimate(flops=0, bytes_accessed=size, transcendentals=0),
        name="load",
    )(rows, *in_hbm(*weights))


def project_kernel(*refs):
    pieces, weight_ref, keep_ref, send_ref, x_ref, product_ref = refs[:-5], *refs[-5:]
    depth = weight_ref.shape[0]
    rows = pieces[0].shape[0]
    expert, half, pair = lax.axis_index("expert"), lax.axis_index("half"), lax.axis_index("pair")
    for j, piece in enumerate(pieces):
        base = (expert ^ (j // 2)) * 2 + (half ^ (j % 2))
        x_ref[pl.ds(pl.multiple_of(base * rows, rows), rows)] = piece[:, :depth]
    product_ref[...] = dot(x_ref[...], weight_ref[...])
    own = rows // 2
    for b in range(len(pieces)):
        mine = pl.ds(pl.multiple_of(b * rows + pair * own, own), own)
        keep_ref[b * own : (b + 1) * own] = product_ref[mine]
    for b in range(0, len(pieces), 2):
        theirs = [
            product_ref[pl.ds(pl.multiple_of(c * rows + (1 - pair) * own, own), own)]
            for c in (b, b + 1)
        ]
        send_ref[b * own : (b + 2) * own] = jnp.concatenate(theirs, axis=0).astype(BF16)


def project(pieces, weight):
    rows = pieces[0].shape[0] * len(pieces)
    depth, columns = weight.shape
    return pl.pallas_call(
        project_kernel,
        in_specs=[VMEM] * (len(pieces) + 1),
        out_specs=[VMEM] * 2,
        out_shape=[
            jax.ShapeDtypeStruct((rows // 2, columns), F32),
            jax.ShapeDtypeStruct((rows // 2, columns), BF16),
        ],
        scratch_shapes=[pltpu.VMEM((rows, depth), BF16), pltpu.VMEM((rows, columns), F32)],
        compiler_params=limits(8),
        name="projection",
    )(*pieces, weight)


def route_kernel(capacity, own_ids_ref, weights_ref, *refs):
    pieces, weight_hbm = refs[:-8], refs[-7]
    choose_ref, residual_ref, weight_ref, weighting_ref, ids_ref, sem = refs[-6:]
    top, own_count = own_ids_ref.shape
    copy = pltpu.make_async_copy(weight_hbm.at[: weight_ref.shape[0]], weight_ref, sem)
    copy.start()
    columns = residual_ref.shape[1]
    own = pieces[0].shape[0] // 2
    rows = ids_ref.shape[0]
    experts = len(pieces) // 2
    expert, half = lax.axis_index("expert"), lax.axis_index("half")
    for j, piece in enumerate(pieces):
        base = (expert ^ (j // 2)) * 2 + (half ^ (j % 2))
        at = pl.ds(pl.multiple_of(base * own, own), own)
        last = piece.shape[1] - columns
        both = piece[:, last:].astype(F32)
        residual_ref[at] = jnp.where(half == 0, both[:own], both[own:])
        ids_ref[at] = piece[:, last - ID_LANES : last].astype(F32)[:own]
    ids = ids_ref[...].T
    line = lax.broadcasted_iota(jnp.int32, (8, rows), 0)
    wanted = jnp.bitwise_xor(line, expert).astype(F32)
    named = jnp.zeros((8, rows), F32)
    for k in range(top):
        named = named + jnp.where(ids[k : k + 1] == wanted, 1.0, 0.0)
    before = lax.broadcasted_iota(jnp.int32, (rows, rows), 0)
    after = lax.broadcasted_iota(jnp.int32, (rows, rows), 1)
    earlier = jnp.where((before // own == after // own) & (before < after), 1.0, 0.0)
    rank = dot(named.astype(BF16), earlier.astype(BF16))
    dev = lax.broadcasted_iota(jnp.int32, (8, rows), 1) // own
    place = (dev % 2 * experts + dev // 2) * capacity
    place = jnp.where(named > 0.5, place.astype(F32) + rank, -1.0)
    count = choose_ref.shape[0] // experts
    slot = lax.broadcasted_iota(jnp.int32, (count, rows), 0).astype(F32)
    for d in range(experts):
        choose_ref[d * count : (d + 1) * count] = jnp.where(
            slot == place[d : d + 1], 1.0, 0.0
        ).astype(BF16)

    places = weighting_ref.shape[1]
    row = lax.broadcasted_iota(jnp.int32, (own_count, places), 0)
    at_place = lax.broadcasted_iota(jnp.int32, (own_count, places), 1)
    slot = at_place // 8 * capacity + at_place % capacity
    weighting = jnp.zeros((own_count, places), F32)
    order = [(t, k) for t in range(own_count) for k in range(top)]
    named = [own_ids_ref[k, t] for t, k in order]
    for j, (t, k) in enumerate(order):
        rank = jnp.int32(0)
        for i in range(j):
            rank = rank + jnp.where(named[i] == named[j], 1, 0)
        to = (named[j] ^ expert) * capacity + rank
        weighting = jnp.where((slot == to) & (row == t), weights_ref[k, t], weighting)
    for h in range(8 // capacity):
        high, low = halves_of(jnp.where(at_place % 8 // capacity == h, weighting, 0.0))
        both = jnp.concatenate([high.astype(F32), low.astype(F32)], axis=0)
        weighting_ref[h * 16 : (h + 1) * 16] = both.astype(BF16)
    copy.wait()


def route(ids, weights, pieces, after, columns, capacity, weight, first):
    rows = pieces[0].shape[0] // 2 * len(pieces)
    experts = len(pieces) // 2
    return pl.pallas_call(
        functools.partial(route_kernel, capacity),
        in_specs=[SMEM] * 2 + [VMEM] * len(pieces) + [ANY] * 2,
        out_specs=[VMEM] * 4,
        out_shape=[
            jax.ShapeDtypeStruct((experts * 2 * experts * capacity, rows), BF16),
            jax.ShapeDtypeStruct((rows, columns), F32),
            pltpu.VMEM((first, weight.shape[1]), weight.dtype),
            jax.ShapeDtypeStruct((16 * (8 // capacity), experts * 8), BF16),
        ],
        scratch_shapes=[pltpu.VMEM((rows, ID_LANES), F32), pltpu.SemaphoreType.DMA],
        compiler_params=limits(4),
        cost_estimate=pl.CostEstimate(flops=10**6, bytes_accessed=8 * 10**6, transcendentals=0),
        name="route",
    )(*in_hbm(ids, weights), *pieces, after, *in_hbm(weight))


def pack_kernel(keep_ref, got_ref, residual_ref, choose_ref, *refs):
    outs, own_ref, cross_ref, sum_ref = refs[:-3], *refs[-3:]
    sum_ref[...] = keep_ref[...] + got_ref[...].astype(F32)
    combined = (sum_ref[...] + residual_ref[...]).astype(BF16)
    packed = dot(choose_ref[...], combined).astype(BF16)
    count = choose_ref.shape[0] // len(outs)
    own = sum_ref.shape[0] // len(outs) // 2
    expert, half = lax.axis_index("expert"), lax.axis_index("half")
    for d, out in enumerate(outs):
        out[...] = packed[d * count : (d + 1) * count]
    for d in range(0, len(outs), 2):
        for ref, which in ((own_ref, half), (cross_ref, 1 - half)):
            rows = [
                sum_ref[pl.ds(pl.multiple_of(((expert ^ c) * 2 + which) * own, own), own)]
                for c in (d, d + 1)
            ]
            ref[d * own : (d + 2) * own] = jnp.concatenate(rows, axis=0).astype(BF16)


def pack(keep, got, residual, choose, experts):
    rows, columns = keep.shape
    count = choose.shape[0] // experts
    return pl.pallas_call(
        pack_kernel,
        in_specs=[VMEM] * 4,
        out_specs=[VMEM] * (experts + 2),
        out_shape=[jax.ShapeDtypeStruct((count, columns), BF16)] * experts
        + [jax.ShapeDtypeStruct((rows // 2, columns), BF16)] * 2,
        scratch_shapes=[pltpu.VMEM((rows, columns), F32)],
        compiler_params=limits(4),
        name="pack",
    )(keep, got, residual, choose)


def turn(turned_ref, gain_ref, pieces, first, count):
    near, near_cross, far, far_cross = pieces
    columns = near.shape[1]
    expert, half = lax.axis_index("expert"), lax.axis_index("half")
    squares = jnp.zeros((2 * count, 128), F32)
    for d in range(2):
        for c, (mine, theirs) in enumerate(((near, far), (near_cross, far_cross))):
            rows = slice(d * count, (d + 1) * count)
            x = jnp.concatenate([mine[rows].astype(F32), theirs[rows].astype(F32)], axis=0)
            for b in range(columns // 128):
                part = x[:, b * 128 : (b + 1) * 128]
                squares = squares + part * part
            block = (expert ^ (first + d)) * 2 + (half ^ c)
            at = pl.ds(pl.multiple_of(block * columns, columns), columns)
            to = pl.ds(pl.multiple_of(block % 4 * columns, columns), columns)
            turned_ref[to] = (x * gain_ref[:, at]).T.astype(BF16)
    return squares


def half_of(ref, first):
    width = ref.shape[1] // 2
    which = (lax.axis_index("expert") ^ first) // 2
    return pl.ds(pl.multiple_of(which * width, width), width)


def expert_first_kernel(count, *refs):
    pieces, gain_ref, gate_ref, up_ref, up_hbm = refs[:4], *refs[4:8]
    gate_sum_ref, up_sum_ref, squares_ref, up_rest_ref, turned_ref, sem = refs[8:]
    cut = up_ref.shape[0]
    rest = pltpu.make_async_copy(up_hbm.at[cut:], up_rest_ref, sem)
    rest.start()
    squares_ref[...] = turn(turned_ref, gain_ref, pieces, 0, count)
    columns = half_of(gate_ref, 0)
    for at in (slice(0, cut), slice(cut, gate_ref.shape[0])):
        gate_sum_ref[at] = dot(gate_ref[at, columns], turned_ref[...])
    up_sum_ref[:cut] = dot(up_ref[:, columns], turned_ref[...])
    rest.wait()
    up_sum_ref[cut:] = dot(up_rest_ref[:, columns], turned_ref[...])


def expert_second_kernel(count, *refs):
    pieces, gain_ref, gate_ref, up_ref, up_rest_ref = refs[:4], *refs[4:8]
    gate_sum_ref, up_sum_ref, squares_ref, down_hbm, hidden_ref, down_ref, turned_ref, sem = refs[8:]
    units, width = gate_ref.shape
    cut = up_ref.shape[0]
    down = pltpu.make_async_copy(down_hbm, down_ref, sem)
    down.start()
    squares = squares_ref[...] + turn(turned_ref, gain_ref, pieces, 2, count)
    spread = jnp.sum(squares.T, axis=0, keepdims=True) / width
    scale = lax.rsqrt(spread + EPSILON)
    columns = half_of(gate_ref, 2)
    for at, weight_ref in ((slice(0, cut), up_ref), (slice(cut, units), up_rest_ref)):
        gate_value = (gate_sum_ref[at] + dot(gate_ref[at, columns], turned_ref[...])) * scale
        lifted = (up_sum_ref[at] + dot(weight_ref[:, columns], turned_ref[...])) * scale
        hidden = gate_value / (1.0 + jnp.exp(-gate_value)) * lifted
        hidden_ref[:, at] = hidden.T.astype(BF16)
    down.wait()


def down_kernel(start, wide, hidden_ref, weight_ref, keep_ref, send_ref):
    half = lax.axis_index("half")
    count = keep_ref.shape[0]
    part = count // 2
    for n in range(keep_ref.shape[1] // wide):
        at = slice(start + n * wide, start + (n + 1) * wide)
        out = slice(n * wide, (n + 1) * wide)
        total = dot(hidden_ref[...], weight_ref[:, at])
        for p in range(2):
            low = total[p * count : p * count + part]
            high = total[p * count + part : (p + 1) * count]
            to = slice(p * part, (p + 1) * part)
            keep_ref[to, out] = jnp.where(half == 0, low, high)
            send_ref[to, out] = jnp.where(half == 0, high, low).astype(BF16)


def cost(flops, size):
    return pl.CostEstimate(flops=flops, bytes_accessed=size, transcendentals=0)


def expert_first(pieces, gain, gate, up_first, up_part, count):
    units, width = gate.shape
    cut = up_first.shape[0]
    sums = jax.ShapeDtypeStruct((units, 2 * count), F32)
    return pl.pallas_call(
        functools.partial(expert_first_kernel, count),
        in_specs=[VMEM] * 7 + [ANY],
        out_specs=[VMEM] * 4,
        out_shape=[
            sums,
            sums,
            jax.ShapeDtypeStruct((2 * count, 128), F32),
            pltpu.VMEM((units - cut, width), BF16),
        ],
        scratch_shapes=[pltpu.VMEM((width // 2, 2 * count), BF16), pltpu.SemaphoreType.DMA],
        compiler_params=limits(8),
        cost_estimate=cost(4 * units * width * count, 2 * units * width),
        name="experts_first",
    )(*pieces, gain, gate, up_first, *in_hbm(up_part))


def relay_kernel(rows_ref, *refs):
    refs[-1][...] = rows_ref[...]


def relay(rows, *after):
    return pl.pallas_call(
        relay_kernel,
        in_specs=[VMEM] * (1 + len(after)),
        out_specs=VMEM,
        out_shape=jax.ShapeDtypeStruct(rows.shape, rows.dtype),
        compiler_params=limits(2),
        cost_estimate=cost(0, 10**5),
        name="relay",
    )(rows, *after)


def expert_second(pieces, gain, gate, up_first, up_rest, sums, down_part, count):
    units, width = gate.shape
    return pl.pallas_call(
        functools.partial(expert_second_kernel, count),
        in_specs=[VMEM] * 11 + [ANY],
        out_specs=[VMEM] * 2,
        out_shape=[
            jax.ShapeDtypeStruct((2 * count, units), BF16),
            pltpu.VMEM((units, width), BF16),
        ],
        scratch_shapes=[pltpu.VMEM((width // 2, 2 * count), BF16), pltpu.SemaphoreType.DMA],
        compiler_params=limits(8),
        cost_estimate=cost(4 * units * width * count, 2 * units * width),
        name="experts_second",
    )(*pieces, gain, gate, up_first, up_rest, *sums, *in_hbm(down_part))


def expert_down(hidden, weight, start, width, count):
    return pl.pallas_call(
        functools.partial(down_kernel, start, 512),
        in_specs=[VMEM] * 2,
        out_specs=[VMEM] * 2,
        out_shape=[
            jax.ShapeDtypeStruct((count, width), F32),
            jax.ShapeDtypeStruct((count, width), BF16),
        ],
        compiler_params=limits(8),
        cost_estimate=cost(4 * hidden.size * width, 2 * hidden.shape[1] * width),
        name="experts_down",
    )(hidden, weight)


def chip_sum_kernel(count, *refs):
    mine, got = refs[:count], refs[count : 2 * count]
    keep_ref, send_ref = refs[2 * count :]
    rows = keep_ref.shape[0]
    width = mine[0].shape[1]
    for g in range(count):
        at = slice(g * width, (g + 1) * width)
        keep_ref[:, at] = mine[g][:rows] + got[g][:rows].astype(F32)
        send_ref[:, at] = (mine[g][rows:] + got[g][rows:].astype(F32)).astype(BF16)


def chip_sum(mine, got):
    rows, width = mine[0].shape
    shape = (rows // 2, width * len(mine))
    return pl.pallas_call(
        functools.partial(chip_sum_kernel, len(mine)),
        in_specs=[VMEM] * (2 * len(mine)),
        out_specs=[VMEM] * 2,
        out_shape=[jax.ShapeDtypeStruct(shape, F32), jax.ShapeDtypeStruct(shape, BF16)],
        compiler_params=limits(4),
        name="chip_sum",
    )(*mine, *got)


def cut_kernel(own_ref, cross_ref, after_ref, *outs):
    rows = own_ref.shape[0] // len(outs)
    own, cross = own_ref[...].astype(F32), cross_ref[...].astype(F32)
    for d, out in enumerate(outs):
        at = slice(d * rows, (d + 1) * rows)
        out[...] = jnp.concatenate([own[at], cross[at]], axis=0).astype(BF16)


def cut(own, cross, after, experts):
    rows, columns = own.shape
    return pl.pallas_call(
        cut_kernel,
        in_specs=[VMEM] * 3,
        out_specs=[VMEM] * experts,
        out_shape=[jax.ShapeDtypeStruct((2 * rows // experts, columns), BF16)] * experts,
        compiler_params=limits(2),
        cost_estimate=cost(0, 10**5),
        name="cut",
    )(own, cross, after)


def pair_sum_kernel(capacity, extra, keep_ref, got_ref, *refs):
    outs, fold_ref = refs[extra:-1], refs[-1]
    experts = len(outs)
    parts = 8 // capacity
    part = outs[0].shape[1]
    total = keep_ref[...] + got_ref[...].astype(F32)
    for e in range(experts):
        mine = total[e * capacity : (e + 1) * capacity]
        fold_ref[e] = jnp.concatenate(
            [mine[:, h * part : (h + 1) * part] for h in range(parts)], axis=0
        )
    expert = lax.axis_index("expert")
    for d, out in enumerate(outs):
        out[...] = fold_ref[expert ^ d].astype(BF16)


def pair_sum(keep, got, capacity, experts, after):
    part = keep.shape[1] * capacity // 8
    return pl.pallas_call(
        functools.partial(pair_sum_kernel, capacity, len(after)),
        in_specs=[VMEM] * (2 + len(after)),
        out_specs=[VMEM] * experts,
        out_shape=[jax.ShapeDtypeStruct((8, part), BF16)] * experts,
        scratch_shapes=[pltpu.VMEM((experts, 8, part), F32)],
        compiler_params=limits(4),
        name="pair_sum",
    )(keep, got, *after)


def own_rows_kernel(residual_ref, *refs):
    pieces, combined_ref = refs[:-1], refs[-1]
    rows = combined_ref.shape[0]
    columns = pieces[0].shape[1]
    expert, half = lax.axis_index("expert"), lax.axis_index("half")
    for d, piece in enumerate(pieces):
        both = piece[...].astype(F32)
        for c in range(2):
            base = ((expert ^ d) * 2 + (half ^ c)) * columns
            at = pl.ds(pl.multiple_of(base, columns), columns)
            combined_ref[:, at] = residual_ref[:, at].astype(F32) + both[c * rows : (c + 1) * rows]


def own_rows(residual, pieces):
    return pl.pallas_call(
        own_rows_kernel,
        in_specs=[VMEM] * (len(pieces) + 1),
        out_specs=VMEM,
        out_shape=jax.ShapeDtypeStruct(residual.shape, F32),
        compiler_params=limits(4),
        cost_estimate=cost(10**6, 10**6),
        name="own_rows",
    )(*in_hbm(residual), *pieces)


def finish_kernel(combined_ref, weighting_ref, *refs):
    got, out_ref = refs[:-1], refs[-1]
    part = got[0].shape[1]
    rows = combined_ref.shape[0]
    terms = jnp.concatenate([piece[...].astype(F32) for piece in got], axis=0).astype(BF16)
    for h in range(combined_ref.shape[1] // part):
        at = slice(h * part, (h + 1) * part)
        mixture = dot(weighting_ref[h * 16 : (h + 1) * 16], terms)
        out_ref[:, at] = (combined_ref[:, at] + mixture[:rows] + mixture[rows:]).astype(BF16)


def finish(combined, weighting, got):
    return pl.pallas_call(
        finish_kernel,
        in_specs=[VMEM] * (2 + len(got)),
        out_specs=VMEM,
        out_shape=jax.ShapeDtypeStruct(combined.shape, BF16),
        compiler_params=limits(4),
        name="finish",
    )(combined, weighting, *got)


def swap(x, axis, by):
    return lax.ppermute(x, axis, [(i, i ^ by) for i in range(lax.axis_size(axis))]) if by else x


def on_chips(
    queries,
    key_rows,
    value_rows,
    states,
    decay_rates,
    head_gain,
    out_weight,
    residual,
    norm_gain,
    expert_ids,
    gate_weights,
    expert_gate,
    expert_up,
    expert_down_part,
):
    experts = lax.axis_size("expert")
    local_rows = residual.shape[0]
    columns = out_weight.shape[1]
    top = expert_ids.shape[1]
    capacity = max(2, local_rows * top // experts)
    count = 2 * experts * capacity
    ids, weights = expert_ids.T, gate_weights.T

    messages = attend(
        queries, key_rows, value_rows, states, decay_rates, head_gain, ids, residual, columns, experts
    )
    messages = list(messages)
    messages[0], weight_here, gain_here, gate_here = load(
        messages[0], [out_weight, norm_gain.reshape(1, -1), expert_gate]
    )
    pieces = []
    for d, message in enumerate(messages):
        message = swap(message, "expert", d)
        pieces += [message, swap(message, "half", 1)]

    keep, send = project(pieces, weight_here)
    first = expert_up.shape[0] // 256 * 128 + 128
    choose, residual_part, up_first, weighting = route(
        ids, weights, pieces, keep, columns, capacity, expert_up, first
    )
    *packed, own, cross = pack(keep, swap(send, "pair", 1), residual_part, choose, experts)

    packed[2:] = [relay(rows, packed[1]) for rows in packed[2:]]
    arrived = [swap(rows, "expert", d) for d, rows in enumerate(packed)]
    near = [jnp.concatenate(arrived[d : d + 2], axis=0) for d in range(0, experts, 2)]
    far = [swap(rows, "pair", 1) for rows in near]
    near_cross = [swap(rows, "half", 1) for rows in near]
    *sums, up_rest = expert_first(
        [near[0], near_cross[0], far[0], swap(far[0], "half", 1)],
        gain_here, gate_here, up_first, expert_up, count,
    )
    cross = swap(cross, "half", 1)
    far[1] = relay(far[1], sums[2], cross)
    hidden, down_here = expert_second(
        [near[1], near_cross[1], far[1], swap(far[1], "half", 1)],
        gain_here, gate_here, up_first, up_rest, sums, expert_down_part, count,
    )

    width = residual.shape[1] // 2
    mine, got = [], []
    for g in range(2):
        terms, send = expert_down(hidden, down_here, g * width, width, count)
        mine.append(terms)
        got.append(swap(send, "half", 1))
    keep, send = chip_sum(mine, got)
    own = cut(own, cross, keep, experts)
    own = [swap(rows, "expert", d) for d, rows in enumerate(own)]
    terms = pair_sum(keep, swap(send, "pair", 1), capacity, experts, own)
    combined = own_rows(residual, own)
    back = [swap(term, "expert", d) for d, term in enumerate(terms)]
    return finish(combined, weighting, back)


def plain_attend(queries, key_rows, value_rows, states, decay_rates, head_gain):
    requests = states.shape[0]
    head_count = states.shape[1]
    head_size = states.shape[2]
    positions = queries.shape[0] // requests
    layout = (requests, positions, head_count, head_size)
    query_plain = queries.reshape(layout)
    key_plain = key_rows.reshape(layout)
    query_float = query_plain.astype(jnp.float32)
    value_float = value_rows.reshape(layout).astype(jnp.float32)
    offsets = jnp.arange(positions, dtype=jnp.float32)
    carried = jnp.exp(-decay_rates[None, :] * (offsets[:, None] + 1.0))
    from_state = jnp.einsum("rphk,rhkv->rphv", query_float, states, precision=HIGHEST)
    from_state = from_state * carried[None, :, :, None]
    scores = jnp.einsum(
        "rthk,rjhk->rhtj", query_plain, key_plain, preferred_element_type=jnp.float32
    )
    distance = offsets[:, None] - offsets[None, :]
    fading = jnp.exp(-decay_rates[:, None, None] * jnp.maximum(distance, 0.0)[None, :, :])
    fading = jnp.where(distance[None, :, :] >= 0.0, fading, 0.0)
    scores = scores * fading[None]
    within = jnp.einsum("rhtj,rjhv->rthv", scores, value_float, precision=HIGHEST)
    mixed_heads = from_state + within
    spread = jnp.mean(mixed_heads * mixed_heads, axis=3, keepdims=True)
    normal = (
        mixed_heads
        * lax.rsqrt(spread + EPSILON)
        * head_gain.reshape(head_count, head_size)[None, None]
    )
    return normal.astype(jnp.bfloat16).reshape(requests * positions, head_count * head_size)


def plain_experts(picked, gate_part, up_part, down_part):
    leading = picked.shape
    flattened = picked.reshape(-1, leading[-1])
    contract = (((1,), (1,)), ((), ()))
    gate_value = lax.dot_general(flattened, gate_part, contract, preferred_element_type=jnp.float32)
    lifted = lax.dot_general(flattened, up_part, contract, preferred_element_type=jnp.float32)
    hidden = (jax.nn.silu(gate_value) * lifted).astype(jnp.bfloat16)
    output = jnp.dot(hidden, down_part, preferred_element_type=jnp.float32)
    return output.reshape(leading)


def plain(
    queries,
    key_rows,
    value_rows,
    states,
    decay_rates,
    head_gain,
    out_weight,
    residual,
    norm_gain,
    expert_ids,
    gate_weights,
    expert_gate,
    expert_up,
    expert_down,
):
    outer_count = lax.axis_size("dev")
    pair_count = lax.axis_size("pair")
    core_count = lax.axis_size("sub")
    attended = plain_attend(queries, key_rows, value_rows, states, decay_rates, head_gain)
    partial_value = jnp.dot(
        lax.all_gather(attended, ("dev", "sub"), axis=0, tiled=True),
        out_weight,
        preferred_element_type=jnp.float32,
    )
    local_rows = residual.shape[0]
    columns = partial_value.shape[1]
    blocks = partial_value.reshape(outer_count, pair_count, core_count, local_rows, columns)
    ordered = jnp.transpose(blocks, (1, 0, 2, 3, 4)).reshape(
        pair_count, outer_count * core_count * local_rows, columns
    )
    shared = lax.psum_scatter(ordered, "pair", scatter_dimension=0, tiled=True)
    shared = shared.reshape(outer_count * core_count, local_rows, columns)
    regrouped = lax.all_to_all(shared, ("dev", "sub"), split_axis=0, concat_axis=2, tiled=True)
    own_rows = regrouped[0]
    combined = residual.astype(jnp.float32) + own_rows
    spread = jnp.mean(combined * combined, axis=-1, keepdims=True)
    normed = (combined * lax.rsqrt(spread + EPSILON) * norm_gain).astype(jnp.bfloat16)
    width = normed.shape[1]
    top_count = expert_ids.shape[1]
    expert_count = outer_count // 2
    capacity = max(2, local_rows * top_count // expert_count)
    chosen_ids = expert_ids.reshape(-1)
    choose = (chosen_ids[:, None] == jnp.arange(expert_count, dtype=jnp.int32)[None, :]).astype(
        jnp.int32
    )
    before = jnp.cumsum(choose, axis=0) - choose
    position = jnp.sum(before * choose, axis=1)
    target = chosen_ids * capacity + position
    placing = (
        target[None, :] == jnp.arange(expert_count * capacity, dtype=jnp.int32)[:, None]
    ).astype(jnp.bfloat16)
    repeated = jnp.repeat(normed, top_count, axis=0)
    packed = jnp.dot(placing, repeated, preferred_element_type=jnp.float32).astype(jnp.bfloat16)
    slot_rows = packed.reshape(expert_count, 1, capacity, width)
    outgoing = jnp.broadcast_to(slot_rows, (expert_count, 2, capacity, width)).reshape(
        outer_count, capacity, width
    )
    partials = plain_experts(
        lax.all_gather(
            lax.all_to_all(outgoing, "dev", split_axis=0, concat_axis=0, tiled=True)[None],
            ("pair", "sub"),
            axis=0,
            tiled=True,
        ),
        expert_gate,
        expert_up,
        expert_down,
    )
    summed_terms = lax.psum_scatter(partials, ("pair", "sub"), scatter_dimension=0, tiled=True)
    returned = lax.all_to_all(summed_terms[0], "dev", split_axis=0, concat_axis=0, tiled=True)
    halves = jnp.sum(returned.reshape(expert_count, -1, capacity, width), axis=1).reshape(
        expert_count * capacity, width
    )
    weighting = placing.astype(jnp.float32) * gate_weights.reshape(-1)[None, :]
    per_slot = lax.dot_general(
        weighting,
        halves,
        (((0,), (0,)), ((), ())),
        precision=HIGHEST,
        preferred_element_type=jnp.float32,
    )
    mixture = jnp.sum(per_slot.reshape(local_rows, top_count, width), axis=1)
    return (combined + mixture).astype(jnp.bfloat16)


def solution(mesh):
    sizes = dict(mesh.shape)
    plain_axes = (("dev",), ("pair", "sub"), ("sub",))
    chip_axes = (("expert", "half"), ("pair",), ())

    def specs(dev, inner, sub):
        requests = P(("grp",) + dev + sub, "pair")
        tokens = P(("grp",) + dev + inner, None)
        units = P(dev + inner, None)
        arguments = (
            requests,
            requests,
            requests,
            P(("grp",) + dev + sub, "pair", None, None),
            P("pair"),
            P("pair"),
            P("pair", dev + sub),
            tokens,
            P(),
            tokens,
            tokens,
            units,
            units,
            units,
        )
        return dict(in_specs=arguments, out_specs=tokens, check_vma=False)

    experts = sizes["dev"] // 2
    chips = sizes["pair"] == 2 and sizes["sub"] == 1 and experts == 4

    def run(*arguments):
        rows = arguments[7].shape[0] // mesh.size
        columns = arguments[6].shape[1] // (sizes["dev"] * sizes["sub"])
        units = arguments[11].shape[0] * sizes["grp"] // mesh.size
        if chips and rows == 8 and columns % 128 == 0 and units % 384 == 0:
            cut = Mesh(
                mesh.devices.reshape(sizes["grp"], experts, 2, 2),
                ("grp", "expert", "half", "pair"),
            )
            return jax.shard_map(on_chips, mesh=cut, **specs(*chip_axes))(*arguments)
        return jax.shard_map(plain, mesh=mesh, **specs(*plain_axes))(*arguments)

    return run
```

```python
import functools

import jax
import jax.numpy as jnp
from jax import lax
from jax.experimental import pallas as pl
from jax.experimental.pallas import tpu as pltpu
from jax.sharding import Mesh
from jax.sharding import PartitionSpec as P

EPSILON = 1e-06
F32 = jnp.float32
BF16 = jnp.bfloat16
MIB = 1 << 20
ID_LANES = 128
HIGHEST = lax.Precision.HIGHEST
VMEM = pl.BlockSpec(memory_space=pltpu.VMEM)
SMEM = pl.BlockSpec(memory_space=pltpu.SMEM)
ANY = pl.BlockSpec(memory_space=pl.ANY)


def in_hbm(*arrays):
    return [pltpu.with_memory_space_constraint(a, pltpu.HBM) for a in arrays]


def limits(mib):
    return pltpu.CompilerParams(vmem_limit_bytes=mib * MIB)


def dot(a, b):
    return jnp.dot(a, b, preferred_element_type=F32)


def dot_t(a, b):
    return lax.dot_general(a, b, (((1,), (1,)), ((), ())), preferred_element_type=F32)


def halves_of(x):
    high = x.astype(BF16)
    return high, (x - high.astype(F32)).astype(BF16)


def attend_kernel(positions, steps, decay_ref, ids_ref, q_ref, k_ref, v_ref, gain_ref, s_ref, residual_ref, *refs):
    outs = refs
    requests, heads, size, _ = s_ref.shape
    rows = q_ref.shape[0]
    step = pl.program_id(0)
    first = step * heads
    @pl.when(step == 0)
    def _():
        width = steps * heads * size
        lanes = ID_LANES
        row = lax.broadcasted_iota(jnp.int32, (rows, lanes), 0)
        lane = lax.broadcasted_iota(jnp.int32, (rows, lanes), 1)
        ids = jnp.zeros((rows, lanes), jnp.int32)
        for k in range(ids_ref.shape[0]):
            for t in range(ids_ref.shape[1]):
                ids = jnp.where((row == t) & (lane == k), ids_ref[k, t], ids)
        ids = ids.astype(F32).astype(BF16)
        columns = outs[0].shape[1] - width - lanes
        expert = lax.axis_index("expert")
        for d, out in enumerate(outs):
            out[:, width : width + lanes] = ids
            base = (expert ^ d) * 2 * columns
            both = [
                residual_ref[:, pl.ds(pl.multiple_of(base + h * columns, columns), columns)]
                for h in range(2)
            ]
            both = jnp.concatenate([b.astype(F32) for b in both], axis=0)
            out[:, width + lanes :] = both.astype(BF16)

    row = lax.broadcasted_iota(jnp.int32, (rows, rows), 0)
    col = lax.broadcasted_iota(jnp.int32, (rows, rows), 1)
    seen = (row // positions == col // positions) & (row >= col)
    distance = jnp.maximum(row - col, 0).astype(F32)
    owner = lax.broadcasted_iota(jnp.int32, (rows, size), 0)
    age = (owner % positions + 1).astype(F32)
    of_request = [
        jnp.where(owner // positions == r, 1.0, 0.0).astype(BF16) for r in range(requests)
    ]
    for i in range(heads):
        rate = decay_ref[first + i]
        at = slice(i * size, (i + 1) * size)
        q = q_ref[:, at]
        spread_q = jnp.concatenate([q * mask for mask in of_request], axis=1)
        high, low = halves_of(s_ref[:, i].reshape(requests * size, size))
        from_state = (dot(spread_q, high) + dot(spread_q, low)) * jnp.exp(-rate * age)
        scores = jnp.where(seen, dot_t(q, k_ref[:, at]) * jnp.exp(-rate * distance), 0.0)
        score_high, score_low = halves_of(scores)
        v = v_ref[:, at]
        mixed = from_state + dot(score_high, v) + dot(score_low, v)
        spread = jnp.mean(mixed * mixed, axis=1, keepdims=True)
        normal = mixed * lax.rsqrt(spread + EPSILON) * gain_ref[:, at]
        normal = normal.astype(BF16)
        for out in outs:
            out[:, pl.ds(pl.multiple_of((first + i) * size, size), size)] = normal


def attend(
    queries, key_rows, value_rows, states, decay_rates, head_gain, ids, residual, columns, experts
):
    requests, heads, size, _ = states.shape
    rows = queries.shape[0]
    step = 8 if heads % 8 == 0 else 1
    wide = pl.BlockSpec((rows, step * size), lambda i: (0, i))
    message = (rows, queries.shape[1] + ID_LANES + columns)
    return pl.pallas_call(
        functools.partial(attend_kernel, rows // requests, heads // step),
        grid=(heads // step,),
        in_specs=[
            SMEM,
            SMEM,
            wide,
            wide,
            wide,
            pl.BlockSpec((1, step * size), lambda i: (0, i)),
            pl.BlockSpec((requests, step, size, size), lambda i: (0, i, 0, 0)),
            pl.BlockSpec(residual.shape, lambda i: (0, 0)),
        ],
        out_specs=[pl.BlockSpec(message, lambda i: (0, 0))] * experts,
        out_shape=[jax.ShapeDtypeStruct(message, BF16)] * experts,
        compiler_params=limits(16),
        name="attention",
    )(
        *in_hbm(
            decay_rates, ids, queries, key_rows, value_rows, head_gain.reshape(1, -1), states, residual,
        )
    )


def load_kernel(count, rows_hbm, *refs):
    sources, rows_ref, targets, sem = refs[:count], refs[count], refs[count + 1 : -1], refs[-1]
    copies = [
        pltpu.make_async_copy(source, target, sem.at[i])
        for i, (source, target) in enumerate(zip(sources, targets))
    ]
    copies.append(pltpu.make_async_copy(rows_hbm, rows_ref, sem.at[count]))
    for copy in copies:
        copy.start()
    for copy in copies:
        copy.wait()


def load(rows, weights):
    size = sum(w.size * w.dtype.itemsize for w in weights)
    return pl.pallas_call(
        functools.partial(load_kernel, len(weights)),
        in_specs=[ANY] * (1 + len(weights)),
        out_specs=[VMEM] * (1 + len(weights)),
        out_shape=[jax.ShapeDtypeStruct(rows.shape, rows.dtype)]
        + [pltpu.VMEM(w.shape, w.dtype) for w in weights],
        scratch_shapes=[pltpu.SemaphoreType.DMA((1 + len(weights),))],
        compiler_params=limits(1),
        cost_estimate=pl.CostEstimate(flops=0, bytes_accessed=size, transcendentals=0),
        name="load",
    )(rows, *in_hbm(*weights))


def project_kernel(*refs):
    pieces, weight_ref, keep_ref, send_ref, x_ref, product_ref = refs[:-5], *refs[-5:]
    depth = weight_ref.shape[0]
    rows = pieces[0].shape[0]
    expert, half, pair = lax.axis_index("expert"), lax.axis_index("half"), lax.axis_index("pair")
    for j, piece in enumerate(pieces):
        base = (expert ^ (j // 2)) * 2 + (half ^ (j % 2))
        x_ref[pl.ds(pl.multiple_of(base * rows, rows), rows)] = piece[:, :depth]
    product_ref[...] = dot(x_ref[...], weight_ref[...])
    own = rows // 2
    for b in range(len(pieces)):
        mine = pl.ds(pl.multiple_of(b * rows + pair * own, own), own)
        keep_ref[b * own : (b + 1) * own] = product_ref[mine]
    for b in range(0, len(pieces), 2):
        theirs = [
            product_ref[pl.ds(pl.multiple_of(c * rows + (1 - pair) * own, own), own)]
            for c in (b, b + 1)
        ]
        send_ref[b * own : (b + 2) * own] = jnp.concatenate(theirs, axis=0).astype(BF16)


def project(pieces, weight):
    rows = pieces[0].shape[0] * len(pieces)
    depth, columns = weight.shape
    return pl.pallas_call(
        project_kernel,
        in_specs=[VMEM] * (len(pieces) + 1),
        out_specs=[VMEM] * 2,
        out_shape=[
            jax.ShapeDtypeStruct((rows // 2, columns), F32),
            jax.ShapeDtypeStruct((rows // 2, columns), BF16),
        ],
        scratch_shapes=[pltpu.VMEM((rows, depth), BF16), pltpu.VMEM((rows, columns), F32)],
        compiler_params=limits(8),
        name="projection",
    )(*pieces, weight)


def route_kernel(capacity, top, *refs):
    pieces, weight_hbm = refs[:-7], refs[-6]
    choose_ref, residual_ref, weight_ref, ids_ref, sem = refs[-5:]
    copy = pltpu.make_async_copy(weight_hbm.at[: weight_ref.shape[0]], weight_ref, sem)
    copy.start()
    columns = residual_ref.shape[1]
    own = pieces[0].shape[0] // 2
    rows = ids_ref.shape[0]
    experts = len(pieces) // 2
    expert, half = lax.axis_index("expert"), lax.axis_index("half")
    for j, piece in enumerate(pieces):
        base = (expert ^ (j // 2)) * 2 + (half ^ (j % 2))
        at = pl.ds(pl.multiple_of(base * own, own), own)
        last = piece.shape[1] - columns
        both = piece[:, last:].astype(F32)
        residual_ref[at] = jnp.where(half == 0, both[:own], both[own:])
        ids_ref[at] = piece[:, last - ID_LANES : last].astype(F32)[:own]
    ids = ids_ref[...].T
    line = lax.broadcasted_iota(jnp.int32, (8, rows), 0)
    wanted = jnp.bitwise_xor(line, expert).astype(F32)
    named = jnp.zeros((8, rows), F32)
    for k in range(top):
        named = named + jnp.where(ids[k : k + 1] == wanted, 1.0, 0.0)
    before = lax.broadcasted_iota(jnp.int32, (rows, rows), 0)
    after = lax.broadcasted_iota(jnp.int32, (rows, rows), 1)
    earlier = jnp.where((before // own == after // own) & (before < after), 1.0, 0.0)
    rank = dot(named.astype(BF16), earlier.astype(BF16))
    dev = lax.broadcasted_iota(jnp.int32, (8, rows), 1) // own
    place = (dev % 2 * experts + dev // 2) * capacity
    place = jnp.where(named > 0.5, place.astype(F32) + rank, -1.0)
    count = choose_ref.shape[0] // experts
    slot = lax.broadcasted_iota(jnp.int32, (count, rows), 0).astype(F32)
    for d in range(experts):
        choose_ref[d * count : (d + 1) * count] = jnp.where(
            slot == place[d : d + 1], 1.0, 0.0
        ).astype(BF16)
    copy.wait()


def route(pieces, after, columns, capacity, top, weight, first):
    rows = pieces[0].shape[0] // 2 * len(pieces)
    experts = len(pieces) // 2
    return pl.pallas_call(
        functools.partial(route_kernel, capacity, top),
        in_specs=[VMEM] * len(pieces) + [ANY] * 2,
        out_specs=[VMEM] * 3,
        out_shape=[
            jax.ShapeDtypeStruct((experts * 2 * experts * capacity, rows), BF16),
            jax.ShapeDtypeStruct((rows, columns), F32),
            pltpu.VMEM((first, weight.shape[1]), weight.dtype),
        ],
        scratch_shapes=[pltpu.VMEM((rows, ID_LANES), F32), pltpu.SemaphoreType.DMA],
        compiler_params=limits(4),
        cost_estimate=pl.CostEstimate(flops=10**6, bytes_accessed=8 * 10**6, transcendentals=0),
        name="route",
    )(*pieces, after, *in_hbm(weight))


def pack_kernel(keep_ref, got_ref, residual_ref, choose_ref, *refs):
    outs, own_ref, cross_ref, sum_ref = refs[:-3], *refs[-3:]
    sum_ref[...] = keep_ref[...] + got_ref[...].astype(F32)
    combined = (sum_ref[...] + residual_ref[...]).astype(BF16)
    packed = dot(choose_ref[...], combined).astype(BF16)
    count = choose_ref.shape[0] // len(outs)
    own = sum_ref.shape[0] // len(outs) // 2
    expert, half = lax.axis_index("expert"), lax.axis_index("half")
    for d, out in enumerate(outs):
        out[...] = packed[d * count : (d + 1) * count]
    for d in range(0, len(outs), 2):
        for ref, which in ((own_ref, half), (cross_ref, 1 - half)):
            rows = [
                sum_ref[pl.ds(pl.multiple_of(((expert ^ c) * 2 + which) * own, own), own)]
                for c in (d, d + 1)
            ]
            ref[d * own : (d + 2) * own] = jnp.concatenate(rows, axis=0).astype(BF16)


def pack(keep, got, residual, choose, experts):
    rows, columns = keep.shape
    count = choose.shape[0] // experts
    return pl.pallas_call(
        pack_kernel,
        in_specs=[VMEM] * 4,
        out_specs=[VMEM] * (experts + 2),
        out_shape=[jax.ShapeDtypeStruct((count, columns), BF16)] * experts
        + [jax.ShapeDtypeStruct((rows // 2, columns), BF16)] * 2,
        scratch_shapes=[pltpu.VMEM((rows, columns), F32)],
        compiler_params=limits(4),
        name="pack",
    )(keep, got, residual, choose)


def turn(turned_ref, gain_ref, pieces, first, count):
    near, near_cross, far, far_cross = pieces
    columns = near.shape[1]
    expert, half = lax.axis_index("expert"), lax.axis_index("half")
    squares = jnp.zeros((2 * count, 128), F32)
    for d in range(2):
        for c, (mine, theirs) in enumerate(((near, far), (near_cross, far_cross))):
            rows = slice(d * count, (d + 1) * count)
            x = jnp.concatenate([mine[rows].astype(F32), theirs[rows].astype(F32)], axis=0)
            for b in range(columns // 128):
                part = x[:, b * 128 : (b + 1) * 128]
                squares = squares + part * part
            block = (expert ^ (first + d)) * 2 + (half ^ c)
            at = pl.ds(pl.multiple_of(block * columns, columns), columns)
            to = pl.ds(pl.multiple_of(block % 4 * columns, columns), columns)
            turned_ref[to] = (x * gain_ref[:, at]).T.astype(BF16)
    return squares


def half_of(ref, first):
    width = ref.shape[1] // 2
    which = (lax.axis_index("expert") ^ first) // 2
    return pl.ds(pl.multiple_of(which * width, width), width)


def expert_first_kernel(count, *refs):
    pieces, gain_ref, gate_ref, up_ref, up_hbm = refs[:4], *refs[4:8]
    gate_sum_ref, up_sum_ref, squares_ref, up_rest_ref, turned_ref, sem = refs[8:]
    cut = up_ref.shape[0]
    rest = pltpu.make_async_copy(up_hbm.at[cut:], up_rest_ref, sem)
    rest.start()
    squares_ref[...] = turn(turned_ref, gain_ref, pieces, 0, count)
    columns = half_of(gate_ref, 0)
    for at in (slice(0, cut), slice(cut, gate_ref.shape[0])):
        gate_sum_ref[at] = dot(gate_ref[at, columns], turned_ref[...])
    up_sum_ref[:cut] = dot(up_ref[:, columns], turned_ref[...])
    rest.wait()
    up_sum_ref[cut:] = dot(up_rest_ref[:, columns], turned_ref[...])


def expert_second_kernel(count, *refs):
    pieces, gain_ref, gate_ref, up_ref, up_rest_ref = refs[:4], *refs[4:8]
    gate_sum_ref, up_sum_ref, squares_ref, down_hbm, hidden_ref, down_ref, turned_ref, sem = refs[8:]
    units, width = gate_ref.shape
    cut = up_ref.shape[0]
    down = pltpu.make_async_copy(down_hbm, down_ref, sem)
    down.start()
    squares = squares_ref[...] + turn(turned_ref, gain_ref, pieces, 2, count)
    spread = jnp.sum(squares.T, axis=0, keepdims=True) / width
    scale = lax.rsqrt(spread + EPSILON)
    columns = half_of(gate_ref, 2)
    for at, weight_ref in ((slice(0, cut), up_ref), (slice(cut, units), up_rest_ref)):
        gate_value = (gate_sum_ref[at] + dot(gate_ref[at, columns], turned_ref[...])) * scale
        lifted = (up_sum_ref[at] + dot(weight_ref[:, columns], turned_ref[...])) * scale
        hidden = gate_value / (1.0 + jnp.exp(-gate_value)) * lifted
        hidden_ref[:, at] = hidden.T.astype(BF16)
    down.wait()


def down_kernel(start, wide, hidden_ref, weight_ref, keep_ref, send_ref):
    half = lax.axis_index("half")
    count = keep_ref.shape[0]
    part = count // 2
    for n in range(keep_ref.shape[1] // wide):
        at = slice(start + n * wide, start + (n + 1) * wide)
        out = slice(n * wide, (n + 1) * wide)
        total = dot(hidden_ref[...], weight_ref[:, at])
        for p in range(2):
            low = total[p * count : p * count + part]
            high = total[p * count + part : (p + 1) * count]
            to = slice(p * part, (p + 1) * part)
            keep_ref[to, out] = jnp.where(half == 0, low, high)
            send_ref[to, out] = jnp.where(half == 0, high, low).astype(BF16)


def cost(flops, size):
    return pl.CostEstimate(flops=flops, bytes_accessed=size, transcendentals=0)


def expert_first(pieces, gain, gate, up_first, up_part, count):
    units, width = gate.shape
    cut = up_first.shape[0]
    sums = jax.ShapeDtypeStruct((units, 2 * count), F32)
    return pl.pallas_call(
        functools.partial(expert_first_kernel, count),
        in_specs=[VMEM] * 7 + [ANY],
        out_specs=[VMEM] * 4,
        out_shape=[
            sums,
            sums,
            jax.ShapeDtypeStruct((2 * count, 128), F32),
            pltpu.VMEM((units - cut, width), BF16),
        ],
        scratch_shapes=[pltpu.VMEM((width // 2, 2 * count), BF16), pltpu.SemaphoreType.DMA],
        compiler_params=limits(8),
        cost_estimate=cost(4 * units * width * count, 2 * units * width),
        name="experts_first",
    )(*pieces, gain, gate, up_first, *in_hbm(up_part))


def relay_kernel(rows_ref, *refs):
    refs[-1][...] = rows_ref[...]


def relay(rows, *after):
    return pl.pallas_call(
        relay_kernel,
        in_specs=[VMEM] * (1 + len(after)),
        out_specs=VMEM,
        out_shape=jax.ShapeDtypeStruct(rows.shape, rows.dtype),
        compiler_params=limits(2),
        cost_estimate=cost(0, 10**5),
        name="relay",
    )(rows, *after)


def expert_second(pieces, gain, gate, up_first, up_rest, sums, down_part, count):
    units, width = gate.shape
    return pl.pallas_call(
        functools.partial(expert_second_kernel, count),
        in_specs=[VMEM] * 11 + [ANY],
        out_specs=[VMEM] * 2,
        out_shape=[
            jax.ShapeDtypeStruct((2 * count, units), BF16),
            pltpu.VMEM((units, width), BF16),
        ],
        scratch_shapes=[pltpu.VMEM((width // 2, 2 * count), BF16), pltpu.SemaphoreType.DMA],
        compiler_params=limits(8),
        cost_estimate=cost(4 * units * width * count, 2 * units * width),
        name="experts_second",
    )(*pieces, gain, gate, up_first, up_rest, *sums, *in_hbm(down_part))


def expert_down(hidden, weight, start, width, count):
    return pl.pallas_call(
        functools.partial(down_kernel, start, 512),
        in_specs=[VMEM] * 2,
        out_specs=[VMEM] * 2,
        out_shape=[
            jax.ShapeDtypeStruct((count, width), F32),
            jax.ShapeDtypeStruct((count, width), BF16),
        ],
        compiler_params=limits(8),
        cost_estimate=cost(4 * hidden.size * width, 2 * hidden.shape[1] * width),
        name="experts_down",
    )(hidden, weight)


def chip_sum_kernel(count, *refs):
    mine, got = refs[:count], refs[count : 2 * count]
    keep_ref, send_ref = refs[2 * count :]
    rows = keep_ref.shape[0]
    width = mine[0].shape[1]
    for g in range(count):
        at = slice(g * width, (g + 1) * width)
        keep_ref[:, at] = mine[g][:rows] + got[g][:rows].astype(F32)
        send_ref[:, at] = (mine[g][rows:] + got[g][rows:].astype(F32)).astype(BF16)


def chip_sum(mine, got):
    rows, width = mine[0].shape
    shape = (rows // 2, width * len(mine))
    return pl.pallas_call(
        functools.partial(chip_sum_kernel, len(mine)),
        in_specs=[VMEM] * (2 * len(mine)),
        out_specs=[VMEM] * 2,
        out_shape=[jax.ShapeDtypeStruct(shape, F32), jax.ShapeDtypeStruct(shape, BF16)],
        compiler_params=limits(4),
        name="chip_sum",
    )(*mine, *got)


def cut_kernel(own_ref, cross_ref, after_ref, *outs):
    rows = own_ref.shape[0] // len(outs)
    own, cross = own_ref[...].astype(F32), cross_ref[...].astype(F32)
    for d, out in enumerate(outs):
        at = slice(d * rows, (d + 1) * rows)
        out[...] = jnp.concatenate([own[at], cross[at]], axis=0).astype(BF16)


def cut(own, cross, after, experts):
    rows, columns = own.shape
    return pl.pallas_call(
        cut_kernel,
        in_specs=[VMEM] * 3,
        out_specs=[VMEM] * experts,
        out_shape=[jax.ShapeDtypeStruct((2 * rows // experts, columns), BF16)] * experts,
        compiler_params=limits(2),
        cost_estimate=cost(0, 10**5),
        name="cut",
    )(own, cross, after)


def pair_sum_kernel(capacity, extra, keep_ref, got_ref, *refs):
    outs, fold_ref = refs[extra:-1], refs[-1]
    experts = len(outs)
    parts = 8 // capacity
    part = outs[0].shape[1]
    total = keep_ref[...] + got_ref[...].astype(F32)
    for e in range(experts):
        mine = total[e * capacity : (e + 1) * capacity]
        fold_ref[e] = jnp.concatenate(
            [mine[:, h * part : (h + 1) * part] for h in range(parts)], axis=0
        )
    expert = lax.axis_index("expert")
    for d, out in enumerate(outs):
        out[...] = fold_ref[expert ^ d].astype(BF16)


def pair_sum(keep, got, capacity, experts, after):
    part = keep.shape[1] * capacity // 8
    return pl.pallas_call(
        functools.partial(pair_sum_kernel, capacity, len(after)),
        in_specs=[VMEM] * (2 + len(after)),
        out_specs=[VMEM] * experts,
        out_shape=[jax.ShapeDtypeStruct((8, part), BF16)] * experts,
        scratch_shapes=[pltpu.VMEM((experts, 8, part), F32)],
        compiler_params=limits(4),
        name="pair_sum",
    )(keep, got, *after)


def own_rows_kernel(capacity, own_ids_ref, weights_ref, residual_ref, *refs):
    pieces, combined_ref, weighting_ref = refs[:-2], *refs[-2:]
    rows = combined_ref.shape[0]
    top, own_count = own_ids_ref.shape
    columns = pieces[0].shape[1]
    expert, half = lax.axis_index("expert"), lax.axis_index("half")
    for d, piece in enumerate(pieces):
        both = piece[...].astype(F32)
        for c in range(2):
            base = ((expert ^ d) * 2 + (half ^ c)) * columns
            at = pl.ds(pl.multiple_of(base, columns), columns)
            combined_ref[:, at] = residual_ref[:, at].astype(F32) + both[c * rows : (c + 1) * rows]

    places = weighting_ref.shape[1]
    row = lax.broadcasted_iota(jnp.int32, (own_count, places), 0)
    at_place = lax.broadcasted_iota(jnp.int32, (own_count, places), 1)
    slot = at_place // 8 * capacity + at_place % capacity
    weighting = jnp.zeros((own_count, places), F32)
    order = [(t, k) for t in range(own_count) for k in range(top)]
    named = [own_ids_ref[k, t] for t, k in order]
    for j, (t, k) in enumerate(order):
        rank = jnp.int32(0)
        for i in range(j):
            rank = rank + jnp.where(named[i] == named[j], 1, 0)
        to = (named[j] ^ expert) * capacity + rank
        weighting = jnp.where((slot == to) & (row == t), weights_ref[k, t], weighting)
    for h in range(8 // capacity):
        high, low = halves_of(jnp.where(at_place % 8 // capacity == h, weighting, 0.0))
        both = jnp.concatenate([high.astype(F32), low.astype(F32)], axis=0)
        weighting_ref[h * 16 : (h + 1) * 16] = both.astype(BF16)


def own_rows(ids, weights, residual, pieces, capacity):
    experts = len(pieces)
    return pl.pallas_call(
        functools.partial(own_rows_kernel, capacity),
        in_specs=[SMEM] * 2 + [VMEM] * (len(pieces) + 1),
        out_specs=[VMEM] * 2,
        out_shape=[
            jax.ShapeDtypeStruct(residual.shape, F32),
            jax.ShapeDtypeStruct((16 * (8 // capacity), experts * 8), BF16),
        ],
        compiler_params=limits(4),
        cost_estimate=cost(10**6, 10**6),
        name="own_rows",
    )(*in_hbm(ids, weights, residual), *pieces)


def finish_kernel(combined_ref, weighting_ref, *refs):
    got, out_ref = refs[:-1], refs[-1]
    part = got[0].shape[1]
    rows = combined_ref.shape[0]
    terms = jnp.concatenate([piece[...].astype(F32) for piece in got], axis=0).astype(BF16)
    for h in range(combined_ref.shape[1] // part):
        at = slice(h * part, (h + 1) * part)
        mixture = dot(weighting_ref[h * 16 : (h + 1) * 16], terms)
        out_ref[:, at] = (combined_ref[:, at] + mixture[:rows] + mixture[rows:]).astype(BF16)


def finish(combined, weighting, got):
    return pl.pallas_call(
        finish_kernel,
        in_specs=[VMEM] * (2 + len(got)),
        out_specs=VMEM,
        out_shape=jax.ShapeDtypeStruct(combined.shape, BF16),
        compiler_params=limits(4),
        name="finish",
    )(combined, weighting, *got)


def swap(x, axis, by):
    return lax.ppermute(x, axis, [(i, i ^ by) for i in range(lax.axis_size(axis))]) if by else x


def on_chips(
    queries,
    key_rows,
    value_rows,
    states,
    decay_rates,
    head_gain,
    out_weight,
    residual,
    norm_gain,
    expert_ids,
    gate_weights,
    expert_gate,
    expert_up,
    expert_down_part,
):
    experts = lax.axis_size("expert")
    local_rows = residual.shape[0]
    columns = out_weight.shape[1]
    top = expert_ids.shape[1]
    capacity = max(2, local_rows * top // experts)
    count = 2 * experts * capacity
    ids, weights = expert_ids.T, gate_weights.T

    messages = attend(
        queries, key_rows, value_rows, states, decay_rates, head_gain, ids, residual, columns, experts
    )
    messages = list(messages)
    messages[0], weight_here, gain_here, gate_here = load(
        messages[0], [out_weight, norm_gain.reshape(1, -1), expert_gate]
    )
    pieces = []
    for d, message in enumerate(messages):
        message = swap(message, "expert", d)
        pieces += [message, swap(message, "half", 1)]

    keep, send = project(pieces, weight_here)
    first = expert_up.shape[0] // 256 * 128 + 128
    choose, residual_part, up_first = route(
        pieces, keep, columns, capacity, expert_ids.shape[1], expert_up, first
    )
    *packed, own, cross = pack(keep, swap(send, "pair", 1), residual_part, choose, experts)

    packed[2:] = [relay(rows, packed[1]) for rows in packed[2:]]
    arrived = [swap(rows, "expert", d) for d, rows in enumerate(packed)]
    near = [jnp.concatenate(arrived[d : d + 2], axis=0) for d in range(0, experts, 2)]
    far = [swap(rows, "pair", 1) for rows in near]
    near_cross = [swap(rows, "half", 1) for rows in near]
    *sums, up_rest = expert_first(
        [near[0], near_cross[0], far[0], swap(far[0], "half", 1)],
        gain_here, gate_here, up_first, expert_up, count,
    )
    cross = swap(cross, "half", 1)
    far[1] = relay(far[1], sums[2], cross)
    hidden, down_here = expert_second(
        [near[1], near_cross[1], far[1], swap(far[1], "half", 1)],
        gain_here, gate_here, up_first, up_rest, sums, expert_down_part, count,
    )

    width = residual.shape[1] // 2
    mine, got = [], []
    for g in range(2):
        terms, send = expert_down(hidden, down_here, g * width, width, count)
        mine.append(terms)
        got.append(swap(send, "half", 1))
    keep, send = chip_sum(mine, got)
    own = cut(own, cross, keep, experts)
    own = [swap(rows, "expert", d) for d, rows in enumerate(own)]
    terms = pair_sum(keep, swap(send, "pair", 1), capacity, experts, own)
    combined, weighting = own_rows(ids, weights, residual, own, capacity)
    back = [swap(term, "expert", d) for d, term in enumerate(terms)]
    return finish(combined, weighting, back)


def plain_attend(queries, key_rows, value_rows, states, decay_rates, head_gain):
    requests = states.shape[0]
    head_count = states.shape[1]
    head_size = states.shape[2]
    positions = queries.shape[0] // requests
    layout = (requests, positions, head_count, head_size)
    query_plain = queries.reshape(layout)
    key_plain = key_rows.reshape(layout)
    query_float = query_plain.astype(jnp.float32)
    value_float = value_rows.reshape(layout).astype(jnp.float32)
    offsets = jnp.arange(positions, dtype=jnp.float32)
    carried = jnp.exp(-decay_rates[None, :] * (offsets[:, None] + 1.0))
    from_state = jnp.einsum("rphk,rhkv->rphv", query_float, states, precision=HIGHEST)
    from_state = from_state * carried[None, :, :, None]
    scores = jnp.einsum(
        "rthk,rjhk->rhtj", query_plain, key_plain, preferred_element_type=jnp.float32
    )
    distance = offsets[:, None] - offsets[None, :]
    fading = jnp.exp(-decay_rates[:, None, None] * jnp.maximum(distance, 0.0)[None, :, :])
    fading = jnp.where(distance[None, :, :] >= 0.0, fading, 0.0)
    scores = scores * fading[None]
    within = jnp.einsum("rhtj,rjhv->rthv", scores, value_float, precision=HIGHEST)
    mixed_heads = from_state + within
    spread = jnp.mean(mixed_heads * mixed_heads, axis=3, keepdims=True)
    normal = (
        mixed_heads
        * lax.rsqrt(spread + EPSILON)
        * head_gain.reshape(head_count, head_size)[None, None]
    )
    return normal.astype(jnp.bfloat16).reshape(requests * positions, head_count * head_size)


def plain_experts(picked, gate_part, up_part, down_part):
    leading = picked.shape
    flattened = picked.reshape(-1, leading[-1])
    contract = (((1,), (1,)), ((), ()))
    gate_value = lax.dot_general(flattened, gate_part, contract, preferred_element_type=jnp.float32)
    lifted = lax.dot_general(flattened, up_part, contract, preferred_element_type=jnp.float32)
    hidden = (jax.nn.silu(gate_value) * lifted).astype(jnp.bfloat16)
    output = jnp.dot(hidden, down_part, preferred_element_type=jnp.float32)
    return output.reshape(leading)


def plain(
    queries,
    key_rows,
    value_rows,
    states,
    decay_rates,
    head_gain,
    out_weight,
    residual,
    norm_gain,
    expert_ids,
    gate_weights,
    expert_gate,
    expert_up,
    expert_down,
):
    outer_count = lax.axis_size("dev")
    pair_count = lax.axis_size("pair")
    core_count = lax.axis_size("sub")
    attended = plain_attend(queries, key_rows, value_rows, states, decay_rates, head_gain)
    partial_value = jnp.dot(
        lax.all_gather(attended, ("dev", "sub"), axis=0, tiled=True),
        out_weight,
        preferred_element_type=jnp.float32,
    )
    local_rows = residual.shape[0]
    columns = partial_value.shape[1]
    blocks = partial_value.reshape(outer_count, pair_count, core_count, local_rows, columns)
    ordered = jnp.transpose(blocks, (1, 0, 2, 3, 4)).reshape(
        pair_count, outer_count * core_count * local_rows, columns
    )
    shared = lax.psum_scatter(ordered, "pair", scatter_dimension=0, tiled=True)
    shared = shared.reshape(outer_count * core_count, local_rows, columns)
    regrouped = lax.all_to_all(shared, ("dev", "sub"), split_axis=0, concat_axis=2, tiled=True)
    own_rows = regrouped[0]
    combined = residual.astype(jnp.float32) + own_rows
    spread = jnp.mean(combined * combined, axis=-1, keepdims=True)
    normed = (combined * lax.rsqrt(spread + EPSILON) * norm_gain).astype(jnp.bfloat16)
    width = normed.shape[1]
    top_count = expert_ids.shape[1]
    expert_count = outer_count // 2
    capacity = max(2, local_rows * top_count // expert_count)
    chosen_ids = expert_ids.reshape(-1)
    choose = (chosen_ids[:, None] == jnp.arange(expert_count, dtype=jnp.int32)[None, :]).astype(
        jnp.int32
    )
    before = jnp.cumsum(choose, axis=0) - choose
    position = jnp.sum(before * choose, axis=1)
    target = chosen_ids * capacity + position
    placing = (
        target[None, :] == jnp.arange(expert_count * capacity, dtype=jnp.int32)[:, None]
    ).astype(jnp.bfloat16)
    repeated = jnp.repeat(normed, top_count, axis=0)
    packed = jnp.dot(placing, repeated, preferred_element_type=jnp.float32).astype(jnp.bfloat16)
    slot_rows = packed.reshape(expert_count, 1, capacity, width)
    outgoing = jnp.broadcast_to(slot_rows, (expert_count, 2, capacity, width)).reshape(
        outer_count, capacity, width
    )
    partials = plain_experts(
        lax.all_gather(
            lax.all_to_all(outgoing, "dev", split_axis=0, concat_axis=0, tiled=True)[None],
            ("pair", "sub"),
            axis=0,
            tiled=True,
        ),
        expert_gate,
        expert_up,
        expert_down,
    )
    summed_terms = lax.psum_scatter(partials, ("pair", "sub"), scatter_dimension=0, tiled=True)
    returned = lax.all_to_all(summed_terms[0], "dev", split_axis=0, concat_axis=0, tiled=True)
    halves = jnp.sum(returned.reshape(expert_count, -1, capacity, width), axis=1).reshape(
        expert_count * capacity, width
    )
    weighting = placing.astype(jnp.float32) * gate_weights.reshape(-1)[None, :]
    per_slot = lax.dot_general(
        weighting,
        halves,
        (((0,), (0,)), ((), ())),
        precision=HIGHEST,
        preferred_element_type=jnp.float32,
    )
    mixture = jnp.sum(per_slot.reshape(local_rows, top_count, width), axis=1)
    return (combined + mixture).astype(jnp.bfloat16)


def solution(mesh):
    sizes = dict(mesh.shape)
    plain_axes = (("dev",), ("pair", "sub"), ("sub",))
    chip_axes = (("expert", "half"), ("pair",), ())

    def specs(dev, inner, sub):
        requests = P(("grp",) + dev + sub, "pair")
        tokens = P(("grp",) + dev + inner, None)
        units = P(dev + inner, None)
        arguments = (
            requests,
            requests,
            requests,
            P(("grp",) + dev + sub, "pair", None, None),
            P("pair"),
            P("pair"),
            P("pair", dev + sub),
            tokens,
            P(),
            tokens,
            tokens,
            units,
            units,
            units,
        )
        return dict(in_specs=arguments, out_specs=tokens, check_vma=False)

    experts = sizes["dev"] // 2
    chips = sizes["pair"] == 2 and sizes["sub"] == 1 and experts == 4

    def run(*arguments):
        rows = arguments[7].shape[0] // mesh.size
        columns = arguments[6].shape[1] // (sizes["dev"] * sizes["sub"])
        units = arguments[11].shape[0] * sizes["grp"] // mesh.size
        if chips and rows == 8 and columns % 128 == 0 and units % 384 == 0:
            cut = Mesh(
                mesh.devices.reshape(sizes["grp"], experts, 2, 2),
                ("grp", "expert", "half", "pair"),
            )
            return jax.shard_map(on_chips, mesh=cut, **specs(*chip_axes))(*arguments)
        return jax.shard_map(plain, mesh=mesh, **specs(*plain_axes))(*arguments)

    return run
```

```python
import functools

import jax
import jax.numpy as jnp
from jax import lax
from jax.experimental import pallas as pl
from jax.experimental.pallas import tpu as pltpu
from jax.sharding import Mesh
from jax.sharding import PartitionSpec as P

EPSILON = 1e-06
F32 = jnp.float32
BF16 = jnp.bfloat16
MIB = 1 << 20
ID_LANES = 128
HIGHEST = lax.Precision.HIGHEST
VMEM = pl.BlockSpec(memory_space=pltpu.VMEM)
SMEM = pl.BlockSpec(memory_space=pltpu.SMEM)
ANY = pl.BlockSpec(memory_space=pl.ANY)


def in_hbm(*arrays):
    return [pltpu.with_memory_space_constraint(a, pltpu.HBM) for a in arrays]


def limits(mib):
    return pltpu.CompilerParams(vmem_limit_bytes=mib * MIB)


def far_first(count):
    return [-d % count for d in range(count)]


def dot(a, b):
    return jnp.dot(a, b, preferred_element_type=F32)


def dot_t(a, b):
    return lax.dot_general(a, b, (((1,), (1,)), ((), ())), preferred_element_type=F32)


def halves_of(x):
    high = x.astype(BF16)
    return high, (x - high.astype(F32)).astype(BF16)


def attend_kernel(positions, steps, decay_ref, ids_ref, q_ref, k_ref, v_ref, gain_ref, s_ref, residual_ref, *refs):
    outs = refs
    requests, heads, size, _ = s_ref.shape
    rows = q_ref.shape[0]
    step = pl.program_id(0)
    first = step * heads
    @pl.when(step == 0)
    def _():
        width = steps * heads * size
        lanes = ID_LANES
        row = lax.broadcasted_iota(jnp.int32, (rows, lanes), 0)
        lane = lax.broadcasted_iota(jnp.int32, (rows, lanes), 1)
        ids = jnp.zeros((rows, lanes), jnp.int32)
        for k in range(ids_ref.shape[0]):
            for t in range(ids_ref.shape[1]):
                ids = jnp.where((row == t) & (lane == k), ids_ref[k, t], ids)
        ids = ids.astype(F32).astype(BF16)
        columns = outs[0].shape[1] - width - lanes
        expert = lax.axis_index("expert")
        for d, out in enumerate(outs):
            out[:, width : width + lanes] = ids
            base = (expert ^ d) * 2 * columns
            both = [
                residual_ref[:, pl.ds(pl.multiple_of(base + h * columns, columns), columns)]
                for h in range(2)
            ]
            both = jnp.concatenate([b.astype(F32) for b in both], axis=0)
            out[:, width + lanes :] = both.astype(BF16)

    row = lax.broadcasted_iota(jnp.int32, (rows, rows), 0)
    col = lax.broadcasted_iota(jnp.int32, (rows, rows), 1)
    seen = (row // positions == col // positions) & (row >= col)
    distance = jnp.maximum(row - col, 0).astype(F32)
    owner = lax.broadcasted_iota(jnp.int32, (rows, size), 0)
    age = (owner % positions + 1).astype(F32)
    of_request = [
        jnp.where(owner // positions == r, 1.0, 0.0).astype(BF16) for r in range(requests)
    ]
    for i in range(heads):
        rate = decay_ref[first + i]
        at = slice(i * size, (i + 1) * size)
        q = q_ref[:, at]
        spread_q = jnp.concatenate([q * mask for mask in of_request], axis=1)
        high, low = halves_of(s_ref[:, i].reshape(requests * size, size))
        from_state = (dot(spread_q, high) + dot(spread_q, low)) * jnp.exp(-rate * age)
        scores = jnp.where(seen, dot_t(q, k_ref[:, at]) * jnp.exp(-rate * distance), 0.0)
        score_high, score_low = halves_of(scores)
        v = v_ref[:, at]
        mixed = from_state + dot(score_high, v) + dot(score_low, v)
        spread = jnp.mean(mixed * mixed, axis=1, keepdims=True)
        normal = mixed * lax.rsqrt(spread + EPSILON) * gain_ref[:, at]
        normal = normal.astype(BF16)
        for out in outs:
            out[:, pl.ds(pl.multiple_of((first + i) * size, size), size)] = normal


def attend(
    queries, key_rows, value_rows, states, decay_rates, head_gain, ids, residual, columns, experts
):
    requests, heads, size, _ = states.shape
    rows = queries.shape[0]
    step = 8 if heads % 8 == 0 else 1
    wide = pl.BlockSpec((rows, step * size), lambda i: (0, i))
    message = (rows, queries.shape[1] + ID_LANES + columns)
    return pl.pallas_call(
        functools.partial(attend_kernel, rows // requests, heads // step),
        grid=(heads // step,),
        in_specs=[
            SMEM,
            SMEM,
            wide,
            wide,
            wide,
            pl.BlockSpec((1, step * size), lambda i: (0, i)),
            pl.BlockSpec((requests, step, size, size), lambda i: (0, i, 0, 0)),
            pl.BlockSpec(residual.shape, lambda i: (0, 0)),
        ],
        out_specs=[pl.BlockSpec(message, lambda i: (0, 0))] * experts,
        out_shape=[jax.ShapeDtypeStruct(message, BF16)] * experts,
        compiler_params=limits(16),
        name="attention",
    )(
        *in_hbm(
            decay_rates, ids, queries, key_rows, value_rows, head_gain.reshape(1, -1), states, residual,
        )
    )


def load_kernel(count, rows_hbm, *refs):
    sources, rows_ref, targets, sem = refs[:count], refs[count], refs[count + 1 : -1], refs[-1]
    copies = [
        pltpu.make_async_copy(source, target, sem.at[i])
        for i, (source, target) in enumerate(zip(sources, targets))
    ]
    copies.append(pltpu.make_async_copy(rows_hbm, rows_ref, sem.at[count]))
    for copy in copies:
        copy.start()
    for copy in copies:
        copy.wait()


def load(rows, weights):
    size = sum(w.size * w.dtype.itemsize for w in weights)
    return pl.pallas_call(
        functools.partial(load_kernel, len(weights)),
        in_specs=[ANY] * (1 + len(weights)),
        out_specs=[VMEM] * (1 + len(weights)),
        out_shape=[jax.ShapeDtypeStruct(rows.shape, rows.dtype)]
        + [pltpu.VMEM(w.shape, w.dtype) for w in weights],
        scratch_shapes=[pltpu.SemaphoreType.DMA((1 + len(weights),))],
        compiler_params=limits(1),
        cost_estimate=pl.CostEstimate(flops=0, bytes_accessed=size, transcendentals=0),
        name="load",
    )(rows, *in_hbm(*weights))


def project_kernel(*refs):
    pieces, weight_ref, keep_ref, send_ref, x_ref, product_ref = refs[:-5], *refs[-5:]
    depth = weight_ref.shape[0]
    rows = pieces[0].shape[0]
    expert, half, pair = lax.axis_index("expert"), lax.axis_index("half"), lax.axis_index("pair")
    for j, piece in enumerate(pieces):
        base = (expert ^ far_first(len(pieces) // 2)[j // 2]) * 2 + (half ^ (j % 2))
        x_ref[pl.ds(pl.multiple_of(base * rows, rows), rows)] = piece[:, :depth]
    product_ref[...] = dot(x_ref[...], weight_ref[...])
    own = rows // 2
    for b in range(len(pieces)):
        mine = pl.ds(pl.multiple_of(b * rows + pair * own, own), own)
        keep_ref[b * own : (b + 1) * own] = product_ref[mine]
    for b in range(0, len(pieces), 2):
        theirs = [
            product_ref[pl.ds(pl.multiple_of(c * rows + (1 - pair) * own, own), own)]
            for c in (b, b + 1)
        ]
        send_ref[b * own : (b + 2) * own] = jnp.concatenate(theirs, axis=0).astype(BF16)


def project(pieces, weight):
    rows = pieces[0].shape[0] * len(pieces)
    depth, columns = weight.shape
    return pl.pallas_call(
        project_kernel,
        in_specs=[VMEM] * (len(pieces) + 1),
        out_specs=[VMEM] * 2,
        out_shape=[
            jax.ShapeDtypeStruct((rows // 2, columns), F32),
            jax.ShapeDtypeStruct((rows // 2, columns), BF16),
        ],
        scratch_shapes=[pltpu.VMEM((rows, depth), BF16), pltpu.VMEM((rows, columns), F32)],
        compiler_params=limits(8),
        name="projection",
    )(*pieces, weight)


def route_kernel(capacity, top, *refs):
    pieces, weight_hbm = refs[:-7], refs[-6]
    choose_ref, residual_ref, weight_ref, ids_ref, sem = refs[-5:]
    copy = pltpu.make_async_copy(weight_hbm.at[: weight_ref.shape[0]], weight_ref, sem)
    copy.start()
    columns = residual_ref.shape[1]
    own = pieces[0].shape[0] // 2
    rows = ids_ref.shape[0]
    experts = len(pieces) // 2
    expert, half = lax.axis_index("expert"), lax.axis_index("half")
    for j, piece in enumerate(pieces):
        base = (expert ^ far_first(len(pieces) // 2)[j // 2]) * 2 + (half ^ (j % 2))
        at = pl.ds(pl.multiple_of(base * own, own), own)
        last = piece.shape[1] - columns
        both = piece[:, last:].astype(F32)
        residual_ref[at] = jnp.where(half == 0, both[:own], both[own:])
        ids_ref[at] = piece[:, last - ID_LANES : last].astype(F32)[:own]
    ids = ids_ref[...].T
    line = lax.broadcasted_iota(jnp.int32, (8, rows), 0)
    wanted = jnp.bitwise_xor(line, expert).astype(F32)
    named = jnp.zeros((8, rows), F32)
    for k in range(top):
        named = named + jnp.where(ids[k : k + 1] == wanted, 1.0, 0.0)
    before = lax.broadcasted_iota(jnp.int32, (rows, rows), 0)
    after = lax.broadcasted_iota(jnp.int32, (rows, rows), 1)
    earlier = jnp.where((before // own == after // own) & (before < after), 1.0, 0.0)
    rank = dot(named.astype(BF16), earlier.astype(BF16))
    dev = lax.broadcasted_iota(jnp.int32, (8, rows), 1) // own
    place = (dev % 2 * experts + dev // 2) * capacity
    place = jnp.where(named > 0.5, place.astype(F32) + rank, -1.0)
    count = choose_ref.shape[0] // experts
    slot = lax.broadcasted_iota(jnp.int32, (count, rows), 0).astype(F32)
    for d in range(experts):
        choose_ref[d * count : (d + 1) * count] = jnp.where(
            slot == place[d : d + 1], 1.0, 0.0
        ).astype(BF16)
    copy.wait()


def route(pieces, after, columns, capacity, top, weight, first):
    rows = pieces[0].shape[0] // 2 * len(pieces)
    experts = len(pieces) // 2
    return pl.pallas_call(
        functools.partial(route_kernel, capacity, top),
        in_specs=[VMEM] * len(pieces) + [ANY] * 2,
        out_specs=[VMEM] * 3,
        out_shape=[
            jax.ShapeDtypeStruct((experts * 2 * experts * capacity, rows), BF16),
            jax.ShapeDtypeStruct((rows, columns), F32),
            pltpu.VMEM((first, weight.shape[1]), weight.dtype),
        ],
        scratch_shapes=[pltpu.VMEM((rows, ID_LANES), F32), pltpu.SemaphoreType.DMA],
        compiler_params=limits(4),
        cost_estimate=pl.CostEstimate(flops=10**6, bytes_accessed=8 * 10**6, transcendentals=0),
        name="route",
    )(*pieces, after, *in_hbm(weight))


def pack_kernel(keep_ref, got_ref, residual_ref, choose_ref, *refs):
    outs, own_ref, cross_ref, sum_ref = refs[:-3], *refs[-3:]
    sum_ref[...] = keep_ref[...] + got_ref[...].astype(F32)
    combined = (sum_ref[...] + residual_ref[...]).astype(BF16)
    packed = dot(choose_ref[...], combined).astype(BF16)
    count = choose_ref.shape[0] // len(outs)
    own = sum_ref.shape[0] // len(outs) // 2
    expert, half = lax.axis_index("expert"), lax.axis_index("half")
    for d, out in enumerate(outs):
        out[...] = packed[d * count : (d + 1) * count]
    for d in range(0, len(outs), 2):
        for ref, which in ((own_ref, half), (cross_ref, 1 - half)):
            rows = [
                sum_ref[pl.ds(pl.multiple_of(((expert ^ c) * 2 + which) * own, own), own)]
                for c in (d, d + 1)
            ]
            ref[d * own : (d + 2) * own] = jnp.concatenate(rows, axis=0).astype(BF16)


def pack(keep, got, residual, choose, experts):
    rows, columns = keep.shape
    count = choose.shape[0] // experts
    return pl.pallas_call(
        pack_kernel,
        in_specs=[VMEM] * 4,
        out_specs=[VMEM] * (experts + 2),
        out_shape=[jax.ShapeDtypeStruct((count, columns), BF16)] * experts
        + [jax.ShapeDtypeStruct((rows // 2, columns), BF16)] * 2,
        scratch_shapes=[pltpu.VMEM((rows, columns), F32)],
        compiler_params=limits(4),
        name="pack",
    )(keep, got, residual, choose)


def turn(turned_ref, gain_ref, pieces, first, count):
    near, near_cross, far, far_cross = pieces
    columns = near.shape[1]
    expert, half = lax.axis_index("expert"), lax.axis_index("half")
    squares = jnp.zeros((2 * count, 128), F32)
    for d in range(2):
        for c, (mine, theirs) in enumerate(((near, far), (near_cross, far_cross))):
            rows = slice(d * count, (d + 1) * count)
            x = jnp.concatenate([mine[rows].astype(F32), theirs[rows].astype(F32)], axis=0)
            for b in range(columns // 128):
                part = x[:, b * 128 : (b + 1) * 128]
                squares = squares + part * part
            block = (expert ^ (first + d)) * 2 + (half ^ c)
            at = pl.ds(pl.multiple_of(block * columns, columns), columns)
            to = pl.ds(pl.multiple_of(block % 4 * columns, columns), columns)
            turned_ref[to] = (x * gain_ref[:, at]).T.astype(BF16)
    return squares


def half_of(ref, first):
    width = ref.shape[1] // 2
    which = (lax.axis_index("expert") ^ first) // 2
    return pl.ds(pl.multiple_of(which * width, width), width)


def expert_first_kernel(count, *refs):
    pieces, gain_ref, gate_ref, up_ref, up_hbm = refs[:4], *refs[4:8]
    gate_sum_ref, up_sum_ref, squares_ref, up_rest_ref, turned_ref, sem = refs[8:]
    cut = up_ref.shape[0]
    rest = pltpu.make_async_copy(up_hbm.at[cut:], up_rest_ref, sem)
    rest.start()
    squares_ref[...] = turn(turned_ref, gain_ref, pieces, 0, count)
    columns = half_of(gate_ref, 0)
    for at in (slice(0, cut), slice(cut, gate_ref.shape[0])):
        gate_sum_ref[at] = dot(gate_ref[at, columns], turned_ref[...])
    up_sum_ref[:cut] = dot(up_ref[:, columns], turned_ref[...])
    rest.wait()
    up_sum_ref[cut:] = dot(up_rest_ref[:, columns], turned_ref[...])


def expert_second_kernel(count, *refs):
    pieces, gain_ref, gate_ref, up_ref, up_rest_ref = refs[:4], *refs[4:8]
    gate_sum_ref, up_sum_ref, squares_ref, down_hbm, hidden_ref, down_ref, turned_ref, sem = refs[8:]
    units, width = gate_ref.shape
    cut = up_ref.shape[0]
    down = pltpu.make_async_copy(down_hbm, down_ref, sem)
    down.start()
    squares = squares_ref[...] + turn(turned_ref, gain_ref, pieces, 2, count)
    spread = jnp.sum(squares.T, axis=0, keepdims=True) / width
    scale = lax.rsqrt(spread + EPSILON)
    columns = half_of(gate_ref, 2)
    for at, weight_ref in ((slice(0, cut), up_ref), (slice(cut, units), up_rest_ref)):
        gate_value = (gate_sum_ref[at] + dot(gate_ref[at, columns], turned_ref[...])) * scale
        lifted = (up_sum_ref[at] + dot(weight_ref[:, columns], turned_ref[...])) * scale
        hidden = gate_value / (1.0 + jnp.exp(-gate_value)) * lifted
        hidden_ref[:, at] = hidden.T.astype(BF16)
    down.wait()


def down_kernel(start, wide, hidden_ref, weight_ref, keep_ref, send_ref):
    half = lax.axis_index("half")
    count = keep_ref.shape[0]
    part = count // 2
    for n in range(keep_ref.shape[1] // wide):
        at = slice(start + n * wide, start + (n + 1) * wide)
        out = slice(n * wide, (n + 1) * wide)
        total = dot(hidden_ref[...], weight_ref[:, at])
        for p in range(2):
            low = total[p * count : p * count + part]
            high = total[p * count + part : (p + 1) * count]
            to = slice(p * part, (p + 1) * part)
            keep_ref[to, out] = jnp.where(half == 0, low, high)
            send_ref[to, out] = jnp.where(half == 0, high, low).astype(BF16)


def cost(flops, size):
    return pl.CostEstimate(flops=flops, bytes_accessed=size, transcendentals=0)


def expert_first(pieces, gain, gate, up_first, up_part, count):
    units, width = gate.shape
    cut = up_first.shape[0]
    sums = jax.ShapeDtypeStruct((units, 2 * count), F32)
    return pl.pallas_call(
        functools.partial(expert_first_kernel, count),
        in_specs=[VMEM] * 7 + [ANY],
        out_specs=[VMEM] * 4,
        out_shape=[
            sums,
            sums,
            jax.ShapeDtypeStruct((2 * count, 128), F32),
            pltpu.VMEM((units - cut, width), BF16),
        ],
        scratch_shapes=[pltpu.VMEM((width // 2, 2 * count), BF16), pltpu.SemaphoreType.DMA],
        compiler_params=limits(8),
        cost_estimate=cost(4 * units * width * count, 2 * units * width),
        name="experts_first",
    )(*pieces, gain, gate, up_first, *in_hbm(up_part))


def relay_kernel(rows_ref, *refs):
    refs[-1][...] = rows_ref[...]


def relay(rows, *after):
    return pl.pallas_call(
        relay_kernel,
        in_specs=[VMEM] * (1 + len(after)),
        out_specs=VMEM,
        out_shape=jax.ShapeDtypeStruct(rows.shape, rows.dtype),
        compiler_params=limits(2),
        cost_estimate=cost(0, 10**5),
        name="relay",
    )(rows, *after)


def expert_second(pieces, gain, gate, up_first, up_rest, sums, down_part, count):
    units, width = gate.shape
    return pl.pallas_call(
        functools.partial(expert_second_kernel, count),
        in_specs=[VMEM] * 11 + [ANY],
        out_specs=[VMEM] * 2,
        out_shape=[
            jax.ShapeDtypeStruct((2 * count, units), BF16),
            pltpu.VMEM((units, width), BF16),
        ],
        scratch_shapes=[pltpu.VMEM((width // 2, 2 * count), BF16), pltpu.SemaphoreType.DMA],
        compiler_params=limits(8),
        cost_estimate=cost(4 * units * width * count, 2 * units * width),
        name="experts_second",
    )(*pieces, gain, gate, up_first, up_rest, *sums, *in_hbm(down_part))


def expert_down(hidden, weight, start, width, count):
    return pl.pallas_call(
        functools.partial(down_kernel, start, 512),
        in_specs=[VMEM] * 2,
        out_specs=[VMEM] * 2,
        out_shape=[
            jax.ShapeDtypeStruct((count, width), F32),
            jax.ShapeDtypeStruct((count, width), BF16),
        ],
        compiler_params=limits(8),
        cost_estimate=cost(4 * hidden.size * width, 2 * hidden.shape[1] * width),
        name="experts_down",
    )(hidden, weight)


def chip_sum_kernel(count, *refs):
    mine, got = refs[:count], refs[count : 2 * count]
    keep_ref, send_ref = refs[2 * count :]
    rows = keep_ref.shape[0]
    width = mine[0].shape[1]
    for g in range(count):
        at = slice(g * width, (g + 1) * width)
        keep_ref[:, at] = mine[g][:rows] + got[g][:rows].astype(F32)
        send_ref[:, at] = (mine[g][rows:] + got[g][rows:].astype(F32)).astype(BF16)


def chip_sum(mine, got):
    rows, width = mine[0].shape
    shape = (rows // 2, width * len(mine))
    return pl.pallas_call(
        functools.partial(chip_sum_kernel, len(mine)),
        in_specs=[VMEM] * (2 * len(mine)),
        out_specs=[VMEM] * 2,
        out_shape=[jax.ShapeDtypeStruct(shape, F32), jax.ShapeDtypeStruct(shape, BF16)],
        compiler_params=limits(4),
        name="chip_sum",
    )(*mine, *got)


def cut_kernel(own_ref, cross_ref, after_ref, *outs):
    rows = own_ref.shape[0] // len(outs)
    own, cross = own_ref[...].astype(F32), cross_ref[...].astype(F32)
    for d, out in enumerate(outs):
        at = slice(d * rows, (d + 1) * rows)
        out[...] = jnp.concatenate([own[at], cross[at]], axis=0).astype(BF16)


def cut(own, cross, after, experts):
    rows, columns = own.shape
    return pl.pallas_call(
        cut_kernel,
        in_specs=[VMEM] * 3,
        out_specs=[VMEM] * experts,
        out_shape=[jax.ShapeDtypeStruct((2 * rows // experts, columns), BF16)] * experts,
        compiler_params=limits(2),
        cost_estimate=cost(0, 10**5),
        name="cut",
    )(own, cross, after)


def pair_sum_kernel(capacity, extra, keep_ref, got_ref, *refs):
    outs, fold_ref = refs[extra:-1], refs[-1]
    experts = len(outs)
    parts = 8 // capacity
    part = outs[0].shape[1]
    total = keep_ref[...] + got_ref[...].astype(F32)
    for e in range(experts):
        mine = total[e * capacity : (e + 1) * capacity]
        fold_ref[e] = jnp.concatenate(
            [mine[:, h * part : (h + 1) * part] for h in range(parts)], axis=0
        )
    expert = lax.axis_index("expert")
    for d, out in enumerate(outs):
        out[...] = fold_ref[expert ^ d].astype(BF16)


def pair_sum(keep, got, capacity, experts, after):
    part = keep.shape[1] * capacity // 8
    return pl.pallas_call(
        functools.partial(pair_sum_kernel, capacity, len(after)),
        in_specs=[VMEM] * (2 + len(after)),
        out_specs=[VMEM] * experts,
        out_shape=[jax.ShapeDtypeStruct((8, part), BF16)] * experts,
        scratch_shapes=[pltpu.VMEM((experts, 8, part), F32)],
        compiler_params=limits(4),
        name="pair_sum",
    )(keep, got, *after)


def own_rows_kernel(capacity, own_ids_ref, weights_ref, residual_ref, *refs):
    pieces, combined_ref, weighting_ref = refs[:-2], *refs[-2:]
    rows = combined_ref.shape[0]
    top, own_count = own_ids_ref.shape
    columns = pieces[0].shape[1]
    expert, half = lax.axis_index("expert"), lax.axis_index("half")
    for d, piece in zip(far_first(len(pieces)), pieces):
        both = piece[...].astype(F32)
        for c in range(2):
            base = ((expert ^ d) * 2 + (half ^ c)) * columns
            at = pl.ds(pl.multiple_of(base, columns), columns)
            combined_ref[:, at] = residual_ref[:, at].astype(F32) + both[c * rows : (c + 1) * rows]

    places = weighting_ref.shape[1]
    row = lax.broadcasted_iota(jnp.int32, (own_count, places), 0)
    at_place = lax.broadcasted_iota(jnp.int32, (own_count, places), 1)
    slot = at_place // 8 * capacity + at_place % capacity
    weighting = jnp.zeros((own_count, places), F32)
    order = [(t, k) for t in range(own_count) for k in range(top)]
    named = [own_ids_ref[k, t] for t, k in order]
    for j, (t, k) in enumerate(order):
        rank = jnp.int32(0)
        for i in range(j):
            rank = rank + jnp.where(named[i] == named[j], 1, 0)
        to = (named[j] ^ expert) * capacity + rank
        weighting = jnp.where((slot == to) & (row == t), weights_ref[k, t], weighting)
    for h in range(8 // capacity):
        high, low = halves_of(jnp.where(at_place % 8 // capacity == h, weighting, 0.0))
        both = jnp.concatenate([high.astype(F32), low.astype(F32)], axis=0)
        weighting_ref[h * 16 : (h + 1) * 16] = both.astype(BF16)


def own_rows(ids, weights, residual, pieces, capacity):
    experts = len(pieces)
    return pl.pallas_call(
        functools.partial(own_rows_kernel, capacity),
        in_specs=[SMEM] * 2 + [VMEM] * (len(pieces) + 1),
        out_specs=[VMEM] * 2,
        out_shape=[
            jax.ShapeDtypeStruct(residual.shape, F32),
            jax.ShapeDtypeStruct((16 * (8 // capacity), experts * 8), BF16),
        ],
        compiler_params=limits(4),
        cost_estimate=cost(10**6, 10**6),
        name="own_rows",
    )(*in_hbm(ids, weights, residual), *pieces)


def finish_kernel(combined_ref, weighting_ref, *refs):
    got, out_ref = refs[:-1], refs[-1]
    part = got[0].shape[1]
    rows = combined_ref.shape[0]
    terms = [got[d][...].astype(F32) for d in far_first(len(got))]
    terms = jnp.concatenate(terms, axis=0).astype(BF16)
    for h in range(combined_ref.shape[1] // part):
        at = slice(h * part, (h + 1) * part)
        mixture = dot(weighting_ref[h * 16 : (h + 1) * 16], terms)
        out_ref[:, at] = (combined_ref[:, at] + mixture[:rows] + mixture[rows:]).astype(BF16)


def finish(combined, weighting, got):
    return pl.pallas_call(
        finish_kernel,
        in_specs=[VMEM] * (2 + len(got)),
        out_specs=VMEM,
        out_shape=jax.ShapeDtypeStruct(combined.shape, BF16),
        compiler_params=limits(4),
        name="finish",
    )(combined, weighting, *got)


def swap(x, axis, by):
    return lax.ppermute(x, axis, [(i, i ^ by) for i in range(lax.axis_size(axis))]) if by else x


def on_chips(
    queries,
    key_rows,
    value_rows,
    states,
    decay_rates,
    head_gain,
    out_weight,
    residual,
    norm_gain,
    expert_ids,
    gate_weights,
    expert_gate,
    expert_up,
    expert_down_part,
):
    experts = lax.axis_size("expert")
    local_rows = residual.shape[0]
    columns = out_weight.shape[1]
    top = expert_ids.shape[1]
    capacity = max(2, local_rows * top // experts)
    count = 2 * experts * capacity
    ids, weights = expert_ids.T, gate_weights.T

    messages = attend(
        queries, key_rows, value_rows, states, decay_rates, head_gain, ids, residual, columns, experts
    )
    messages = list(messages)
    messages[0], weight_here, gain_here, gate_here = load(
        messages[0], [out_weight, norm_gain.reshape(1, -1), expert_gate]
    )
    pieces = []
    for d in far_first(experts):
        message = swap(messages[d], "expert", d)
        pieces += [message, swap(message, "half", 1)]

    keep, send = project(pieces, weight_here)
    first = expert_up.shape[0] // 256 * 128 + 128
    choose, residual_part, up_first = route(
        pieces, keep, columns, capacity, expert_ids.shape[1], expert_up, first
    )
    *packed, own, cross = pack(keep, swap(send, "pair", 1), residual_part, choose, experts)

    packed[2:] = [relay(rows, packed[1]) for rows in packed[2:]]
    arrived = [swap(rows, "expert", d) for d, rows in enumerate(packed)]
    near = [jnp.concatenate(arrived[d : d + 2], axis=0) for d in range(0, experts, 2)]
    far = [swap(rows, "pair", 1) for rows in near]
    near_cross = [swap(rows, "half", 1) for rows in near]
    *sums, up_rest = expert_first(
        [near[0], near_cross[0], far[0], swap(far[0], "half", 1)],
        gain_here, gate_here, up_first, expert_up, count,
    )
    cross = swap(cross, "half", 1)
    far[1] = relay(far[1], sums[2], cross)
    hidden, down_here = expert_second(
        [near[1], near_cross[1], far[1], swap(far[1], "half", 1)],
        gain_here, gate_here, up_first, up_rest, sums, expert_down_part, count,
    )

    width = residual.shape[1] // 2
    mine, got = [], []
    for g in range(2):
        terms, send = expert_down(hidden, down_here, g * width, width, count)
        mine.append(terms)
        got.append(swap(send, "half", 1))
    keep, send = chip_sum(mine, got)
    own = cut(own, cross, keep, experts)
    own = [swap(own[d], "expert", d) for d in far_first(experts)]
    terms = pair_sum(keep, swap(send, "pair", 1), capacity, experts, own)
    combined, weighting = own_rows(ids, weights, residual, own, capacity)
    back = [swap(terms[d], "expert", d) for d in far_first(experts)]
    return finish(combined, weighting, back)


def plain_attend(queries, key_rows, value_rows, states, decay_rates, head_gain):
    requests = states.shape[0]
    head_count = states.shape[1]
    head_size = states.shape[2]
    positions = queries.shape[0] // requests
    layout = (requests, positions, head_count, head_size)
    query_plain = queries.reshape(layout)
    key_plain = key_rows.reshape(layout)
    query_float = query_plain.astype(jnp.float32)
    value_float = value_rows.reshape(layout).astype(jnp.float32)
    offsets = jnp.arange(positions, dtype=jnp.float32)
    carried = jnp.exp(-decay_rates[None, :] * (offsets[:, None] + 1.0))
    from_state = jnp.einsum("rphk,rhkv->rphv", query_float, states, precision=HIGHEST)
    from_state = from_state * carried[None, :, :, None]
    scores = jnp.einsum(
        "rthk,rjhk->rhtj", query_plain, key_plain, preferred_element_type=jnp.float32
    )
    distance = offsets[:, None] - offsets[None, :]
    fading = jnp.exp(-decay_rates[:, None, None] * jnp.maximum(distance, 0.0)[None, :, :])
    fading = jnp.where(distance[None, :, :] >= 0.0, fading, 0.0)
    scores = scores * fading[None]
    within = jnp.einsum("rhtj,rjhv->rthv", scores, value_float, precision=HIGHEST)
    mixed_heads = from_state + within
    spread = jnp.mean(mixed_heads * mixed_heads, axis=3, keepdims=True)
    normal = (
        mixed_heads
        * lax.rsqrt(spread + EPSILON)
        * head_gain.reshape(head_count, head_size)[None, None]
    )
    return normal.astype(jnp.bfloat16).reshape(requests * positions, head_count * head_size)


def plain_experts(picked, gate_part, up_part, down_part):
    leading = picked.shape
    flattened = picked.reshape(-1, leading[-1])
    contract = (((1,), (1,)), ((), ()))
    gate_value = lax.dot_general(flattened, gate_part, contract, preferred_element_type=jnp.float32)
    lifted = lax.dot_general(flattened, up_part, contract, preferred_element_type=jnp.float32)
    hidden = (jax.nn.silu(gate_value) * lifted).astype(jnp.bfloat16)
    output = jnp.dot(hidden, down_part, preferred_element_type=jnp.float32)
    return output.reshape(leading)


def plain(
    queries,
    key_rows,
    value_rows,
    states,
    decay_rates,
    head_gain,
    out_weight,
    residual,
    norm_gain,
    expert_ids,
    gate_weights,
    expert_gate,
    expert_up,
    expert_down,
):
    outer_count = lax.axis_size("dev")
    pair_count = lax.axis_size("pair")
    core_count = lax.axis_size("sub")
    attended = plain_attend(queries, key_rows, value_rows, states, decay_rates, head_gain)
    partial_value = jnp.dot(
        lax.all_gather(attended, ("dev", "sub"), axis=0, tiled=True),
        out_weight,
        preferred_element_type=jnp.float32,
    )
    local_rows = residual.shape[0]
    columns = partial_value.shape[1]
    blocks = partial_value.reshape(outer_count, pair_count, core_count, local_rows, columns)
    ordered = jnp.transpose(blocks, (1, 0, 2, 3, 4)).reshape(
        pair_count, outer_count * core_count * local_rows, columns
    )
    shared = lax.psum_scatter(ordered, "pair", scatter_dimension=0, tiled=True)
    shared = shared.reshape(outer_count * core_count, local_rows, columns)
    regrouped = lax.all_to_all(shared, ("dev", "sub"), split_axis=0, concat_axis=2, tiled=True)
    own_rows = regrouped[0]
    combined = residual.astype(jnp.float32) + own_rows
    spread = jnp.mean(combined * combined, axis=-1, keepdims=True)
    normed = (combined * lax.rsqrt(spread + EPSILON) * norm_gain).astype(jnp.bfloat16)
    width = normed.shape[1]
    top_count = expert_ids.shape[1]
    expert_count = outer_count // 2
    capacity = max(2, local_rows * top_count // expert_count)
    chosen_ids = expert_ids.reshape(-1)
    choose = (chosen_ids[:, None] == jnp.arange(expert_count, dtype=jnp.int32)[None, :]).astype(
        jnp.int32
    )
    before = jnp.cumsum(choose, axis=0) - choose
    position = jnp.sum(before * choose, axis=1)
    target = chosen_ids * capacity + position
    placing = (
        target[None, :] == jnp.arange(expert_count * capacity, dtype=jnp.int32)[:, None]
    ).astype(jnp.bfloat16)
    repeated = jnp.repeat(normed, top_count, axis=0)
    packed = jnp.dot(placing, repeated, preferred_element_type=jnp.float32).astype(jnp.bfloat16)
    slot_rows = packed.reshape(expert_count, 1, capacity, width)
    outgoing = jnp.broadcast_to(slot_rows, (expert_count, 2, capacity, width)).reshape(
        outer_count, capacity, width
    )
    partials = plain_experts(
        lax.all_gather(
            lax.all_to_all(outgoing, "dev", split_axis=0, concat_axis=0, tiled=True)[None],
            ("pair", "sub"),
            axis=0,
            tiled=True,
        ),
        expert_gate,
        expert_up,
        expert_down,
    )
    summed_terms = lax.psum_scatter(partials, ("pair", "sub"), scatter_dimension=0, tiled=True)
    returned = lax.all_to_all(summed_terms[0], "dev", split_axis=0, concat_axis=0, tiled=True)
    halves = jnp.sum(returned.reshape(expert_count, -1, capacity, width), axis=1).reshape(
        expert_count * capacity, width
    )
    weighting = placing.astype(jnp.float32) * gate_weights.reshape(-1)[None, :]
    per_slot = lax.dot_general(
        weighting,
        halves,
        (((0,), (0,)), ((), ())),
        precision=HIGHEST,
        preferred_element_type=jnp.float32,
    )
    mixture = jnp.sum(per_slot.reshape(local_rows, top_count, width), axis=1)
    return (combined + mixture).astype(jnp.bfloat16)


def solution(mesh):
    sizes = dict(mesh.shape)
    plain_axes = (("dev",), ("pair", "sub"), ("sub",))
    chip_axes = (("expert", "half"), ("pair",), ())

    def specs(dev, inner, sub):
        requests = P(("grp",) + dev + sub, "pair")
        tokens = P(("grp",) + dev + inner, None)
        units = P(dev + inner, None)
        arguments = (
            requests,
            requests,
            requests,
            P(("grp",) + dev + sub, "pair", None, None),
            P("pair"),
            P("pair"),
            P("pair", dev + sub),
            tokens,
            P(),
            tokens,
            tokens,
            units,
            units,
            units,
        )
        return dict(in_specs=arguments, out_specs=tokens, check_vma=False)

    experts = sizes["dev"] // 2
    chips = sizes["pair"] == 2 and sizes["sub"] == 1 and experts == 4

    def run(*arguments):
        rows = arguments[7].shape[0] // mesh.size
        columns = arguments[6].shape[1] // (sizes["dev"] * sizes["sub"])
        units = arguments[11].shape[0] * sizes["grp"] // mesh.size
        if chips and rows == 8 and columns % 128 == 0 and units % 384 == 0:
            cut = Mesh(
                mesh.devices.reshape(sizes["grp"], experts, 2, 2),
                ("grp", "expert", "half", "pair"),
            )
            return jax.shard_map(on_chips, mesh=cut, **specs(*chip_axes))(*arguments)
        return jax.shard_map(plain, mesh=mesh, **specs(*plain_axes))(*arguments)

    return run
```

```python
import functools

import jax
import jax.numpy as jnp
from jax import lax
from jax.experimental import pallas as pl
from jax.experimental.pallas import tpu as pltpu
from jax.sharding import Mesh
from jax.sharding import PartitionSpec as P

EPSILON = 1e-06
F32 = jnp.float32
BF16 = jnp.bfloat16
MIB = 1 << 20
ID_LANES = 128
HIGHEST = lax.Precision.HIGHEST
VMEM = pl.BlockSpec(memory_space=pltpu.VMEM)
SMEM = pl.BlockSpec(memory_space=pltpu.SMEM)
ANY = pl.BlockSpec(memory_space=pl.ANY)


def in_hbm(*arrays):
    return [pltpu.with_memory_space_constraint(a, pltpu.HBM) for a in arrays]


def limits(mib):
    return pltpu.CompilerParams(vmem_limit_bytes=mib * MIB)


def far_first(count):
    return [-d % count for d in range(count)]


def dot(a, b):
    return jnp.dot(a, b, preferred_element_type=F32)


def dot_t(a, b):
    return lax.dot_general(a, b, (((1,), (1,)), ((), ())), preferred_element_type=F32)


def halves_of(x):
    high = x.astype(BF16)
    return high, (x - high.astype(F32)).astype(BF16)


def attend_kernel(positions, steps, decay_ref, ids_ref, q_ref, k_ref, v_ref, gain_ref, s_ref, residual_ref, *refs):
    outs = refs
    requests, heads, size, _ = s_ref.shape
    rows = q_ref.shape[0]
    step = pl.program_id(0)
    first = step * heads
    @pl.when(step == 0)
    def _():
        width = steps * heads * size
        lanes = ID_LANES
        row = lax.broadcasted_iota(jnp.int32, (rows, lanes), 0)
        lane = lax.broadcasted_iota(jnp.int32, (rows, lanes), 1)
        ids = jnp.zeros((rows, lanes), jnp.int32)
        for k in range(ids_ref.shape[0]):
            for t in range(ids_ref.shape[1]):
                ids = jnp.where((row == t) & (lane == k), ids_ref[k, t], ids)
        ids = ids.astype(F32).astype(BF16)
        columns = outs[0].shape[1] - width - lanes
        expert = lax.axis_index("expert")
        for d, out in enumerate(outs):
            out[:, width : width + lanes] = ids
            base = (expert ^ d) * 2 * columns
            both = [
                residual_ref[:, pl.ds(pl.multiple_of(base + h * columns, columns), columns)]
                for h in range(2)
            ]
            both = jnp.concatenate([b.astype(F32) for b in both], axis=0)
            out[:, width + lanes :] = both.astype(BF16)

    row = lax.broadcasted_iota(jnp.int32, (rows, rows), 0)
    col = lax.broadcasted_iota(jnp.int32, (rows, rows), 1)
    seen = (row // positions == col // positions) & (row >= col)
    distance = jnp.maximum(row - col, 0).astype(F32)
    owner = lax.broadcasted_iota(jnp.int32, (rows, size), 0)
    age = (owner % positions + 1).astype(F32)
    of_request = [
        jnp.where(owner // positions == r, 1.0, 0.0).astype(BF16) for r in range(requests)
    ]
    for i in range(heads):
        rate = decay_ref[first + i]
        at = slice(i * size, (i + 1) * size)
        q = q_ref[:, at]
        spread_q = jnp.concatenate([q * mask for mask in of_request], axis=1)
        high, low = halves_of(s_ref[:, i].reshape(requests * size, size))
        from_state = (dot(spread_q, high) + dot(spread_q, low)) * jnp.exp(-rate * age)
        scores = jnp.where(seen, dot_t(q, k_ref[:, at]) * jnp.exp(-rate * distance), 0.0)
        score_high, score_low = halves_of(scores)
        v = v_ref[:, at]
        mixed = from_state + dot(score_high, v) + dot(score_low, v)
        spread = jnp.mean(mixed * mixed, axis=1, keepdims=True)
        normal = mixed * lax.rsqrt(spread + EPSILON) * gain_ref[:, at]
        normal = normal.astype(BF16)
        for out in outs:
            out[:, pl.ds(pl.multiple_of((first + i) * size, size), size)] = normal


def attend(
    queries, key_rows, value_rows, states, decay_rates, head_gain, ids, residual, columns, experts
):
    requests, heads, size, _ = states.shape
    rows = queries.shape[0]
    step = 8 if heads % 8 == 0 else 1
    wide = pl.BlockSpec((rows, step * size), lambda i: (0, i))
    message = (rows, queries.shape[1] + ID_LANES + columns)
    return pl.pallas_call(
        functools.partial(attend_kernel, rows // requests, heads // step),
        grid=(heads // step,),
        in_specs=[
            SMEM,
            SMEM,
            wide,
            wide,
            wide,
            pl.BlockSpec((1, step * size), lambda i: (0, i)),
            pl.BlockSpec((requests, step, size, size), lambda i: (0, i, 0, 0)),
            pl.BlockSpec(residual.shape, lambda i: (0, 0)),
        ],
        out_specs=[pl.BlockSpec(message, lambda i: (0, 0))] * experts,
        out_shape=[jax.ShapeDtypeStruct(message, BF16)] * experts,
        compiler_params=limits(16),
        name="attention",
    )(
        *in_hbm(
            decay_rates, ids, queries, key_rows, value_rows, head_gain.reshape(1, -1), states, residual,
        )
    )


def load_kernel(count, rows_hbm, *refs):
    sources, rows_ref, targets, sem = refs[:count], refs[count], refs[count + 1 : -1], refs[-1]
    copies = [
        pltpu.make_async_copy(source, target, sem.at[i])
        for i, (source, target) in enumerate(zip(sources, targets))
    ]
    copies.append(pltpu.make_async_copy(rows_hbm, rows_ref, sem.at[count]))
    for copy in copies:
        copy.start()
    for copy in copies:
        copy.wait()


def load(rows, weights):
    size = sum(w.size * w.dtype.itemsize for w in weights)
    return pl.pallas_call(
        functools.partial(load_kernel, len(weights)),
        in_specs=[ANY] * (1 + len(weights)),
        out_specs=[VMEM] * (1 + len(weights)),
        out_shape=[jax.ShapeDtypeStruct(rows.shape, rows.dtype)]
        + [pltpu.VMEM(w.shape, w.dtype) for w in weights],
        scratch_shapes=[pltpu.SemaphoreType.DMA((1 + len(weights),))],
        compiler_params=limits(1),
        cost_estimate=pl.CostEstimate(flops=0, bytes_accessed=size, transcendentals=0),
        name="load",
    )(rows, *in_hbm(*weights))


def project_kernel(*refs):
    pieces, weight_ref, keep_ref, send_ref, x_ref, product_ref = refs[:-5], *refs[-5:]
    depth = weight_ref.shape[0]
    rows = pieces[0].shape[0]
    expert, half, pair = lax.axis_index("expert"), lax.axis_index("half"), lax.axis_index("pair")
    for j, piece in enumerate(pieces):
        base = (expert ^ far_first(len(pieces) // 2)[j // 2]) * 2 + (half ^ (j % 2))
        x_ref[pl.ds(pl.multiple_of(base * rows, rows), rows)] = piece[:, :depth]
    product_ref[...] = dot(x_ref[...], weight_ref[...])
    own = rows // 2
    for b in range(len(pieces)):
        mine = pl.ds(pl.multiple_of(b * rows + pair * own, own), own)
        keep_ref[b * own : (b + 1) * own] = product_ref[mine]
    for b in range(0, len(pieces), 2):
        theirs = [
            product_ref[pl.ds(pl.multiple_of(c * rows + (1 - pair) * own, own), own)]
            for c in (b, b + 1)
        ]
        send_ref[b * own : (b + 2) * own] = jnp.concatenate(theirs, axis=0).astype(BF16)


def project(pieces, weight):
    rows = pieces[0].shape[0] * len(pieces)
    depth, columns = weight.shape
    return pl.pallas_call(
        project_kernel,
        in_specs=[VMEM] * (len(pieces) + 1),
        out_specs=[VMEM] * 2,
        out_shape=[
            jax.ShapeDtypeStruct((rows // 2, columns), F32),
            jax.ShapeDtypeStruct((rows // 2, columns), BF16),
        ],
        scratch_shapes=[pltpu.VMEM((rows, depth), BF16), pltpu.VMEM((rows, columns), F32)],
        compiler_params=limits(8),
        name="projection",
    )(*pieces, weight)


def route_kernel(capacity, top, *refs):
    pieces, weight_hbm = refs[:-7], refs[-6]
    choose_ref, residual_ref, weight_ref, ids_ref, sem = refs[-5:]
    copy = pltpu.make_async_copy(weight_hbm.at[: weight_ref.shape[0]], weight_ref, sem)
    copy.start()
    columns = residual_ref.shape[1]
    own = pieces[0].shape[0] // 2
    rows = ids_ref.shape[0]
    experts = len(pieces) // 2
    expert, half = lax.axis_index("expert"), lax.axis_index("half")
    for j, piece in enumerate(pieces):
        base = (expert ^ far_first(len(pieces) // 2)[j // 2]) * 2 + (half ^ (j % 2))
        at = pl.ds(pl.multiple_of(base * own, own), own)
        last = piece.shape[1] - columns
        both = piece[:, last:].astype(F32)
        residual_ref[at] = jnp.where(half == 0, both[:own], both[own:])
        ids_ref[at] = piece[:, last - ID_LANES : last].astype(F32)[:own]
    ids = ids_ref[...].T
    line = lax.broadcasted_iota(jnp.int32, (8, rows), 0)
    wanted = jnp.bitwise_xor(line, expert).astype(F32)
    named = jnp.zeros((8, rows), F32)
    for k in range(top):
        named = named + jnp.where(ids[k : k + 1] == wanted, 1.0, 0.0)
    before = lax.broadcasted_iota(jnp.int32, (rows, rows), 0)
    after = lax.broadcasted_iota(jnp.int32, (rows, rows), 1)
    earlier = jnp.where((before // own == after // own) & (before < after), 1.0, 0.0)
    rank = dot(named.astype(BF16), earlier.astype(BF16))
    dev = lax.broadcasted_iota(jnp.int32, (8, rows), 1) // own
    place = (dev % 2 * experts + dev // 2) * capacity
    place = jnp.where(named > 0.5, place.astype(F32) + rank, -1.0)
    count = choose_ref.shape[0] // experts
    slot = lax.broadcasted_iota(jnp.int32, (count, rows), 0).astype(F32)
    for d in range(experts):
        choose_ref[d * count : (d + 1) * count] = jnp.where(
            slot == place[d : d + 1], 1.0, 0.0
        ).astype(BF16)
    copy.wait()


def route(pieces, after, columns, capacity, top, weight, first):
    rows = pieces[0].shape[0] // 2 * len(pieces)
    experts = len(pieces) // 2
    return pl.pallas_call(
        functools.partial(route_kernel, capacity, top),
        in_specs=[VMEM] * len(pieces) + [ANY] * 2,
        out_specs=[VMEM] * 3,
        out_shape=[
            jax.ShapeDtypeStruct((experts * 2 * experts * capacity, rows), BF16),
            jax.ShapeDtypeStruct((rows, columns), F32),
            pltpu.VMEM((first, weight.shape[1]), weight.dtype),
        ],
        scratch_shapes=[pltpu.VMEM((rows, ID_LANES), F32), pltpu.SemaphoreType.DMA],
        compiler_params=limits(4),
        cost_estimate=pl.CostEstimate(flops=10**6, bytes_accessed=8 * 10**6, transcendentals=0),
        name="route",
    )(*pieces, after, *in_hbm(weight))


def pack_kernel(keep_ref, got_ref, residual_ref, choose_ref, *refs):
    outs, own_ref, cross_ref, sum_ref = refs[:-3], *refs[-3:]
    sum_ref[...] = keep_ref[...] + got_ref[...].astype(F32)
    combined = (sum_ref[...] + residual_ref[...]).astype(BF16)
    packed = dot(choose_ref[...], combined).astype(BF16)
    count = choose_ref.shape[0] // len(outs)
    own = sum_ref.shape[0] // len(outs) // 2
    expert, half = lax.axis_index("expert"), lax.axis_index("half")
    for d, out in enumerate(outs):
        out[...] = packed[d * count : (d + 1) * count]
    for d in range(0, len(outs), 2):
        for ref, which in ((own_ref, half), (cross_ref, 1 - half)):
            rows = [
                sum_ref[pl.ds(pl.multiple_of(((expert ^ c) * 2 + which) * own, own), own)]
                for c in (d, d + 1)
            ]
            ref[d * own : (d + 2) * own] = jnp.concatenate(rows, axis=0).astype(BF16)


def pack(keep, got, residual, choose, experts):
    rows, columns = keep.shape
    count = choose.shape[0] // experts
    return pl.pallas_call(
        pack_kernel,
        in_specs=[VMEM] * 4,
        out_specs=[VMEM] * (experts + 2),
        out_shape=[jax.ShapeDtypeStruct((count, columns), BF16)] * experts
        + [jax.ShapeDtypeStruct((rows // 2, columns), BF16)] * 2,
        scratch_shapes=[pltpu.VMEM((rows, columns), F32)],
        compiler_params=limits(4),
        name="pack",
    )(keep, got, residual, choose)


def turn(turned_ref, gain_ref, pieces, first, count):
    near, near_cross, far, far_cross = pieces
    columns = near.shape[1]
    expert, half = lax.axis_index("expert"), lax.axis_index("half")
    squares = jnp.zeros((2 * count, 128), F32)
    for d in range(2):
        for c, (mine, theirs) in enumerate(((near, far), (near_cross, far_cross))):
            rows = slice(d * count, (d + 1) * count)
            x = jnp.concatenate([mine[rows].astype(F32), theirs[rows].astype(F32)], axis=0)
            for b in range(columns // 128):
                part = x[:, b * 128 : (b + 1) * 128]
                squares = squares + part * part
            block = (expert ^ (first + d)) * 2 + (half ^ c)
            at = pl.ds(pl.multiple_of(block * columns, columns), columns)
            to = pl.ds(pl.multiple_of(block % 4 * columns, columns), columns)
            turned_ref[to] = (x * gain_ref[:, at]).astype(BF16).T
    return squares


def half_of(ref, first):
    width = ref.shape[1] // 2
    which = (lax.axis_index("expert") ^ first) // 2
    return pl.ds(pl.multiple_of(which * width, width), width)


def expert_first_kernel(count, *refs):
    pieces, gain_ref, gate_ref, up_ref, up_hbm = refs[:4], *refs[4:8]
    gate_sum_ref, up_sum_ref, squares_ref, up_rest_ref, turned_ref, sem = refs[8:]
    cut = up_ref.shape[0]
    rest = pltpu.make_async_copy(up_hbm.at[cut:], up_rest_ref, sem)
    rest.start()
    squares_ref[...] = turn(turned_ref, gain_ref, pieces, 0, count)
    columns = half_of(gate_ref, 0)
    gate_sum_ref[...] = dot(gate_ref[:, columns], turned_ref[...])
    up_sum_ref[:cut] = dot(up_ref[:, columns], turned_ref[...])
    rest.wait()
    up_sum_ref[cut:] = dot(up_rest_ref[:, columns], turned_ref[...])


def expert_second_kernel(count, *refs):
    pieces, gain_ref, gate_ref, up_ref, up_rest_ref = refs[:4], *refs[4:8]
    gate_sum_ref, up_sum_ref, squares_ref, down_hbm, hidden_ref, down_ref = refs[8:14]
    turned_ref, gate_value_ref, sem = refs[14:]
    units, width = gate_ref.shape
    cut = up_ref.shape[0]
    down = pltpu.make_async_copy(down_hbm, down_ref, sem)
    down.start()
    squares = squares_ref[...] + turn(turned_ref, gain_ref, pieces, 2, count)
    spread = jnp.sum(squares.T, axis=0, keepdims=True) / width
    scale = lax.rsqrt(spread + EPSILON)
    columns = half_of(gate_ref, 2)
    gate_value_ref[...] = (gate_sum_ref[...] + dot(gate_ref[:, columns], turned_ref[...])) * scale
    for at, weight_ref in ((slice(0, cut), up_ref), (slice(cut, units), up_rest_ref)):
        gate_value = gate_value_ref[at]
        lifted = (up_sum_ref[at] + dot(weight_ref[:, columns], turned_ref[...])) * scale
        hidden = gate_value / (1.0 + jnp.exp(-gate_value)) * lifted
        hidden_ref[:, at] = hidden.T.astype(BF16)
    down.wait()


def down_kernel(start, wide, hidden_ref, weight_ref, keep_ref, send_ref):
    half = lax.axis_index("half")
    count = keep_ref.shape[0]
    part = count // 2
    for n in range(keep_ref.shape[1] // wide):
        at = slice(start + n * wide, start + (n + 1) * wide)
        out = slice(n * wide, (n + 1) * wide)
        total = dot(hidden_ref[...], weight_ref[:, at])
        for p in range(2):
            low = total[p * count : p * count + part]
            high = total[p * count + part : (p + 1) * count]
            to = slice(p * part, (p + 1) * part)
            keep_ref[to, out] = jnp.where(half == 0, low, high)
            send_ref[to, out] = jnp.where(half == 0, high, low).astype(BF16)


def cost(flops, size):
    return pl.CostEstimate(flops=flops, bytes_accessed=size, transcendentals=0)


def expert_first(pieces, gain, gate, up_first, up_part, count):
    units, width = gate.shape
    cut = up_first.shape[0]
    sums = jax.ShapeDtypeStruct((units, 2 * count), F32)
    return pl.pallas_call(
        functools.partial(expert_first_kernel, count),
        in_specs=[VMEM] * 7 + [ANY],
        out_specs=[VMEM] * 4,
        out_shape=[
            sums,
            sums,
            jax.ShapeDtypeStruct((2 * count, 128), F32),
            pltpu.VMEM((units - cut, width), BF16),
        ],
        scratch_shapes=[pltpu.VMEM((width // 2, 2 * count), BF16), pltpu.SemaphoreType.DMA],
        compiler_params=limits(8),
        cost_estimate=cost(4 * units * width * count, 2 * units * width),
        name="experts_first",
    )(*pieces, gain, gate, up_first, *in_hbm(up_part))


def relay_kernel(rows_ref, *refs):
    refs[-1][...] = rows_ref[...]


def relay(rows, *after):
    return pl.pallas_call(
        relay_kernel,
        in_specs=[VMEM] * (1 + len(after)),
        out_specs=VMEM,
        out_shape=jax.ShapeDtypeStruct(rows.shape, rows.dtype),
        compiler_params=limits(2),
        cost_estimate=cost(0, 10**5),
        name="relay",
    )(rows, *after)


def expert_second(pieces, gain, gate, up_first, up_rest, sums, down_part, count):
    units, width = gate.shape
    return pl.pallas_call(
        functools.partial(expert_second_kernel, count),
        in_specs=[VMEM] * 11 + [ANY],
        out_specs=[VMEM] * 2,
        out_shape=[
            jax.ShapeDtypeStruct((2 * count, units), BF16),
            pltpu.VMEM((units, width), BF16),
        ],
        scratch_shapes=[
            pltpu.VMEM((width // 2, 2 * count), BF16),
            pltpu.VMEM((units, 2 * count), F32),
            pltpu.SemaphoreType.DMA,
        ],
        compiler_params=limits(8),
        cost_estimate=cost(4 * units * width * count, 2 * units * width),
        name="experts_second",
    )(*pieces, gain, gate, up_first, up_rest, *sums, *in_hbm(down_part))


def expert_down(hidden, weight, start, width, count):
    return pl.pallas_call(
        functools.partial(down_kernel, start, 512),
        in_specs=[VMEM] * 2,
        out_specs=[VMEM] * 2,
        out_shape=[
            jax.ShapeDtypeStruct((count, width), F32),
            jax.ShapeDtypeStruct((count, width), BF16),
        ],
        compiler_params=limits(8),
        cost_estimate=cost(4 * hidden.size * width, 2 * hidden.shape[1] * width),
        name="experts_down",
    )(hidden, weight)


def chip_sum_kernel(count, *refs):
    mine, got = refs[:count], refs[count : 2 * count]
    keep_ref, send_ref = refs[2 * count :]
    rows = keep_ref.shape[0]
    width = mine[0].shape[1]
    for g in range(count):
        at = slice(g * width, (g + 1) * width)
        keep_ref[:, at] = mine[g][:rows] + got[g][:rows].astype(F32)
        send_ref[:, at] = (mine[g][rows:] + got[g][rows:].astype(F32)).astype(BF16)


def chip_sum(mine, got):
    rows, width = mine[0].shape
    shape = (rows // 2, width * len(mine))
    return pl.pallas_call(
        functools.partial(chip_sum_kernel, len(mine)),
        in_specs=[VMEM] * (2 * len(mine)),
        out_specs=[VMEM] * 2,
        out_shape=[jax.ShapeDtypeStruct(shape, F32), jax.ShapeDtypeStruct(shape, BF16)],
        compiler_params=limits(4),
        name="chip_sum",
    )(*mine, *got)


def cut_kernel(own_ref, cross_ref, after_ref, *outs):
    rows = own_ref.shape[0] // len(outs)
    own, cross = own_ref[...].astype(F32), cross_ref[...].astype(F32)
    for d, out in enumerate(outs):
        at = slice(d * rows, (d + 1) * rows)
        out[...] = jnp.concatenate([own[at], cross[at]], axis=0).astype(BF16)


def cut(own, cross, after, experts):
    rows, columns = own.shape
    return pl.pallas_call(
        cut_kernel,
        in_specs=[VMEM] * 3,
        out_specs=[VMEM] * experts,
        out_shape=[jax.ShapeDtypeStruct((2 * rows // experts, columns), BF16)] * experts,
        compiler_params=limits(2),
        cost_estimate=cost(0, 10**5),
        name="cut",
    )(own, cross, after)


def pair_sum_kernel(capacity, extra, keep_ref, got_ref, *refs):
    outs, fold_ref = refs[extra:-1], refs[-1]
    experts = len(outs)
    parts = 8 // capacity
    part = outs[0].shape[1]
    total = keep_ref[...] + got_ref[...].astype(F32)
    for e in range(experts):
        mine = total[e * capacity : (e + 1) * capacity]
        fold_ref[e] = jnp.concatenate(
            [mine[:, h * part : (h + 1) * part] for h in range(parts)], axis=0
        )
    expert = lax.axis_index("expert")
    for d, out in enumerate(outs):
        out[...] = fold_ref[expert ^ d].astype(BF16)


def pair_sum(keep, got, capacity, experts, after):
    part = keep.shape[1] * capacity // 8
    return pl.pallas_call(
        functools.partial(pair_sum_kernel, capacity, len(after)),
        in_specs=[VMEM] * (2 + len(after)),
        out_specs=[VMEM] * experts,
        out_shape=[jax.ShapeDtypeStruct((8, part), BF16)] * experts,
        scratch_shapes=[pltpu.VMEM((experts, 8, part), F32)],
        compiler_params=limits(4),
        name="pair_sum",
    )(keep, got, *after)


def own_rows_kernel(capacity, own_ids_ref, weights_ref, residual_ref, *refs):
    pieces, combined_ref, weighting_ref = refs[:-2], *refs[-2:]
    rows = combined_ref.shape[0]
    top, own_count = own_ids_ref.shape
    columns = pieces[0].shape[1]
    expert, half = lax.axis_index("expert"), lax.axis_index("half")
    for d, piece in zip(far_first(len(pieces)), pieces):
        both = piece[...].astype(F32)
        for c in range(2):
            base = ((expert ^ d) * 2 + (half ^ c)) * columns
            at = pl.ds(pl.multiple_of(base, columns), columns)
            combined_ref[:, at] = residual_ref[:, at].astype(F32) + both[c * rows : (c + 1) * rows]

    places = weighting_ref.shape[1]
    row = lax.broadcasted_iota(jnp.int32, (own_count, places), 0)
    at_place = lax.broadcasted_iota(jnp.int32, (own_count, places), 1)
    slot = at_place // 8 * capacity + at_place % capacity
    weighting = jnp.zeros((own_count, places), F32)
    order = [(t, k) for t in range(own_count) for k in range(top)]
    named = [own_ids_ref[k, t] for t, k in order]
    for j, (t, k) in enumerate(order):
        rank = jnp.int32(0)
        for i in range(j):
            rank = rank + jnp.where(named[i] == named[j], 1, 0)
        to = (named[j] ^ expert) * capacity + rank
        weighting = jnp.where((slot == to) & (row == t), weights_ref[k, t], weighting)
    for h in range(8 // capacity):
        high, low = halves_of(jnp.where(at_place % 8 // capacity == h, weighting, 0.0))
        both = jnp.concatenate([high.astype(F32), low.astype(F32)], axis=0)
        weighting_ref[h * 16 : (h + 1) * 16] = both.astype(BF16)


def own_rows(ids, weights, residual, pieces, capacity):
    experts = len(pieces)
    return pl.pallas_call(
        functools.partial(own_rows_kernel, capacity),
        in_specs=[SMEM] * 2 + [VMEM] * (len(pieces) + 1),
        out_specs=[VMEM] * 2,
        out_shape=[
            jax.ShapeDtypeStruct(residual.shape, F32),
            jax.ShapeDtypeStruct((16 * (8 // capacity), experts * 8), BF16),
        ],
        compiler_params=limits(4),
        cost_estimate=cost(10**6, 10**6),
        name="own_rows",
    )(*in_hbm(ids, weights, residual), *pieces)


def finish_kernel(combined_ref, weighting_ref, *refs):
    got, out_ref = refs[:-1], refs[-1]
    part = got[0].shape[1]
    rows = combined_ref.shape[0]
    terms = [got[d][...].astype(F32) for d in far_first(len(got))]
    terms = jnp.concatenate(terms, axis=0).astype(BF16)
    for h in range(combined_ref.shape[1] // part):
        at = slice(h * part, (h + 1) * part)
        mixture = dot(weighting_ref[h * 16 : (h + 1) * 16], terms)
        out_ref[:, at] = (combined_ref[:, at] + mixture[:rows] + mixture[rows:]).astype(BF16)


def finish(combined, weighting, got):
    return pl.pallas_call(
        finish_kernel,
        in_specs=[VMEM] * (2 + len(got)),
        out_specs=VMEM,
        out_shape=jax.ShapeDtypeStruct(combined.shape, BF16),
        compiler_params=limits(4),
        name="finish",
    )(combined, weighting, *got)


def swap(x, axis, by):
    return lax.ppermute(x, axis, [(i, i ^ by) for i in range(lax.axis_size(axis))]) if by else x


def on_chips(
    queries,
    key_rows,
    value_rows,
    states,
    decay_rates,
    head_gain,
    out_weight,
    residual,
    norm_gain,
    expert_ids,
    gate_weights,
    expert_gate,
    expert_up,
    expert_down_part,
):
    experts = lax.axis_size("expert")
    local_rows = residual.shape[0]
    columns = out_weight.shape[1]
    top = expert_ids.shape[1]
    capacity = max(2, local_rows * top // experts)
    count = 2 * experts * capacity
    ids, weights = expert_ids.T, gate_weights.T

    messages = attend(
        queries, key_rows, value_rows, states, decay_rates, head_gain, ids, residual, columns, experts
    )
    messages = list(messages)
    messages[0], weight_here, gain_here, gate_here = load(
        messages[0], [out_weight, norm_gain.reshape(1, -1), expert_gate]
    )
    pieces = []
    for d in far_first(experts):
        message = swap(messages[d], "expert", d)
        pieces += [message, swap(message, "half", 1)]

    keep, send = project(pieces, weight_here)
    first = expert_up.shape[0] // 256 * 128 + 128
    choose, residual_part, up_first = route(
        pieces, keep, columns, capacity, expert_ids.shape[1], expert_up, first
    )
    *packed, own, cross = pack(keep, swap(send, "pair", 1), residual_part, choose, experts)

    packed[2:] = [relay(rows, packed[1]) for rows in packed[2:]]
    arrived = [swap(rows, "expert", d) for d, rows in enumerate(packed)]
    near = [jnp.concatenate(arrived[d : d + 2], axis=0) for d in range(0, experts, 2)]
    far = [swap(rows, "pair", 1) for rows in near]
    near_cross = [swap(rows, "half", 1) for rows in near]
    *sums, up_rest = expert_first(
        [near[0], near_cross[0], far[0], swap(far[0], "half", 1)],
        gain_here, gate_here, up_first, expert_up, count,
    )
    cross = swap(cross, "half", 1)
    far[1] = relay(far[1], sums[2], cross)
    hidden, down_here = expert_second(
        [near[1], near_cross[1], far[1], swap(far[1], "half", 1)],
        gain_here, gate_here, up_first, up_rest, sums, expert_down_part, count,
    )

    width = residual.shape[1] // 2
    mine, got = [], []
    for g in range(2):
        terms, send = expert_down(hidden, down_here, g * width, width, count)
        mine.append(terms)
        got.append(swap(send, "half", 1))
    keep, send = chip_sum(mine, got)
    own = cut(own, cross, keep, experts)
    own = [swap(own[d], "expert", d) for d in far_first(experts)]
    terms = pair_sum(keep, swap(send, "pair", 1), capacity, experts, own)
    combined, weighting = own_rows(ids, weights, residual, own, capacity)
    back = [swap(terms[d], "expert", d) for d in far_first(experts)]
    return finish(combined, weighting, back)


def plain_attend(queries, key_rows, value_rows, states, decay_rates, head_gain):
    requests = states.shape[0]
    head_count = states.shape[1]
    head_size = states.shape[2]
    positions = queries.shape[0] // requests
    layout = (requests, positions, head_count, head_size)
    query_plain = queries.reshape(layout)
    key_plain = key_rows.reshape(layout)
    query_float = query_plain.astype(jnp.float32)
    value_float = value_rows.reshape(layout).astype(jnp.float32)
    offsets = jnp.arange(positions, dtype=jnp.float32)
    carried = jnp.exp(-decay_rates[None, :] * (offsets[:, None] + 1.0))
    from_state = jnp.einsum("rphk,rhkv->rphv", query_float, states, precision=HIGHEST)
    from_state = from_state * carried[None, :, :, None]
    scores = jnp.einsum(
        "rthk,rjhk->rhtj", query_plain, key_plain, preferred_element_type=jnp.float32
    )
    distance = offsets[:, None] - offsets[None, :]
    fading = jnp.exp(-decay_rates[:, None, None] * jnp.maximum(distance, 0.0)[None, :, :])
    fading = jnp.where(distance[None, :, :] >= 0.0, fading, 0.0)
    scores = scores * fading[None]
    within = jnp.einsum("rhtj,rjhv->rthv", scores, value_float, precision=HIGHEST)
    mixed_heads = from_state + within
    spread = jnp.mean(mixed_heads * mixed_heads, axis=3, keepdims=True)
    normal = (
        mixed_heads
        * lax.rsqrt(spread + EPSILON)
        * head_gain.reshape(head_count, head_size)[None, None]
    )
    return normal.astype(jnp.bfloat16).reshape(requests * positions, head_count * head_size)


def plain_experts(picked, gate_part, up_part, down_part):
    leading = picked.shape
    flattened = picked.reshape(-1, leading[-1])
    contract = (((1,), (1,)), ((), ()))
    gate_value = lax.dot_general(flattened, gate_part, contract, preferred_element_type=jnp.float32)
    lifted = lax.dot_general(flattened, up_part, contract, preferred_element_type=jnp.float32)
    hidden = (jax.nn.silu(gate_value) * lifted).astype(jnp.bfloat16)
    output = jnp.dot(hidden, down_part, preferred_element_type=jnp.float32)
    return output.reshape(leading)


def plain(
    queries,
    key_rows,
    value_rows,
    states,
    decay_rates,
    head_gain,
    out_weight,
    residual,
    norm_gain,
    expert_ids,
    gate_weights,
    expert_gate,
    expert_up,
    expert_down,
):
    outer_count = lax.axis_size("dev")
    pair_count = lax.axis_size("pair")
    core_count = lax.axis_size("sub")
    attended = plain_attend(queries, key_rows, value_rows, states, decay_rates, head_gain)
    partial_value = jnp.dot(
        lax.all_gather(attended, ("dev", "sub"), axis=0, tiled=True),
        out_weight,
        preferred_element_type=jnp.float32,
    )
    local_rows = residual.shape[0]
    columns = partial_value.shape[1]
    blocks = partial_value.reshape(outer_count, pair_count, core_count, local_rows, columns)
    ordered = jnp.transpose(blocks, (1, 0, 2, 3, 4)).reshape(
        pair_count, outer_count * core_count * local_rows, columns
    )
    shared = lax.psum_scatter(ordered, "pair", scatter_dimension=0, tiled=True)
    shared = shared.reshape(outer_count * core_count, local_rows, columns)
    regrouped = lax.all_to_all(shared, ("dev", "sub"), split_axis=0, concat_axis=2, tiled=True)
    own_rows = regrouped[0]
    combined = residual.astype(jnp.float32) + own_rows
    spread = jnp.mean(combined * combined, axis=-1, keepdims=True)
    normed = (combined * lax.rsqrt(spread + EPSILON) * norm_gain).astype(jnp.bfloat16)
    width = normed.shape[1]
    top_count = expert_ids.shape[1]
    expert_count = outer_count // 2
    capacity = max(2, local_rows * top_count // expert_count)
    chosen_ids = expert_ids.reshape(-1)
    choose = (chosen_ids[:, None] == jnp.arange(expert_count, dtype=jnp.int32)[None, :]).astype(
        jnp.int32
    )
    before = jnp.cumsum(choose, axis=0) - choose
    position = jnp.sum(before * choose, axis=1)
    target = chosen_ids * capacity + position
    placing = (
        target[None, :] == jnp.arange(expert_count * capacity, dtype=jnp.int32)[:, None]
    ).astype(jnp.bfloat16)
    repeated = jnp.repeat(normed, top_count, axis=0)
    packed = jnp.dot(placing, repeated, preferred_element_type=jnp.float32).astype(jnp.bfloat16)
    slot_rows = packed.reshape(expert_count, 1, capacity, width)
    outgoing = jnp.broadcast_to(slot_rows, (expert_count, 2, capacity, width)).reshape(
        outer_count, capacity, width
    )
    partials = plain_experts(
        lax.all_gather(
            lax.all_to_all(outgoing, "dev", split_axis=0, concat_axis=0, tiled=True)[None],
            ("pair", "sub"),
            axis=0,
            tiled=True,
        ),
        expert_gate,
        expert_up,
        expert_down,
    )
    summed_terms = lax.psum_scatter(partials, ("pair", "sub"), scatter_dimension=0, tiled=True)
    returned = lax.all_to_all(summed_terms[0], "dev", split_axis=0, concat_axis=0, tiled=True)
    halves = jnp.sum(returned.reshape(expert_count, -1, capacity, width), axis=1).reshape(
        expert_count * capacity, width
    )
    weighting = placing.astype(jnp.float32) * gate_weights.reshape(-1)[None, :]
    per_slot = lax.dot_general(
        weighting,
        halves,
        (((0,), (0,)), ((), ())),
        precision=HIGHEST,
        preferred_element_type=jnp.float32,
    )
    mixture = jnp.sum(per_slot.reshape(local_rows, top_count, width), axis=1)
    return (combined + mixture).astype(jnp.bfloat16)


def solution(mesh):
    sizes = dict(mesh.shape)
    plain_axes = (("dev",), ("pair", "sub"), ("sub",))
    chip_axes = (("expert", "half"), ("pair",), ())

    def specs(dev, inner, sub):
        requests = P(("grp",) + dev + sub, "pair")
        tokens = P(("grp",) + dev + inner, None)
        units = P(dev + inner, None)
        arguments = (
            requests,
            requests,
            requests,
            P(("grp",) + dev + sub, "pair", None, None),
            P("pair"),
            P("pair"),
            P("pair", dev + sub),
            tokens,
            P(),
            tokens,
            tokens,
            units,
            units,
            units,
        )
        return dict(in_specs=arguments, out_specs=tokens, check_vma=False)

    experts = sizes["dev"] // 2
    chips = sizes["pair"] == 2 and sizes["sub"] == 1 and experts == 4

    def run(*arguments):
        rows = arguments[7].shape[0] // mesh.size
        columns = arguments[6].shape[1] // (sizes["dev"] * sizes["sub"])
        units = arguments[11].shape[0] * sizes["grp"] // mesh.size
        if chips and rows == 8 and columns % 128 == 0 and units % 384 == 0:
            cut = Mesh(
                mesh.devices.reshape(sizes["grp"], experts, 2, 2),
                ("grp", "expert", "half", "pair"),
            )
            return jax.shard_map(on_chips, mesh=cut, **specs(*chip_axes))(*arguments)
        return jax.shard_map(plain, mesh=mesh, **specs(*plain_axes))(*arguments)

    return run
```

```python
import functools

import jax
import jax.numpy as jnp
from jax import lax
from jax.experimental import pallas as pl
from jax.experimental.pallas import tpu as pltpu
from jax.sharding import Mesh
from jax.sharding import PartitionSpec as P

EPSILON = 1e-06
F32 = jnp.float32
BF16 = jnp.bfloat16
MIB = 1 << 20
ID_LANES = 128
HIGHEST = lax.Precision.HIGHEST
VMEM = pl.BlockSpec(memory_space=pltpu.VMEM)
SMEM = pl.BlockSpec(memory_space=pltpu.SMEM)
ANY = pl.BlockSpec(memory_space=pl.ANY)


def in_hbm(*arrays):
    return [pltpu.with_memory_space_constraint(a, pltpu.HBM) for a in arrays]


def limits(mib):
    return pltpu.CompilerParams(vmem_limit_bytes=mib * MIB)


def far_first(count):
    return [-d % count for d in range(count)]


def dot(a, b):
    return jnp.dot(a, b, preferred_element_type=F32)


def dot_t(a, b):
    return lax.dot_general(a, b, (((1,), (1,)), ((), ())), preferred_element_type=F32)


def halves_of(x):
    high = x.astype(BF16)
    return high, (x - high.astype(F32)).astype(BF16)


def attend_kernel(positions, steps, decay_ref, ids_ref, q_ref, k_ref, v_ref, gain_ref, s_ref, residual_ref, *refs):
    outs = refs
    requests, heads, size, _ = s_ref.shape
    rows = q_ref.shape[0]
    step = pl.program_id(0)
    first = step * heads
    @pl.when(step == 0)
    def _():
        width = steps * heads * size
        lanes = ID_LANES
        row = lax.broadcasted_iota(jnp.int32, (rows, lanes), 0)
        lane = lax.broadcasted_iota(jnp.int32, (rows, lanes), 1)
        ids = jnp.zeros((rows, lanes), jnp.int32)
        for k in range(ids_ref.shape[0]):
            for t in range(ids_ref.shape[1]):
                ids = jnp.where((row == t) & (lane == k), ids_ref[k, t], ids)
        ids = ids.astype(F32).astype(BF16)
        columns = outs[0].shape[1] - width - lanes
        expert = lax.axis_index("expert")
        for d, out in enumerate(outs):
            out[:, width : width + lanes] = ids
            base = (expert ^ d) * 2 * columns
            both = [
                residual_ref[:, pl.ds(pl.multiple_of(base + h * columns, columns), columns)]
                for h in range(2)
            ]
            both = jnp.concatenate([b.astype(F32) for b in both], axis=0)
            out[:, width + lanes :] = both.astype(BF16)

    row = lax.broadcasted_iota(jnp.int32, (rows, rows), 0)
    col = lax.broadcasted_iota(jnp.int32, (rows, rows), 1)
    seen = (row // positions == col // positions) & (row >= col)
    distance = jnp.maximum(row - col, 0).astype(F32)
    owner = lax.broadcasted_iota(jnp.int32, (rows, size), 0)
    age = (owner % positions + 1).astype(F32)
    of_request = [
        jnp.where(owner // positions == r, 1.0, 0.0).astype(BF16) for r in range(requests)
    ]
    for i in range(heads):
        rate = decay_ref[first + i]
        at = slice(i * size, (i + 1) * size)
        q = q_ref[:, at]
        spread_q = jnp.concatenate([q * mask for mask in of_request], axis=1)
        high, low = halves_of(s_ref[:, i].reshape(requests * size, size))
        from_state = (dot(spread_q, high) + dot(spread_q, low)) * jnp.exp(-rate * age)
        scores = jnp.where(seen, dot_t(q, k_ref[:, at]) * jnp.exp(-rate * distance), 0.0)
        score_high, score_low = halves_of(scores)
        v = v_ref[:, at]
        mixed = from_state + dot(score_high, v) + dot(score_low, v)
        spread = jnp.mean(mixed * mixed, axis=1, keepdims=True)
        normal = mixed * lax.rsqrt(spread + EPSILON) * gain_ref[:, at]
        normal = normal.astype(BF16)
        for out in outs:
            out[:, pl.ds(pl.multiple_of((first + i) * size, size), size)] = normal


def attend(
    queries, key_rows, value_rows, states, decay_rates, head_gain, ids, residual, columns, experts
):
    requests, heads, size, _ = states.shape
    rows = queries.shape[0]
    step = 8 if heads % 8 == 0 else 1
    wide = pl.BlockSpec((rows, step * size), lambda i: (0, i))
    message = (rows, queries.shape[1] + ID_LANES + columns)
    return pl.pallas_call(
        functools.partial(attend_kernel, rows // requests, heads // step),
        grid=(heads // step,),
        in_specs=[
            SMEM,
            SMEM,
            wide,
            wide,
            wide,
            pl.BlockSpec((1, step * size), lambda i: (0, i)),
            pl.BlockSpec((requests, step, size, size), lambda i: (0, i, 0, 0)),
            pl.BlockSpec(residual.shape, lambda i: (0, 0)),
        ],
        out_specs=[pl.BlockSpec(message, lambda i: (0, 0))] * experts,
        out_shape=[jax.ShapeDtypeStruct(message, BF16)] * experts,
        compiler_params=limits(16),
        name="attention",
    )(
        *in_hbm(
            decay_rates, ids, queries, key_rows, value_rows, head_gain.reshape(1, -1), states, residual,
        )
    )


def load_kernel(count, rows_hbm, *refs):
    sources, rows_ref, targets, sem = refs[:count], refs[count], refs[count + 1 : -1], refs[-1]
    copies = [
        pltpu.make_async_copy(source, target, sem.at[i])
        for i, (source, target) in enumerate(zip(sources, targets))
    ]
    copies.append(pltpu.make_async_copy(rows_hbm, rows_ref, sem.at[count]))
    for copy in copies:
        copy.start()
    for copy in copies:
        copy.wait()


def load(rows, weights):
    size = sum(w.size * w.dtype.itemsize for w in weights)
    return pl.pallas_call(
        functools.partial(load_kernel, len(weights)),
        in_specs=[ANY] * (1 + len(weights)),
        out_specs=[VMEM] * (1 + len(weights)),
        out_shape=[jax.ShapeDtypeStruct(rows.shape, rows.dtype)]
        + [pltpu.VMEM(w.shape, w.dtype) for w in weights],
        scratch_shapes=[pltpu.SemaphoreType.DMA((1 + len(weights),))],
        compiler_params=limits(1),
        cost_estimate=pl.CostEstimate(flops=0, bytes_accessed=size, transcendentals=0),
        name="load",
    )(rows, *in_hbm(*weights))


def project_kernel(*refs):
    pieces, weight_ref, keep_ref, send_ref, x_ref, product_ref = refs[:-5], *refs[-5:]
    depth = weight_ref.shape[0]
    rows = pieces[0].shape[0]
    expert, half, pair = lax.axis_index("expert"), lax.axis_index("half"), lax.axis_index("pair")
    for j, piece in enumerate(pieces):
        base = (expert ^ far_first(len(pieces) // 2)[j // 2]) * 2 + (half ^ (j % 2))
        x_ref[pl.ds(pl.multiple_of(base * rows, rows), rows)] = piece[:, :depth]
    product_ref[...] = dot(x_ref[...], weight_ref[...])
    own = rows // 2
    for b in range(len(pieces)):
        mine = pl.ds(pl.multiple_of(b * rows + pair * own, own), own)
        keep_ref[b * own : (b + 1) * own] = product_ref[mine]
    for b in range(0, len(pieces), 2):
        theirs = [
            product_ref[pl.ds(pl.multiple_of(c * rows + (1 - pair) * own, own), own)]
            for c in (b, b + 1)
        ]
        send_ref[b * own : (b + 2) * own] = jnp.concatenate(theirs, axis=0).astype(BF16)


def project(pieces, weight):
    rows = pieces[0].shape[0] * len(pieces)
    depth, columns = weight.shape
    return pl.pallas_call(
        project_kernel,
        in_specs=[VMEM] * (len(pieces) + 1),
        out_specs=[VMEM] * 2,
        out_shape=[
            jax.ShapeDtypeStruct((rows // 2, columns), F32),
            jax.ShapeDtypeStruct((rows // 2, columns), BF16),
        ],
        scratch_shapes=[pltpu.VMEM((rows, depth), BF16), pltpu.VMEM((rows, columns), F32)],
        compiler_params=limits(8),
        name="projection",
    )(*pieces, weight)


def route_kernel(capacity, top, *refs):
    pieces, weight_hbm = refs[:-7], refs[-6]
    choose_ref, residual_ref, weight_ref, ids_ref, sem = refs[-5:]
    copy = pltpu.make_async_copy(weight_hbm.at[: weight_ref.shape[0]], weight_ref, sem)
    copy.start()
    columns = residual_ref.shape[1]
    own = pieces[0].shape[0] // 2
    rows = ids_ref.shape[0]
    experts = len(pieces) // 2
    expert, half = lax.axis_index("expert"), lax.axis_index("half")
    for j, piece in enumerate(pieces):
        base = (expert ^ far_first(len(pieces) // 2)[j // 2]) * 2 + (half ^ (j % 2))
        at = pl.ds(pl.multiple_of(base * own, own), own)
        last = piece.shape[1] - columns
        both = piece[:, last:].astype(F32)
        residual_ref[at] = jnp.where(half == 0, both[:own], both[own:])
        ids_ref[at] = piece[:, last - ID_LANES : last].astype(F32)[:own]
    ids = ids_ref[...].T
    line = lax.broadcasted_iota(jnp.int32, (8, rows), 0)
    wanted = jnp.bitwise_xor(line, expert).astype(F32)
    named = jnp.zeros((8, rows), F32)
    for k in range(top):
        named = named + jnp.where(ids[k : k + 1] == wanted, 1.0, 0.0)
    before = lax.broadcasted_iota(jnp.int32, (rows, rows), 0)
    after = lax.broadcasted_iota(jnp.int32, (rows, rows), 1)
    earlier = jnp.where((before // own == after // own) & (before < after), 1.0, 0.0)
    rank = dot(named.astype(BF16), earlier.astype(BF16))
    dev = lax.broadcasted_iota(jnp.int32, (8, rows), 1) // own
    place = (dev % 2 * experts + dev // 2) * capacity
    place = jnp.where(named > 0.5, place.astype(F32) + rank, -1.0)
    count = choose_ref.shape[0] // experts
    slot = lax.broadcasted_iota(jnp.int32, (count, rows), 0).astype(F32)
    for d in range(experts):
        choose_ref[d * count : (d + 1) * count] = jnp.where(
            slot == place[d : d + 1], 1.0, 0.0
        ).astype(BF16)
    copy.wait()


def route(pieces, after, columns, capacity, top, weight, first):
    rows = pieces[0].shape[0] // 2 * len(pieces)
    experts = len(pieces) // 2
    return pl.pallas_call(
        functools.partial(route_kernel, capacity, top),
        in_specs=[VMEM] * len(pieces) + [ANY] * 2,
        out_specs=[VMEM] * 3,
        out_shape=[
            jax.ShapeDtypeStruct((experts * 2 * experts * capacity, rows), BF16),
            jax.ShapeDtypeStruct((rows, columns), F32),
            pltpu.VMEM((first, weight.shape[1]), weight.dtype),
        ],
        scratch_shapes=[pltpu.VMEM((rows, ID_LANES), F32), pltpu.SemaphoreType.DMA],
        compiler_params=limits(4),
        cost_estimate=pl.CostEstimate(flops=10**6, bytes_accessed=8 * 10**6, transcendentals=0),
        name="route",
    )(*pieces, after, *in_hbm(weight))


def pack_kernel(keep_ref, got_ref, residual_ref, choose_ref, *refs):
    outs, own_ref, cross_ref, sum_ref = refs[:-3], *refs[-3:]
    sum_ref[...] = keep_ref[...] + got_ref[...].astype(F32)
    combined = (sum_ref[...] + residual_ref[...]).astype(BF16)
    packed = dot(choose_ref[...], combined).astype(BF16)
    count = choose_ref.shape[0] // len(outs)
    own = sum_ref.shape[0] // len(outs) // 2
    expert, half = lax.axis_index("expert"), lax.axis_index("half")
    for d, out in enumerate(outs):
        out[...] = packed[d * count : (d + 1) * count]
    for d in range(0, len(outs), 2):
        for ref, which in ((own_ref, half), (cross_ref, 1 - half)):
            rows = [
                sum_ref[pl.ds(pl.multiple_of(((expert ^ c) * 2 + which) * own, own), own)]
                for c in (d, d + 1)
            ]
            ref[d * own : (d + 2) * own] = jnp.concatenate(rows, axis=0).astype(BF16)


def pack(keep, got, residual, choose, experts):
    rows, columns = keep.shape
    count = choose.shape[0] // experts
    return pl.pallas_call(
        pack_kernel,
        in_specs=[VMEM] * 4,
        out_specs=[VMEM] * (experts + 2),
        out_shape=[jax.ShapeDtypeStruct((count, columns), BF16)] * experts
        + [jax.ShapeDtypeStruct((rows // 2, columns), BF16)] * 2,
        scratch_shapes=[pltpu.VMEM((rows, columns), F32)],
        compiler_params=limits(4),
        name="pack",
    )(keep, got, residual, choose)


def turn(turned_ref, gain_ref, pieces, first, count):
    near, near_cross, far, far_cross = pieces
    columns = near.shape[1]
    expert, half = lax.axis_index("expert"), lax.axis_index("half")
    squares = jnp.zeros((2 * count, 128), F32)
    for d in range(2):
        for c, (mine, theirs) in enumerate(((near, far), (near_cross, far_cross))):
            rows = slice(d * count, (d + 1) * count)
            x = jnp.concatenate([mine[rows].astype(F32), theirs[rows].astype(F32)], axis=0)
            for b in range(columns // 128):
                part = x[:, b * 128 : (b + 1) * 128]
                squares = squares + part * part
            block = (expert ^ (first + d)) * 2 + (half ^ c)
            at = pl.ds(pl.multiple_of(block * columns, columns), columns)
            to = pl.ds(pl.multiple_of(block % 4 * columns, columns), columns)
            turned_ref[to] = (x * gain_ref[:, at]).astype(BF16).T
    return squares


def meet(ref, at, turned_ref, first):
    width = ref.shape[1] // 4
    start = (lax.axis_index("expert") ^ first) // 2 * 2 * width
    halves = [
        dot(
            ref[at, pl.ds(pl.multiple_of(start + h * width, width), width)],
            turned_ref[h * width : (h + 1) * width],
        )
        for h in range(2)
    ]
    return halves[0] + halves[1]


def expert_first_kernel(count, *refs):
    pieces, gain_ref, gate_ref, up_ref, up_hbm = refs[:4], *refs[4:8]
    gate_sum_ref, up_sum_ref, squares_ref, up_rest_ref, turned_ref, sem = refs[8:]
    cut = up_ref.shape[0]
    rest = pltpu.make_async_copy(up_hbm.at[cut:], up_rest_ref, sem)
    rest.start()
    squares_ref[...] = turn(turned_ref, gain_ref, pieces, 0, count)
    gate_sum_ref[...] = meet(gate_ref, slice(None), turned_ref, 0)
    up_sum_ref[:cut] = meet(up_ref, slice(None), turned_ref, 0)
    rest.wait()
    up_sum_ref[cut:] = meet(up_rest_ref, slice(None), turned_ref, 0)


def expert_second_kernel(count, *refs):
    pieces, gain_ref, gate_ref, up_ref, up_rest_ref = refs[:4], *refs[4:8]
    gate_sum_ref, up_sum_ref, squares_ref, down_hbm, hidden_ref, down_ref = refs[8:14]
    turned_ref, gate_value_ref, sem = refs[14:]
    units, width = gate_ref.shape
    cut = up_ref.shape[0]
    down = pltpu.make_async_copy(down_hbm, down_ref, sem)
    down.start()
    squares = squares_ref[...] + turn(turned_ref, gain_ref, pieces, 2, count)
    spread = jnp.sum(squares.T, axis=0, keepdims=True) / width
    scale = lax.rsqrt(spread + EPSILON)
    gate_value_ref[...] = (gate_sum_ref[...] + meet(gate_ref, slice(None), turned_ref, 2)) * scale
    for at, weight_ref in ((slice(0, cut), up_ref), (slice(cut, units), up_rest_ref)):
        gate_value = gate_value_ref[at]
        lifted = (up_sum_ref[at] + meet(weight_ref, slice(None), turned_ref, 2)) * scale
        hidden = gate_value / (1.0 + jnp.exp(-gate_value)) * lifted
        hidden_ref[:, at] = hidden.T.astype(BF16)
    down.wait()


def down_kernel(start, wide, hidden_ref, weight_ref, keep_ref, send_ref):
    half = lax.axis_index("half")
    count = keep_ref.shape[0]
    part = count // 2
    for n in range(keep_ref.shape[1] // wide):
        at = slice(start + n * wide, start + (n + 1) * wide)
        out = slice(n * wide, (n + 1) * wide)
        total = dot(hidden_ref[...], weight_ref[:, at])
        for p in range(2):
            low = total[p * count : p * count + part]
            high = total[p * count + part : (p + 1) * count]
            to = slice(p * part, (p + 1) * part)
            keep_ref[to, out] = jnp.where(half == 0, low, high)
            send_ref[to, out] = jnp.where(half == 0, high, low).astype(BF16)


def cost(flops, size):
    return pl.CostEstimate(flops=flops, bytes_accessed=size, transcendentals=0)


def expert_first(pieces, gain, gate, up_first, up_part, count):
    units, width = gate.shape
    cut = up_first.shape[0]
    sums = jax.ShapeDtypeStruct((units, 2 * count), F32)
    return pl.pallas_call(
        functools.partial(expert_first_kernel, count),
        in_specs=[VMEM] * 7 + [ANY],
        out_specs=[VMEM] * 4,
        out_shape=[
            sums,
            sums,
            jax.ShapeDtypeStruct((2 * count, 128), F32),
            pltpu.VMEM((units - cut, width), BF16),
        ],
        scratch_shapes=[pltpu.VMEM((width // 2, 2 * count), BF16), pltpu.SemaphoreType.DMA],
        compiler_params=limits(8),
        cost_estimate=cost(4 * units * width * count, 2 * units * width),
        name="experts_first",
    )(*pieces, gain, gate, up_first, *in_hbm(up_part))


def relay_kernel(rows_ref, *refs):
    refs[-1][...] = rows_ref[...]


def relay(rows, *after):
    return pl.pallas_call(
        relay_kernel,
        in_specs=[VMEM] * (1 + len(after)),
        out_specs=VMEM,
        out_shape=jax.ShapeDtypeStruct(rows.shape, rows.dtype),
        compiler_params=limits(2),
        cost_estimate=cost(0, 10**5),
        name="relay",
    )(rows, *after)


def expert_second(pieces, gain, gate, up_first, up_rest, sums, down_part, count):
    units, width = gate.shape
    return pl.pallas_call(
        functools.partial(expert_second_kernel, count),
        in_specs=[VMEM] * 11 + [ANY],
        out_specs=[VMEM] * 2,
        out_shape=[
            jax.ShapeDtypeStruct((2 * count, units), BF16),
            pltpu.VMEM((units, width), BF16),
        ],
        scratch_shapes=[
            pltpu.VMEM((width // 2, 2 * count), BF16),
            pltpu.VMEM((units, 2 * count), F32),
            pltpu.SemaphoreType.DMA,
        ],
        compiler_params=limits(8),
        cost_estimate=cost(4 * units * width * count, 2 * units * width),
        name="experts_second",
    )(*pieces, gain, gate, up_first, up_rest, *sums, *in_hbm(down_part))


def expert_down(hidden, weight, start, width, count):
    return pl.pallas_call(
        functools.partial(down_kernel, start, 512),
        in_specs=[VMEM] * 2,
        out_specs=[VMEM] * 2,
        out_shape=[
            jax.ShapeDtypeStruct((count, width), F32),
            jax.ShapeDtypeStruct((count, width), BF16),
        ],
        compiler_params=limits(8),
        cost_estimate=cost(4 * hidden.size * width, 2 * hidden.shape[1] * width),
        name="experts_down",
    )(hidden, weight)


def chip_sum_kernel(count, *refs):
    mine, got = refs[:count], refs[count : 2 * count]
    keep_ref, send_ref = refs[2 * count :]
    rows = keep_ref.shape[0]
    width = mine[0].shape[1]
    for g in range(count):
        at = slice(g * width, (g + 1) * width)
        keep_ref[:, at] = mine[g][:rows] + got[g][:rows].astype(F32)
        send_ref[:, at] = (mine[g][rows:] + got[g][rows:].astype(F32)).astype(BF16)


def chip_sum(mine, got):
    rows, width = mine[0].shape
    shape = (rows // 2, width * len(mine))
    return pl.pallas_call(
        functools.partial(chip_sum_kernel, len(mine)),
        in_specs=[VMEM] * (2 * len(mine)),
        out_specs=[VMEM] * 2,
        out_shape=[jax.ShapeDtypeStruct(shape, F32), jax.ShapeDtypeStruct(shape, BF16)],
        compiler_params=limits(4),
        name="chip_sum",
    )(*mine, *got)


def cut_kernel(own_ref, cross_ref, after_ref, *outs):
    rows = own_ref.shape[0] // len(outs)
    own, cross = own_ref[...].astype(F32), cross_ref[...].astype(F32)
    for d, out in enumerate(outs):
        at = slice(d * rows, (d + 1) * rows)
        out[...] = jnp.concatenate([own[at], cross[at]], axis=0).astype(BF16)


def cut(own, cross, after, experts):
    rows, columns = own.shape
    return pl.pallas_call(
        cut_kernel,
        in_specs=[VMEM] * 3,
        out_specs=[VMEM] * experts,
        out_shape=[jax.ShapeDtypeStruct((2 * rows // experts, columns), BF16)] * experts,
        compiler_params=limits(2),
        cost_estimate=cost(0, 10**5),
        name="cut",
    )(own, cross, after)


def pair_sum_kernel(capacity, extra, keep_ref, got_ref, *refs):
    outs, fold_ref = refs[extra:-1], refs[-1]
    experts = len(outs)
    parts = 8 // capacity
    part = outs[0].shape[1]
    total = keep_ref[...] + got_ref[...].astype(F32)
    for e in range(experts):
        mine = total[e * capacity : (e + 1) * capacity]
        fold_ref[e] = jnp.concatenate(
            [mine[:, h * part : (h + 1) * part] for h in range(parts)], axis=0
        )
    expert = lax.axis_index("expert")
    for d, out in enumerate(outs):
        out[...] = fold_ref[expert ^ d].astype(BF16)


def pair_sum(keep, got, capacity, experts, after):
    part = keep.shape[1] * capacity // 8
    return pl.pallas_call(
        functools.partial(pair_sum_kernel, capacity, len(after)),
        in_specs=[VMEM] * (2 + len(after)),
        out_specs=[VMEM] * experts,
        out_shape=[jax.ShapeDtypeStruct((8, part), BF16)] * experts,
        scratch_shapes=[pltpu.VMEM((experts, 8, part), F32)],
        compiler_params=limits(4),
        name="pair_sum",
    )(keep, got, *after)


def own_rows_kernel(capacity, own_ids_ref, weights_ref, residual_ref, *refs):
    pieces, combined_ref, weighting_ref = refs[:-2], *refs[-2:]
    rows = combined_ref.shape[0]
    top, own_count = own_ids_ref.shape
    columns = pieces[0].shape[1]
    expert, half = lax.axis_index("expert"), lax.axis_index("half")
    for d, piece in zip(far_first(len(pieces)), pieces):
        both = piece[...].astype(F32)
        for c in range(2):
            base = ((expert ^ d) * 2 + (half ^ c)) * columns
            at = pl.ds(pl.multiple_of(base, columns), columns)
            combined_ref[:, at] = residual_ref[:, at].astype(F32) + both[c * rows : (c + 1) * rows]

    places = weighting_ref.shape[1]
    row = lax.broadcasted_iota(jnp.int32, (own_count, places), 0)
    at_place = lax.broadcasted_iota(jnp.int32, (own_count, places), 1)
    slot = at_place // 8 * capacity + at_place % capacity
    weighting = jnp.zeros((own_count, places), F32)
    order = [(t, k) for t in range(own_count) for k in range(top)]
    named = [own_ids_ref[k, t] for t, k in order]
    for j, (t, k) in enumerate(order):
        rank = jnp.int32(0)
        for i in range(j):
            rank = rank + jnp.where(named[i] == named[j], 1, 0)
        to = (named[j] ^ expert) * capacity + rank
        weighting = jnp.where((slot == to) & (row == t), weights_ref[k, t], weighting)
    for h in range(8 // capacity):
        high, low = halves_of(jnp.where(at_place % 8 // capacity == h, weighting, 0.0))
        both = jnp.concatenate([high.astype(F32), low.astype(F32)], axis=0)
        weighting_ref[h * 16 : (h + 1) * 16] = both.astype(BF16)


def own_rows(ids, weights, residual, pieces, capacity):
    experts = len(pieces)
    return pl.pallas_call(
        functools.partial(own_rows_kernel, capacity),
        in_specs=[SMEM] * 2 + [VMEM] * (len(pieces) + 1),
        out_specs=[VMEM] * 2,
        out_shape=[
            jax.ShapeDtypeStruct(residual.shape, F32),
            jax.ShapeDtypeStruct((16 * (8 // capacity), experts * 8), BF16),
        ],
        compiler_params=limits(4),
        cost_estimate=cost(10**6, 10**6),
        name="own_rows",
    )(*in_hbm(ids, weights, residual), *pieces)


def finish_kernel(combined_ref, weighting_ref, *refs):
    got, out_ref = refs[:-1], refs[-1]
    part = got[0].shape[1]
    rows = combined_ref.shape[0]
    terms = [got[d][...].astype(F32) for d in far_first(len(got))]
    terms = jnp.concatenate(terms, axis=0).astype(BF16)
    for h in range(combined_ref.shape[1] // part):
        at = slice(h * part, (h + 1) * part)
        mixture = dot(weighting_ref[h * 16 : (h + 1) * 16], terms)
        out_ref[:, at] = (combined_ref[:, at] + mixture[:rows] + mixture[rows:]).astype(BF16)


def finish(combined, weighting, got):
    return pl.pallas_call(
        finish_kernel,
        in_specs=[VMEM] * (2 + len(got)),
        out_specs=VMEM,
        out_shape=jax.ShapeDtypeStruct(combined.shape, BF16),
        compiler_params=limits(4),
        name="finish",
    )(combined, weighting, *got)


def swap(x, axis, by):
    return lax.ppermute(x, axis, [(i, i ^ by) for i in range(lax.axis_size(axis))]) if by else x


def on_chips(
    queries,
    key_rows,
    value_rows,
    states,
    decay_rates,
    head_gain,
    out_weight,
    residual,
    norm_gain,
    expert_ids,
    gate_weights,
    expert_gate,
    expert_up,
    expert_down_part,
):
    experts = lax.axis_size("expert")
    local_rows = residual.shape[0]
    columns = out_weight.shape[1]
    top = expert_ids.shape[1]
    capacity = max(2, local_rows * top // experts)
    count = 2 * experts * capacity
    ids, weights = expert_ids.T, gate_weights.T

    messages = attend(
        queries, key_rows, value_rows, states, decay_rates, head_gain, ids, residual, columns, experts
    )
    messages = list(messages)
    messages[0], weight_here, gain_here, gate_here = load(
        messages[0], [out_weight, norm_gain.reshape(1, -1), expert_gate]
    )
    pieces = []
    for d in far_first(experts):
        message = swap(messages[d], "expert", d)
        pieces += [message, swap(message, "half", 1)]

    keep, send = project(pieces, weight_here)
    first = expert_up.shape[0] // 256 * 128 + 128
    choose, residual_part, up_first = route(
        pieces, keep, columns, capacity, expert_ids.shape[1], expert_up, first
    )
    *packed, own, cross = pack(keep, swap(send, "pair", 1), residual_part, choose, experts)

    packed[2:] = [relay(rows, packed[1]) for rows in packed[2:]]
    arrived = [swap(rows, "expert", d) for d, rows in enumerate(packed)]
    near = [jnp.concatenate(arrived[d : d + 2], axis=0) for d in range(0, experts, 2)]
    far = [swap(rows, "pair", 1) for rows in near]
    near_cross = [swap(rows, "half", 1) for rows in near]
    *sums, up_rest = expert_first(
        [near[0], near_cross[0], far[0], swap(far[0], "half", 1)],
        gain_here, gate_here, up_first, expert_up, count,
    )
    cross = swap(cross, "half", 1)
    far[1] = relay(far[1], sums[2], cross)
    hidden, down_here = expert_second(
        [near[1], near_cross[1], far[1], swap(far[1], "half", 1)],
        gain_here, gate_here, up_first, up_rest, sums, expert_down_part, count,
    )

    width = residual.shape[1] // 2
    mine, got = [], []
    for g in range(2):
        terms, send = expert_down(hidden, down_here, g * width, width, count)
        mine.append(terms)
        got.append(swap(send, "half", 1))
    keep, send = chip_sum(mine, got)
    own = cut(own, cross, keep, experts)
    own = [swap(own[d], "expert", d) for d in far_first(experts)]
    terms = pair_sum(keep, swap(send, "pair", 1), capacity, experts, own)
    combined, weighting = own_rows(ids, weights, residual, own, capacity)
    back = [swap(terms[d], "expert", d) for d in far_first(experts)]
    return finish(combined, weighting, back)


def plain_attend(queries, key_rows, value_rows, states, decay_rates, head_gain):
    requests = states.shape[0]
    head_count = states.shape[1]
    head_size = states.shape[2]
    positions = queries.shape[0] // requests
    layout = (requests, positions, head_count, head_size)
    query_plain = queries.reshape(layout)
    key_plain = key_rows.reshape(layout)
    query_float = query_plain.astype(jnp.float32)
    value_float = value_rows.reshape(layout).astype(jnp.float32)
    offsets = jnp.arange(positions, dtype=jnp.float32)
    carried = jnp.exp(-decay_rates[None, :] * (offsets[:, None] + 1.0))
    from_state = jnp.einsum("rphk,rhkv->rphv", query_float, states, precision=HIGHEST)
    from_state = from_state * carried[None, :, :, None]
    scores = jnp.einsum(
        "rthk,rjhk->rhtj", query_plain, key_plain, preferred_element_type=jnp.float32
    )
    distance = offsets[:, None] - offsets[None, :]
    fading = jnp.exp(-decay_rates[:, None, None] * jnp.maximum(distance, 0.0)[None, :, :])
    fading = jnp.where(distance[None, :, :] >= 0.0, fading, 0.0)
    scores = scores * fading[None]
    within = jnp.einsum("rhtj,rjhv->rthv", scores, value_float, precision=HIGHEST)
    mixed_heads = from_state + within
    spread = jnp.mean(mixed_heads * mixed_heads, axis=3, keepdims=True)
    normal = (
        mixed_heads
        * lax.rsqrt(spread + EPSILON)
        * head_gain.reshape(head_count, head_size)[None, None]
    )
    return normal.astype(jnp.bfloat16).reshape(requests * positions, head_count * head_size)


def plain_experts(picked, gate_part, up_part, down_part):
    leading = picked.shape
    flattened = picked.reshape(-1, leading[-1])
    contract = (((1,), (1,)), ((), ()))
    gate_value = lax.dot_general(flattened, gate_part, contract, preferred_element_type=jnp.float32)
    lifted = lax.dot_general(flattened, up_part, contract, preferred_element_type=jnp.float32)
    hidden = (jax.nn.silu(gate_value) * lifted).astype(jnp.bfloat16)
    output = jnp.dot(hidden, down_part, preferred_element_type=jnp.float32)
    return output.reshape(leading)


def plain(
    queries,
    key_rows,
    value_rows,
    states,
    decay_rates,
    head_gain,
    out_weight,
    residual,
    norm_gain,
    expert_ids,
    gate_weights,
    expert_gate,
    expert_up,
    expert_down,
):
    outer_count = lax.axis_size("dev")
    pair_count = lax.axis_size("pair")
    core_count = lax.axis_size("sub")
    attended = plain_attend(queries, key_rows, value_rows, states, decay_rates, head_gain)
    partial_value = jnp.dot(
        lax.all_gather(attended, ("dev", "sub"), axis=0, tiled=True),
        out_weight,
        preferred_element_type=jnp.float32,
    )
    local_rows = residual.shape[0]
    columns = partial_value.shape[1]
    blocks = partial_value.reshape(outer_count, pair_count, core_count, local_rows, columns)
    ordered = jnp.transpose(blocks, (1, 0, 2, 3, 4)).reshape(
        pair_count, outer_count * core_count * local_rows, columns
    )
    shared = lax.psum_scatter(ordered, "pair", scatter_dimension=0, tiled=True)
    shared = shared.reshape(outer_count * core_count, local_rows, columns)
    regrouped = lax.all_to_all(shared, ("dev", "sub"), split_axis=0, concat_axis=2, tiled=True)
    own_rows = regrouped[0]
    combined = residual.astype(jnp.float32) + own_rows
    spread = jnp.mean(combined * combined, axis=-1, keepdims=True)
    normed = (combined * lax.rsqrt(spread + EPSILON) * norm_gain).astype(jnp.bfloat16)
    width = normed.shape[1]
    top_count = expert_ids.shape[1]
    expert_count = outer_count // 2
    capacity = max(2, local_rows * top_count // expert_count)
    chosen_ids = expert_ids.reshape(-1)
    choose = (chosen_ids[:, None] == jnp.arange(expert_count, dtype=jnp.int32)[None, :]).astype(
        jnp.int32
    )
    before = jnp.cumsum(choose, axis=0) - choose
    position = jnp.sum(before * choose, axis=1)
    target = chosen_ids * capacity + position
    placing = (
        target[None, :] == jnp.arange(expert_count * capacity, dtype=jnp.int32)[:, None]
    ).astype(jnp.bfloat16)
    repeated = jnp.repeat(normed, top_count, axis=0)
    packed = jnp.dot(placing, repeated, preferred_element_type=jnp.float32).astype(jnp.bfloat16)
    slot_rows = packed.reshape(expert_count, 1, capacity, width)
    outgoing = jnp.broadcast_to(slot_rows, (expert_count, 2, capacity, width)).reshape(
        outer_count, capacity, width
    )
    partials = plain_experts(
        lax.all_gather(
            lax.all_to_all(outgoing, "dev", split_axis=0, concat_axis=0, tiled=True)[None],
            ("pair", "sub"),
            axis=0,
            tiled=True,
        ),
        expert_gate,
        expert_up,
        expert_down,
    )
    summed_terms = lax.psum_scatter(partials, ("pair", "sub"), scatter_dimension=0, tiled=True)
    returned = lax.all_to_all(summed_terms[0], "dev", split_axis=0, concat_axis=0, tiled=True)
    halves = jnp.sum(returned.reshape(expert_count, -1, capacity, width), axis=1).reshape(
        expert_count * capacity, width
    )
    weighting = placing.astype(jnp.float32) * gate_weights.reshape(-1)[None, :]
    per_slot = lax.dot_general(
        weighting,
        halves,
        (((0,), (0,)), ((), ())),
        precision=HIGHEST,
        preferred_element_type=jnp.float32,
    )
    mixture = jnp.sum(per_slot.reshape(local_rows, top_count, width), axis=1)
    return (combined + mixture).astype(jnp.bfloat16)


def solution(mesh):
    sizes = dict(mesh.shape)
    plain_axes = (("dev",), ("pair", "sub"), ("sub",))
    chip_axes = (("expert", "half"), ("pair",), ())

    def specs(dev, inner, sub):
        requests = P(("grp",) + dev + sub, "pair")
        tokens = P(("grp",) + dev + inner, None)
        units = P(dev + inner, None)
        arguments = (
            requests,
            requests,
            requests,
            P(("grp",) + dev + sub, "pair", None, None),
            P("pair"),
            P("pair"),
            P("pair", dev + sub),
            tokens,
            P(),
            tokens,
            tokens,
            units,
            units,
            units,
        )
        return dict(in_specs=arguments, out_specs=tokens, check_vma=False)

    experts = sizes["dev"] // 2
    chips = sizes["pair"] == 2 and sizes["sub"] == 1 and experts == 4

    def run(*arguments):
        rows = arguments[7].shape[0] // mesh.size
        columns = arguments[6].shape[1] // (sizes["dev"] * sizes["sub"])
        units = arguments[11].shape[0] * sizes["grp"] // mesh.size
        if chips and rows == 8 and columns % 128 == 0 and units % 384 == 0:
            cut = Mesh(
                mesh.devices.reshape(sizes["grp"], experts, 2, 2),
                ("grp", "expert", "half", "pair"),
            )
            return jax.shard_map(on_chips, mesh=cut, **specs(*chip_axes))(*arguments)
        return jax.shard_map(plain, mesh=mesh, **specs(*plain_axes))(*arguments)

    return run
```

```python
import functools

import jax
import jax.numpy as jnp
from jax import lax
from jax.experimental import pallas as pl
from jax.experimental.pallas import tpu as pltpu
from jax.sharding import Mesh
from jax.sharding import PartitionSpec as P

EPSILON = 1e-06
F32 = jnp.float32
BF16 = jnp.bfloat16
MIB = 1 << 20
ID_LANES = 128
HIGHEST = lax.Precision.HIGHEST
VMEM = pl.BlockSpec(memory_space=pltpu.VMEM)
SMEM = pl.BlockSpec(memory_space=pltpu.SMEM)
ANY = pl.BlockSpec(memory_space=pl.ANY)


def in_hbm(*arrays):
    return [pltpu.with_memory_space_constraint(a, pltpu.HBM) for a in arrays]


def limits(mib):
    return pltpu.CompilerParams(vmem_limit_bytes=mib * MIB)


def far_first(count):
    return [-d % count for d in range(count)]


def dot(a, b):
    return jnp.dot(a, b, preferred_element_type=F32)


def dot_t(a, b):
    return lax.dot_general(a, b, (((1,), (1,)), ((), ())), preferred_element_type=F32)


def halves_of(x):
    high = x.astype(BF16)
    return high, (x - high.astype(F32)).astype(BF16)


def attend_kernel(positions, steps, decay_ref, ids_ref, q_ref, k_ref, v_ref, gain_ref, s_ref, residual_ref, *refs):
    outs = refs
    requests, heads, size, _ = s_ref.shape
    rows = q_ref.shape[0]
    step = pl.program_id(0)
    first = step * heads
    @pl.when(step == 0)
    def _():
        width = steps * heads * size
        lanes = ID_LANES
        row = lax.broadcasted_iota(jnp.int32, (rows, lanes), 0)
        lane = lax.broadcasted_iota(jnp.int32, (rows, lanes), 1)
        ids = jnp.zeros((rows, lanes), jnp.int32)
        for k in range(ids_ref.shape[0]):
            for t in range(ids_ref.shape[1]):
                ids = jnp.where((row == t) & (lane == k), ids_ref[k, t], ids)
        ids = ids.astype(F32).astype(BF16)
        columns = outs[0].shape[1] - width - lanes
        expert = lax.axis_index("expert")
        for d, out in enumerate(outs):
            out[:, width : width + lanes] = ids
            base = (expert ^ d) * 2 * columns
            both = [
                residual_ref[:, pl.ds(pl.multiple_of(base + h * columns, columns), columns)]
                for h in range(2)
            ]
            both = jnp.concatenate([b.astype(F32) for b in both], axis=0)
            out[:, width + lanes :] = both.astype(BF16)

    row = lax.broadcasted_iota(jnp.int32, (rows, rows), 0)
    col = lax.broadcasted_iota(jnp.int32, (rows, rows), 1)
    seen = (row // positions == col // positions) & (row >= col)
    distance = jnp.maximum(row - col, 0).astype(F32)
    owner = lax.broadcasted_iota(jnp.int32, (rows, size), 0)
    age = (owner % positions + 1).astype(F32)
    of_request = [
        jnp.where(owner // positions == r, 1.0, 0.0).astype(BF16) for r in range(requests)
    ]
    for i in range(heads):
        rate = decay_ref[first + i]
        at = slice(i * size, (i + 1) * size)
        q = q_ref[:, at]
        spread_q = jnp.concatenate([q * mask for mask in of_request], axis=1)
        high, low = halves_of(s_ref[:, i].reshape(requests * size, size))
        from_state = (dot(spread_q, high) + dot(spread_q, low)) * jnp.exp(-rate * age)
        scores = jnp.where(seen, dot_t(q, k_ref[:, at]) * jnp.exp(-rate * distance), 0.0)
        score_high, score_low = halves_of(scores)
        v = v_ref[:, at]
        mixed = from_state + dot(score_high, v) + dot(score_low, v)
        spread = jnp.mean(mixed * mixed, axis=1, keepdims=True)
        normal = mixed * lax.rsqrt(spread + EPSILON) * gain_ref[:, at]
        normal = normal.astype(BF16)
        for out in outs:
            out[:, pl.ds(pl.multiple_of((first + i) * size, size), size)] = normal


def attend(
    queries, key_rows, value_rows, states, decay_rates, head_gain, ids, residual, columns, experts
):
    requests, heads, size, _ = states.shape
    rows = queries.shape[0]
    step = 8 if heads % 8 == 0 else 1
    wide = pl.BlockSpec((rows, step * size), lambda i: (0, i))
    message = (rows, queries.shape[1] + ID_LANES + columns)
    return pl.pallas_call(
        functools.partial(attend_kernel, rows // requests, heads // step),
        grid=(heads // step,),
        in_specs=[
            SMEM,
            SMEM,
            wide,
            wide,
            wide,
            pl.BlockSpec((1, step * size), lambda i: (0, i)),
            pl.BlockSpec((requests, step, size, size), lambda i: (0, i, 0, 0)),
            pl.BlockSpec(residual.shape, lambda i: (0, 0)),
        ],
        out_specs=[pl.BlockSpec(message, lambda i: (0, 0))] * experts,
        out_shape=[jax.ShapeDtypeStruct(message, BF16)] * experts,
        compiler_params=limits(16),
        name="attention",
    )(
        *in_hbm(
            decay_rates, ids, queries, key_rows, value_rows, head_gain.reshape(1, -1), states, residual,
        )
    )


def load_kernel(count, rows_hbm, *refs):
    sources, rows_ref, targets, sem = refs[:count], refs[count], refs[count + 1 : -1], refs[-1]
    copies = [
        pltpu.make_async_copy(source, target, sem.at[i])
        for i, (source, target) in enumerate(zip(sources, targets))
    ]
    copies.append(pltpu.make_async_copy(rows_hbm, rows_ref, sem.at[count]))
    for copy in copies:
        copy.start()
    for copy in copies:
        copy.wait()


def load(rows, weights):
    size = sum(w.size * w.dtype.itemsize for w in weights)
    return pl.pallas_call(
        functools.partial(load_kernel, len(weights)),
        in_specs=[ANY] * (1 + len(weights)),
        out_specs=[VMEM] * (1 + len(weights)),
        out_shape=[jax.ShapeDtypeStruct(rows.shape, rows.dtype)]
        + [pltpu.VMEM(w.shape, w.dtype) for w in weights],
        scratch_shapes=[pltpu.SemaphoreType.DMA((1 + len(weights),))],
        compiler_params=limits(1),
        cost_estimate=pl.CostEstimate(flops=0, bytes_accessed=size, transcendentals=0),
        name="load",
    )(rows, *in_hbm(*weights))


def project_kernel(*refs):
    pieces, weight_ref, keep_ref, send_ref, x_ref, product_ref = refs[:-5], *refs[-5:]
    depth = weight_ref.shape[0]
    rows = pieces[0].shape[0]
    expert, half, pair = lax.axis_index("expert"), lax.axis_index("half"), lax.axis_index("pair")
    for j, piece in enumerate(pieces):
        base = (expert ^ far_first(len(pieces) // 2)[j // 2]) * 2 + (half ^ (j % 2))
        x_ref[pl.ds(pl.multiple_of(base * rows, rows), rows)] = piece[:, :depth]
    product_ref[...] = dot(x_ref[...], weight_ref[...])
    own = rows // 2
    for b in range(len(pieces)):
        mine = pl.ds(pl.multiple_of(b * rows + pair * own, own), own)
        keep_ref[b * own : (b + 1) * own] = product_ref[mine]
    for b in range(0, len(pieces), 2):
        theirs = [
            product_ref[pl.ds(pl.multiple_of(c * rows + (1 - pair) * own, own), own)]
            for c in (b, b + 1)
        ]
        send_ref[b * own : (b + 2) * own] = jnp.concatenate(theirs, axis=0).astype(BF16)


def project(pieces, weight):
    rows = pieces[0].shape[0] * len(pieces)
    depth, columns = weight.shape
    return pl.pallas_call(
        project_kernel,
        in_specs=[VMEM] * (len(pieces) + 1),
        out_specs=[VMEM] * 2,
        out_shape=[
            jax.ShapeDtypeStruct((rows // 2, columns), F32),
            jax.ShapeDtypeStruct((rows // 2, columns), BF16),
        ],
        scratch_shapes=[pltpu.VMEM((rows, depth), BF16), pltpu.VMEM((rows, columns), F32)],
        compiler_params=limits(8),
        name="projection",
    )(*pieces, weight)


def route_kernel(capacity, top, *refs):
    pieces, weight_hbm = refs[:-7], refs[-6]
    choose_ref, residual_ref, weight_ref, ids_ref, sem = refs[-5:]
    copy = pltpu.make_async_copy(weight_hbm.at[: weight_ref.shape[0]], weight_ref, sem)
    copy.start()
    columns = residual_ref.shape[1]
    own = pieces[0].shape[0] // 2
    rows = ids_ref.shape[0]
    experts = len(pieces) // 2
    expert, half = lax.axis_index("expert"), lax.axis_index("half")
    for j, piece in enumerate(pieces):
        base = (expert ^ far_first(len(pieces) // 2)[j // 2]) * 2 + (half ^ (j % 2))
        at = pl.ds(pl.multiple_of(base * own, own), own)
        last = piece.shape[1] - columns
        both = piece[:, last:].astype(F32)
        residual_ref[at] = jnp.where(half == 0, both[:own], both[own:])
        ids_ref[at] = piece[:, last - ID_LANES : last].astype(F32)[:own]
    ids = ids_ref[...].T
    line = lax.broadcasted_iota(jnp.int32, (8, rows), 0)
    wanted = jnp.bitwise_xor(line, expert).astype(F32)
    named = jnp.zeros((8, rows), F32)
    for k in range(top):
        named = named + jnp.where(ids[k : k + 1] == wanted, 1.0, 0.0)
    before = lax.broadcasted_iota(jnp.int32, (rows, rows), 0)
    after = lax.broadcasted_iota(jnp.int32, (rows, rows), 1)
    earlier = jnp.where((before // own == after // own) & (before < after), 1.0, 0.0)
    rank = dot(named.astype(BF16), earlier.astype(BF16))
    dev = lax.broadcasted_iota(jnp.int32, (8, rows), 1) // own
    place = (dev % 2 * experts + dev // 2) * capacity
    place = jnp.where(named > 0.5, place.astype(F32) + rank, -1.0)
    count = choose_ref.shape[0] // experts
    slot = lax.broadcasted_iota(jnp.int32, (count, rows), 0).astype(F32)
    for d in range(experts):
        choose_ref[d * count : (d + 1) * count] = jnp.where(
            slot == place[d : d + 1], 1.0, 0.0
        ).astype(BF16)
    copy.wait()


def route(pieces, after, columns, capacity, top, weight, first):
    rows = pieces[0].shape[0] // 2 * len(pieces)
    experts = len(pieces) // 2
    return pl.pallas_call(
        functools.partial(route_kernel, capacity, top),
        in_specs=[VMEM] * len(pieces) + [ANY] * 2,
        out_specs=[VMEM] * 3,
        out_shape=[
            jax.ShapeDtypeStruct((experts * 2 * experts * capacity, rows), BF16),
            jax.ShapeDtypeStruct((rows, columns), F32),
            pltpu.VMEM((first, weight.shape[1]), weight.dtype),
        ],
        scratch_shapes=[pltpu.VMEM((rows, ID_LANES), F32), pltpu.SemaphoreType.DMA],
        compiler_params=limits(4),
        cost_estimate=pl.CostEstimate(flops=10**6, bytes_accessed=8 * 10**6, transcendentals=0),
        name="route",
    )(*pieces, after, *in_hbm(weight))


def pack_kernel(keep_ref, got_ref, residual_ref, choose_ref, *refs):
    outs, own_ref, cross_ref, sum_ref = refs[:-3], *refs[-3:]
    sum_ref[...] = keep_ref[...] + got_ref[...].astype(F32)
    combined = (sum_ref[...] + residual_ref[...]).astype(BF16)
    packed = dot(choose_ref[...], combined).astype(BF16)
    count = choose_ref.shape[0] // len(outs)
    own = sum_ref.shape[0] // len(outs) // 2
    expert, half = lax.axis_index("expert"), lax.axis_index("half")
    for d, out in enumerate(outs):
        out[...] = packed[d * count : (d + 1) * count]
    for d in range(0, len(outs), 2):
        for ref, which in ((own_ref, half), (cross_ref, 1 - half)):
            rows = [
                sum_ref[pl.ds(pl.multiple_of(((expert ^ c) * 2 + which) * own, own), own)]
                for c in (d, d + 1)
            ]
            ref[d * own : (d + 2) * own] = jnp.concatenate(rows, axis=0).astype(BF16)


def pack(keep, got, residual, choose, experts):
    rows, columns = keep.shape
    count = choose.shape[0] // experts
    return pl.pallas_call(
        pack_kernel,
        in_specs=[VMEM] * 4,
        out_specs=[VMEM] * (experts + 2),
        out_shape=[jax.ShapeDtypeStruct((count, columns), BF16)] * experts
        + [jax.ShapeDtypeStruct((rows // 2, columns), BF16)] * 2,
        scratch_shapes=[pltpu.VMEM((rows, columns), F32)],
        compiler_params=limits(4),
        name="pack",
    )(keep, got, residual, choose)


def turn(turned_ref, gain_ref, pieces, first, count):
    near, near_cross, far, far_cross = pieces
    columns = near.shape[1]
    expert, half = lax.axis_index("expert"), lax.axis_index("half")
    squares = jnp.zeros((2 * count, 128), F32)
    for d in range(2):
        for c, (mine, theirs) in enumerate(((near, far), (near_cross, far_cross))):
            rows = slice(d * count, (d + 1) * count)
            x = jnp.concatenate([mine[rows].astype(F32), theirs[rows].astype(F32)], axis=0)
            for b in range(columns // 128):
                part = x[:, b * 128 : (b + 1) * 128]
                squares = squares + part * part
            block = (expert ^ (first + d)) * 2 + (half ^ c)
            at = pl.ds(pl.multiple_of(block * columns, columns), columns)
            to = pl.ds(pl.multiple_of(block % 4 * columns, columns), columns)
            turned_ref[to] = (x * gain_ref[:, at]).astype(BF16).T
    return squares


def half_of(ref, first):
    width = ref.shape[1] // 2
    which = (lax.axis_index("expert") ^ first) // 2
    return pl.ds(pl.multiple_of(which * width, width), width)


def expert_first_kernel(count, *refs):
    pieces, gain_ref, gate_ref, up_ref, up_hbm = refs[:4], *refs[4:8]
    gate_sum_ref, up_sum_ref, squares_ref, up_rest_ref, turned_ref, sem = refs[8:]
    cut = up_ref.shape[0]
    rest = pltpu.make_async_copy(up_hbm.at[cut:], up_rest_ref, sem)
    rest.start()
    squares_ref[...] = turn(turned_ref, gain_ref, pieces, 0, count)
    columns = half_of(gate_ref, 0)
    rest.wait()
    for at, weight_ref in ((slice(0, cut), up_ref), (slice(cut, gate_ref.shape[0]), up_rest_ref)):
        gate_sum_ref[at] = dot(gate_ref[at, columns], turned_ref[...])
        up_sum_ref[at] = dot(weight_ref[:, columns], turned_ref[...])


def expert_second_kernel(count, *refs):
    pieces, gain_ref, gate_ref, up_ref, up_rest_ref = refs[:4], *refs[4:8]
    gate_sum_ref, up_sum_ref, squares_ref, down_hbm, hidden_ref, down_ref = refs[8:14]
    turned_ref, gate_value_ref, sem = refs[14:]
    units, width = gate_ref.shape
    cut = up_ref.shape[0]
    down = pltpu.make_async_copy(down_hbm, down_ref, sem)
    down.start()
    squares = squares_ref[...] + turn(turned_ref, gain_ref, pieces, 2, count)
    spread = jnp.sum(squares.T, axis=0, keepdims=True) / width
    scale = lax.rsqrt(spread + EPSILON)
    columns = half_of(gate_ref, 2)
    gate_value_ref[...] = (gate_sum_ref[...] + dot(gate_ref[:, columns], turned_ref[...])) * scale
    for at, weight_ref in ((slice(0, cut), up_ref), (slice(cut, units), up_rest_ref)):
        gate_value = gate_value_ref[at]
        lifted = (up_sum_ref[at] + dot(weight_ref[:, columns], turned_ref[...])) * scale
        hidden = gate_value / (1.0 + jnp.exp(-gate_value)) * lifted
        hidden_ref[:, at] = hidden.T.astype(BF16)
    down.wait()


def down_kernel(start, wide, hidden_ref, weight_ref, keep_ref, send_ref):
    half = lax.axis_index("half")
    count = keep_ref.shape[0]
    part = count // 2
    for n in range(keep_ref.shape[1] // wide):
        at = slice(start + n * wide, start + (n + 1) * wide)
        out = slice(n * wide, (n + 1) * wide)
        total = dot(hidden_ref[...], weight_ref[:, at])
        for p in range(2):
            low = total[p * count : p * count + part]
            high = total[p * count + part : (p + 1) * count]
            to = slice(p * part, (p + 1) * part)
            keep_ref[to, out] = jnp.where(half == 0, low, high)
            send_ref[to, out] = jnp.where(half == 0, high, low).astype(BF16)


def cost(flops, size):
    return pl.CostEstimate(flops=flops, bytes_accessed=size, transcendentals=0)


def expert_first(pieces, gain, gate, up_first, up_part, count):
    units, width = gate.shape
    cut = up_first.shape[0]
    sums = jax.ShapeDtypeStruct((units, 2 * count), F32)
    return pl.pallas_call(
        functools.partial(expert_first_kernel, count),
        in_specs=[VMEM] * 7 + [ANY],
        out_specs=[VMEM] * 4,
        out_shape=[
            sums,
            sums,
            jax.ShapeDtypeStruct((2 * count, 128), F32),
            pltpu.VMEM((units - cut, width), BF16),
        ],
        scratch_shapes=[pltpu.VMEM((width // 2, 2 * count), BF16), pltpu.SemaphoreType.DMA],
        compiler_params=limits(8),
        cost_estimate=cost(4 * units * width * count, 2 * units * width),
        name="experts_first",
    )(*pieces, gain, gate, up_first, *in_hbm(up_part))


def relay_kernel(rows_ref, *refs):
    refs[-1][...] = rows_ref[...]


def relay(rows, *after):
    return pl.pallas_call(
        relay_kernel,
        in_specs=[VMEM] * (1 + len(after)),
        out_specs=VMEM,
        out_shape=jax.ShapeDtypeStruct(rows.shape, rows.dtype),
        compiler_params=limits(2),
        cost_estimate=cost(0, 10**5),
        name="relay",
    )(rows, *after)


def expert_second(pieces, gain, gate, up_first, up_rest, sums, down_part, count):
    units, width = gate.shape
    return pl.pallas_call(
        functools.partial(expert_second_kernel, count),
        in_specs=[VMEM] * 11 + [ANY],
        out_specs=[VMEM] * 2,
        out_shape=[
            jax.ShapeDtypeStruct((2 * count, units), BF16),
            pltpu.VMEM((units, width), BF16),
        ],
        scratch_shapes=[
            pltpu.VMEM((width // 2, 2 * count), BF16),
            pltpu.VMEM((units, 2 * count), F32),
            pltpu.SemaphoreType.DMA,
        ],
        compiler_params=limits(8),
        cost_estimate=cost(4 * units * width * count, 2 * units * width),
        name="experts_second",
    )(*pieces, gain, gate, up_first, up_rest, *sums, *in_hbm(down_part))


def expert_down(hidden, weight, start, width, count):
    return pl.pallas_call(
        functools.partial(down_kernel, start, 512),
        in_specs=[VMEM] * 2,
        out_specs=[VMEM] * 2,
        out_shape=[
            jax.ShapeDtypeStruct((count, width), F32),
            jax.ShapeDtypeStruct((count, width), BF16),
        ],
        compiler_params=limits(8),
        cost_estimate=cost(4 * hidden.size * width, 2 * hidden.shape[1] * width),
        name="experts_down",
    )(hidden, weight)


def chip_sum_kernel(count, *refs):
    mine, got = refs[:count], refs[count : 2 * count]
    keep_ref, send_ref = refs[2 * count :]
    rows = keep_ref.shape[0]
    width = mine[0].shape[1]
    for g in range(count):
        at = slice(g * width, (g + 1) * width)
        keep_ref[:, at] = mine[g][:rows] + got[g][:rows].astype(F32)
        send_ref[:, at] = (mine[g][rows:] + got[g][rows:].astype(F32)).astype(BF16)


def chip_sum(mine, got):
    rows, width = mine[0].shape
    shape = (rows // 2, width * len(mine))
    return pl.pallas_call(
        functools.partial(chip_sum_kernel, len(mine)),
        in_specs=[VMEM] * (2 * len(mine)),
        out_specs=[VMEM] * 2,
        out_shape=[jax.ShapeDtypeStruct(shape, F32), jax.ShapeDtypeStruct(shape, BF16)],
        compiler_params=limits(4),
        name="chip_sum",
    )(*mine, *got)


def cut_kernel(own_ref, cross_ref, after_ref, *outs):
    rows = own_ref.shape[0] // len(outs)
    own, cross = own_ref[...].astype(F32), cross_ref[...].astype(F32)
    for d, out in enumerate(outs):
        at = slice(d * rows, (d + 1) * rows)
        out[...] = jnp.concatenate([own[at], cross[at]], axis=0).astype(BF16)


def cut(own, cross, after, experts):
    rows, columns = own.shape
    return pl.pallas_call(
        cut_kernel,
        in_specs=[VMEM] * 3,
        out_specs=[VMEM] * experts,
        out_shape=[jax.ShapeDtypeStruct((2 * rows // experts, columns), BF16)] * experts,
        compiler_params=limits(2),
        cost_estimate=cost(0, 10**5),
        name="cut",
    )(own, cross, after)


def pair_sum_kernel(capacity, extra, keep_ref, got_ref, *refs):
    outs, fold_ref = refs[extra:-1], refs[-1]
    experts = len(outs)
    parts = 8 // capacity
    part = outs[0].shape[1]
    total = keep_ref[...] + got_ref[...].astype(F32)
    for e in range(experts):
        mine = total[e * capacity : (e + 1) * capacity]
        fold_ref[e] = jnp.concatenate(
            [mine[:, h * part : (h + 1) * part] for h in range(parts)], axis=0
        )
    expert = lax.axis_index("expert")
    for d, out in enumerate(outs):
        out[...] = fold_ref[expert ^ d].astype(BF16)


def pair_sum(keep, got, capacity, experts, after):
    part = keep.shape[1] * capacity // 8
    return pl.pallas_call(
        functools.partial(pair_sum_kernel, capacity, len(after)),
        in_specs=[VMEM] * (2 + len(after)),
        out_specs=[VMEM] * experts,
        out_shape=[jax.ShapeDtypeStruct((8, part), BF16)] * experts,
        scratch_shapes=[pltpu.VMEM((experts, 8, part), F32)],
        compiler_params=limits(4),
        name="pair_sum",
    )(keep, got, *after)


def own_rows_kernel(capacity, own_ids_ref, weights_ref, residual_ref, *refs):
    pieces, combined_ref, weighting_ref = refs[:-2], *refs[-2:]
    rows = combined_ref.shape[0]
    top, own_count = own_ids_ref.shape
    columns = pieces[0].shape[1]
    expert, half = lax.axis_index("expert"), lax.axis_index("half")
    for d, piece in zip(far_first(len(pieces)), pieces):
        both = piece[...].astype(F32)
        for c in range(2):
            base = ((expert ^ d) * 2 + (half ^ c)) * columns
            at = pl.ds(pl.multiple_of(base, columns), columns)
            combined_ref[:, at] = residual_ref[:, at].astype(F32) + both[c * rows : (c + 1) * rows]

    places = weighting_ref.shape[1]
    row = lax.broadcasted_iota(jnp.int32, (own_count, places), 0)
    at_place = lax.broadcasted_iota(jnp.int32, (own_count, places), 1)
    slot = at_place // 8 * capacity + at_place % capacity
    weighting = jnp.zeros((own_count, places), F32)
    order = [(t, k) for t in range(own_count) for k in range(top)]
    named = [own_ids_ref[k, t] for t, k in order]
    for j, (t, k) in enumerate(order):
        rank = jnp.int32(0)
        for i in range(j):
            rank = rank + jnp.where(named[i] == named[j], 1, 0)
        to = (named[j] ^ expert) * capacity + rank
        weighting = jnp.where((slot == to) & (row == t), weights_ref[k, t], weighting)
    for h in range(8 // capacity):
        high, low = halves_of(jnp.where(at_place % 8 // capacity == h, weighting, 0.0))
        both = jnp.concatenate([high.astype(F32), low.astype(F32)], axis=0)
        weighting_ref[h * 16 : (h + 1) * 16] = both.astype(BF16)


def own_rows(ids, weights, residual, pieces, capacity):
    experts = len(pieces)
    return pl.pallas_call(
        functools.partial(own_rows_kernel, capacity),
        in_specs=[SMEM] * 2 + [VMEM] * (len(pieces) + 1),
        out_specs=[VMEM] * 2,
        out_shape=[
            jax.ShapeDtypeStruct(residual.shape, F32),
            jax.ShapeDtypeStruct((16 * (8 // capacity), experts * 8), BF16),
        ],
        compiler_params=limits(4),
        cost_estimate=cost(10**6, 10**6),
        name="own_rows",
    )(*in_hbm(ids, weights, residual), *pieces)


def finish_kernel(combined_ref, weighting_ref, *refs):
    got, out_ref = refs[:-1], refs[-1]
    part = got[0].shape[1]
    rows = combined_ref.shape[0]
    terms = [got[d][...].astype(F32) for d in far_first(len(got))]
    terms = jnp.concatenate(terms, axis=0).astype(BF16)
    for h in range(combined_ref.shape[1] // part):
        at = slice(h * part, (h + 1) * part)
        mixture = dot(weighting_ref[h * 16 : (h + 1) * 16], terms)
        out_ref[:, at] = (combined_ref[:, at] + mixture[:rows] + mixture[rows:]).astype(BF16)


def finish(combined, weighting, got):
    return pl.pallas_call(
        finish_kernel,
        in_specs=[VMEM] * (2 + len(got)),
        out_specs=VMEM,
        out_shape=jax.ShapeDtypeStruct(combined.shape, BF16),
        compiler_params=limits(4),
        name="finish",
    )(combined, weighting, *got)


def swap(x, axis, by):
    return lax.ppermute(x, axis, [(i, i ^ by) for i in range(lax.axis_size(axis))]) if by else x


def on_chips(
    queries,
    key_rows,
    value_rows,
    states,
    decay_rates,
    head_gain,
    out_weight,
    residual,
    norm_gain,
    expert_ids,
    gate_weights,
    expert_gate,
    expert_up,
    expert_down_part,
):
    experts = lax.axis_size("expert")
    local_rows = residual.shape[0]
    columns = out_weight.shape[1]
    top = expert_ids.shape[1]
    capacity = max(2, local_rows * top // experts)
    count = 2 * experts * capacity
    ids, weights = expert_ids.T, gate_weights.T

    messages = attend(
        queries, key_rows, value_rows, states, decay_rates, head_gain, ids, residual, columns, experts
    )
    messages = list(messages)
    messages[0], weight_here, gain_here, gate_here = load(
        messages[0], [out_weight, norm_gain.reshape(1, -1), expert_gate]
    )
    pieces = []
    for d in far_first(experts):
        message = swap(messages[d], "expert", d)
        pieces += [message, swap(message, "half", 1)]

    keep, send = project(pieces, weight_here)
    first = expert_up.shape[0] // 256 * 128 + 128
    choose, residual_part, up_first = route(
        pieces, keep, columns, capacity, expert_ids.shape[1], expert_up, first
    )
    *packed, own, cross = pack(keep, swap(send, "pair", 1), residual_part, choose, experts)

    packed[2:] = [relay(rows, packed[1]) for rows in packed[2:]]
    arrived = [swap(rows, "expert", d) for d, rows in enumerate(packed)]
    near = [jnp.concatenate(arrived[d : d + 2], axis=0) for d in range(0, experts, 2)]
    far = [swap(rows, "pair", 1) for rows in near]
    near_cross = [swap(rows, "half", 1) for rows in near]
    *sums, up_rest = expert_first(
        [near[0], near_cross[0], far[0], swap(far[0], "half", 1)],
        gain_here, gate_here, up_first, expert_up, count,
    )
    cross = swap(cross, "half", 1)
    far[1] = relay(far[1], sums[2], cross)
    hidden, down_here = expert_second(
        [near[1], near_cross[1], far[1], swap(far[1], "half", 1)],
        gain_here, gate_here, up_first, up_rest, sums, expert_down_part, count,
    )

    width = residual.shape[1] // 2
    mine, got = [], []
    for g in range(2):
        terms, send = expert_down(hidden, down_here, g * width, width, count)
        mine.append(terms)
        got.append(swap(send, "half", 1))
    keep, send = chip_sum(mine, got)
    own = cut(own, cross, keep, experts)
    own = [swap(own[d], "expert", d) for d in far_first(experts)]
    terms = pair_sum(keep, swap(send, "pair", 1), capacity, experts, own)
    combined, weighting = own_rows(ids, weights, residual, own, capacity)
    back = [swap(terms[d], "expert", d) for d in far_first(experts)]
    return finish(combined, weighting, back)


def plain_attend(queries, key_rows, value_rows, states, decay_rates, head_gain):
    requests = states.shape[0]
    head_count = states.shape[1]
    head_size = states.shape[2]
    positions = queries.shape[0] // requests
    layout = (requests, positions, head_count, head_size)
    query_plain = queries.reshape(layout)
    key_plain = key_rows.reshape(layout)
    query_float = query_plain.astype(jnp.float32)
    value_float = value_rows.reshape(layout).astype(jnp.float32)
    offsets = jnp.arange(positions, dtype=jnp.float32)
    carried = jnp.exp(-decay_rates[None, :] * (offsets[:, None] + 1.0))
    from_state = jnp.einsum("rphk,rhkv->rphv", query_float, states, precision=HIGHEST)
    from_state = from_state * carried[None, :, :, None]
    scores = jnp.einsum(
        "rthk,rjhk->rhtj", query_plain, key_plain, preferred_element_type=jnp.float32
    )
    distance = offsets[:, None] - offsets[None, :]
    fading = jnp.exp(-decay_rates[:, None, None] * jnp.maximum(distance, 0.0)[None, :, :])
    fading = jnp.where(distance[None, :, :] >= 0.0, fading, 0.0)
    scores = scores * fading[None]
    within = jnp.einsum("rhtj,rjhv->rthv", scores, value_float, precision=HIGHEST)
    mixed_heads = from_state + within
    spread = jnp.mean(mixed_heads * mixed_heads, axis=3, keepdims=True)
    normal = (
        mixed_heads
        * lax.rsqrt(spread + EPSILON)
        * head_gain.reshape(head_count, head_size)[None, None]
    )
    return normal.astype(jnp.bfloat16).reshape(requests * positions, head_count * head_size)


def plain_experts(picked, gate_part, up_part, down_part):
    leading = picked.shape
    flattened = picked.reshape(-1, leading[-1])
    contract = (((1,), (1,)), ((), ()))
    gate_value = lax.dot_general(flattened, gate_part, contract, preferred_element_type=jnp.float32)
    lifted = lax.dot_general(flattened, up_part, contract, preferred_element_type=jnp.float32)
    hidden = (jax.nn.silu(gate_value) * lifted).astype(jnp.bfloat16)
    output = jnp.dot(hidden, down_part, preferred_element_type=jnp.float32)
    return output.reshape(leading)


def plain(
    queries,
    key_rows,
    value_rows,
    states,
    decay_rates,
    head_gain,
    out_weight,
    residual,
    norm_gain,
    expert_ids,
    gate_weights,
    expert_gate,
    expert_up,
    expert_down,
):
    outer_count = lax.axis_size("dev")
    pair_count = lax.axis_size("pair")
    core_count = lax.axis_size("sub")
    attended = plain_attend(queries, key_rows, value_rows, states, decay_rates, head_gain)
    partial_value = jnp.dot(
        lax.all_gather(attended, ("dev", "sub"), axis=0, tiled=True),
        out_weight,
        preferred_element_type=jnp.float32,
    )
    local_rows = residual.shape[0]
    columns = partial_value.shape[1]
    blocks = partial_value.reshape(outer_count, pair_count, core_count, local_rows, columns)
    ordered = jnp.transpose(blocks, (1, 0, 2, 3, 4)).reshape(
        pair_count, outer_count * core_count * local_rows, columns
    )
    shared = lax.psum_scatter(ordered, "pair", scatter_dimension=0, tiled=True)
    shared = shared.reshape(outer_count * core_count, local_rows, columns)
    regrouped = lax.all_to_all(shared, ("dev", "sub"), split_axis=0, concat_axis=2, tiled=True)
    own_rows = regrouped[0]
    combined = residual.astype(jnp.float32) + own_rows
    spread = jnp.mean(combined * combined, axis=-1, keepdims=True)
    normed = (combined * lax.rsqrt(spread + EPSILON) * norm_gain).astype(jnp.bfloat16)
    width = normed.shape[1]
    top_count = expert_ids.shape[1]
    expert_count = outer_count // 2
    capacity = max(2, local_rows * top_count // expert_count)
    chosen_ids = expert_ids.reshape(-1)
    choose = (chosen_ids[:, None] == jnp.arange(expert_count, dtype=jnp.int32)[None, :]).astype(
        jnp.int32
    )
    before = jnp.cumsum(choose, axis=0) - choose
    position = jnp.sum(before * choose, axis=1)
    target = chosen_ids * capacity + position
    placing = (
        target[None, :] == jnp.arange(expert_count * capacity, dtype=jnp.int32)[:, None]
    ).astype(jnp.bfloat16)
    repeated = jnp.repeat(normed, top_count, axis=0)
    packed = jnp.dot(placing, repeated, preferred_element_type=jnp.float32).astype(jnp.bfloat16)
    slot_rows = packed.reshape(expert_count, 1, capacity, width)
    outgoing = jnp.broadcast_to(slot_rows, (expert_count, 2, capacity, width)).reshape(
        outer_count, capacity, width
    )
    partials = plain_experts(
        lax.all_gather(
            lax.all_to_all(outgoing, "dev", split_axis=0, concat_axis=0, tiled=True)[None],
            ("pair", "sub"),
            axis=0,
            tiled=True,
        ),
        expert_gate,
        expert_up,
        expert_down,
    )
    summed_terms = lax.psum_scatter(partials, ("pair", "sub"), scatter_dimension=0, tiled=True)
    returned = lax.all_to_all(summed_terms[0], "dev", split_axis=0, concat_axis=0, tiled=True)
    halves = jnp.sum(returned.reshape(expert_count, -1, capacity, width), axis=1).reshape(
        expert_count * capacity, width
    )
    weighting = placing.astype(jnp.float32) * gate_weights.reshape(-1)[None, :]
    per_slot = lax.dot_general(
        weighting,
        halves,
        (((0,), (0,)), ((), ())),
        precision=HIGHEST,
        preferred_element_type=jnp.float32,
    )
    mixture = jnp.sum(per_slot.reshape(local_rows, top_count, width), axis=1)
    return (combined + mixture).astype(jnp.bfloat16)


def solution(mesh):
    sizes = dict(mesh.shape)
    plain_axes = (("dev",), ("pair", "sub"), ("sub",))
    chip_axes = (("expert", "half"), ("pair",), ())

    def specs(dev, inner, sub):
        requests = P(("grp",) + dev + sub, "pair")
        tokens = P(("grp",) + dev + inner, None)
        units = P(dev + inner, None)
        arguments = (
            requests,
            requests,
            requests,
            P(("grp",) + dev + sub, "pair", None, None),
            P("pair"),
            P("pair"),
            P("pair", dev + sub),
            tokens,
            P(),
            tokens,
            tokens,
            units,
            units,
            units,
        )
        return dict(in_specs=arguments, out_specs=tokens, check_vma=False)

    experts = sizes["dev"] // 2
    chips = sizes["pair"] == 2 and sizes["sub"] == 1 and experts == 4

    def run(*arguments):
        rows = arguments[7].shape[0] // mesh.size
        columns = arguments[6].shape[1] // (sizes["dev"] * sizes["sub"])
        units = arguments[11].shape[0] * sizes["grp"] // mesh.size
        if chips and rows == 8 and columns % 128 == 0 and units % 384 == 0:
            cut = Mesh(
                mesh.devices.reshape(sizes["grp"], experts, 2, 2),
                ("grp", "expert", "half", "pair"),
            )
            return jax.shard_map(on_chips, mesh=cut, **specs(*chip_axes))(*arguments)
        return jax.shard_map(plain, mesh=mesh, **specs(*plain_axes))(*arguments)

    return run
```
